32 devices in a mesh: layer: 8 (over z, x), dp: 4 (over y, core).
Axes of the slice: x: 2, y: 2, z: 4, core: 2. Of those that a mesh axis runs over, the one named last changes fastest.
Arguments:
- images: float32 [4, 56, 56, 128], P('dp'), may hold values from -6 to 6
- kernels: bfloat16 [24, 1152, 128], P('layer'), may hold values from -0.1875 to 0.1875
- damping: float32 [24, 128], P('layer'), may hold values from 0.02 to 4
- cotangent: float32 [4, 56, 56, 128], P('dp'), may hold values from -6 to 6
Outputs:
- slab_ends: float32 [8, 4, 56, 56, 128], P('layer', 'dp')
- coarse_ends: float32 [8, 4, 56, 56, 128], P('layer', 'dp')
- adjoint_starts: float32 [8, 4, 56, 56, 128], P('layer', 'dp')
- adjoint_coarse_starts: float32 [8, 4, 56, 56, 128], P('layer', 'dp')
- gradients: float32 [24, 1152, 128], P('layer')
The draws below stay inside these ranges and needn't reach their ends.
All inputs are finite; a program needn't handle non-finite values.
Results may differ from the reference program's by a relative error of at most 0.0054.
Values sent between devices are 32-bit elements; how exact they have to be, the bound alone decides.
No kernel may reach another device: no remote copies, remote signals or barrier semaphores. Data moves between devices by JAX's collectives and lax.ppermute only.
A program may use at most 256 MiB of HBM per device.

```python
import math
import jax
import jax.numpy as jnp
from jax import lax

C = 128
SIDE = 56
SLAB = 3
LAYERS = 24
BATCH = 4
N_LAYER = 8


def block_scale(key, shape, shards, low, top_value):
    def one(axis_at, blocks):
        heights = jax.random.uniform(jax.random.fold_in(jax.random.fold_in(key, 6), axis_at), (blocks,), jnp.float32, low / len(shards), top_value / len(shards))
        return jnp.repeat(jnp.exp(heights), shape[axis_at] // blocks).reshape((-1,) + (1,) * (len(shape) - axis_at - 1))

    loudness = one(*shards[0])
    for cut in shards[1:]:
        loudness = loudness * one(*cut)
    return loudness


def gaussian(own_key, shape, deviation, limit, split=(), kind=jnp.bfloat16):
    array = jax.random.normal(own_key, shape, jnp.float32) * deviation
    if len(split) > 0:
        array = block_scale(own_key, shape, split, -0.22, 0.18) * array
    return jnp.clip(array, min=-limit, max=limit).astype(kind)


def setup_inputs(seed: int = 0) -> dict:
    splits = jax.random.split(jax.random.key(seed), 5)
    return {
        "images": gaussian(splits[0], (BATCH, SIDE, SIDE, C), 1.0, 6.0, ((0, 4),), jnp.float32),
        "kernels": gaussian(splits[1], (LAYERS, 9 * C, C), (9 * C) ** -0.5, 0.1875, ((0, 8),)),
        "damping": jnp.clip(jnp.exp(math.log(4.0) - 5.2983174 * jax.random.uniform(splits[2], (LAYERS, C), jnp.float32) ** block_scale(splits[2], (LAYERS, C), ((0, 8),), -0.2, 0.2)), 0.02, 4.0),
        "cotangent": gaussian(splits[3], (BATCH, SIDE, SIDE, C), 1.0, 6.0, ((0, 4),), jnp.float32),
    }


STEP = 0.125


def patches(field):
    side = field.shape[1]
    padded = jnp.pad(field, ((0, 0), (1, 1), (1, 1), (0, 0)))
    pieces = [padded[:, row_off:row_off + side, col_off:col_off + side, :] for row_off in range(3) for col_off in range(3)]
    return jnp.concatenate(pieces, axis=-1).reshape(-1, 9 * field.shape[3])


def advance(current, kernel, decay):
    columns = patches(current.astype(jnp.bfloat16))
    preact = jnp.dot(columns, kernel, preferred_element_type=jnp.float32).reshape(current.shape)
    activation = jnp.tanh(preact)
    return current + STEP * (activation - decay * current), activation


def retreat(adjoint, activation, kernel_back, decay):
    scaled = (STEP * (1.0 - activation * activation) * adjoint).astype(jnp.bfloat16)
    back_term = jnp.dot(patches(scaled), kernel_back, preferred_element_type=jnp.float32).reshape(adjoint.shape)
    return adjoint - STEP * decay * adjoint + back_term, scaled


def flipped(kernel):
    channels = kernel.shape[1]
    blocks = kernel.reshape(9, channels, channels)[::-1]
    return jnp.swapaxes(blocks, 1, 2).reshape(9 * channels, channels)


def coarse(kernel, decay, layers):
    channels = kernel.shape[1]
    tap_sum = jnp.sum(kernel.astype(jnp.float32).reshape(9, channels, channels), axis=0)
    return jnp.diag(1.0 - layers * STEP * decay) + layers * STEP * tap_sum


def transform(current, matrix):
    flattened = current.reshape(-1, matrix.shape[0])
    return jnp.dot(flattened, matrix, precision=lax.Precision.HIGHEST, preferred_element_type=jnp.float32).reshape(current.shape)


def sweep(current, kernel_set, decay_set):
    for layer_id in range(kernel_set.shape[0]):
        current, _ = advance(current, kernel_set[layer_id], decay_set[layer_id])
    return current


def sweep_back(adjoint, act_set, back_set, decay_set):
    for layer_id in reversed(range(act_set.shape[0])):
        adjoint, _ = retreat(adjoint, act_set[layer_id], back_set[layer_id], decay_set[layer_id])
    return adjoint


def reference(images, kernels, damping, cotangent):
    channels = images.shape[3]
    slab_count = N_LAYER
    kern = kernels.reshape(slab_count, SLAB, 9 * channels, channels)
    decays = damping.reshape(slab_count, SLAB, channels)
    flipped_all = jax.vmap(jax.vmap(flipped))(kern)
    matrices = jax.vmap(lambda kernel_set, decay_set: coarse(kernel_set[0], decay_set[0], SLAB))(kern, decays)

    ends = lax.map(lambda pair: sweep(images, pair[0], pair[1]), (kern, decays))
    start_states = jnp.concatenate([images[None], ends[:-1]], axis=0)

    def second(group):
        start, kernel_set, decay_set, matrix = group
        return sweep(start, kernel_set, decay_set) - transform(start, matrix)

    offsets = lax.map(second, (start_states, kern, decays, matrices))

    def chain_step(carried, group):
        matrix, offset = group
        following = transform(carried, matrix) + offset
        return following, (carried, following)

    _, (begins, coarse_out) = lax.scan(chain_step, images, (matrices, offsets))

    def third(group):
        begin, kernel_set, decay_set = group
        current = begin
        act_list = []
        input_list = []
        for layer_id in range(SLAB):
            input_list.append(current.astype(jnp.bfloat16))
            current, activation = advance(current, kernel_set[layer_id], decay_set[layer_id])
            act_list.append(activation)
        return current, jnp.stack(act_list), jnp.stack(input_list)

    finals, acts, inputs = lax.map(third, (begins, kern, decays))

    heads = lax.map(lambda group: sweep_back(cotangent, group[0], group[1], group[2]), (acts, flipped_all, decays))
    top_states = jnp.concatenate([heads[1:], cotangent[None]], axis=0)

    def adjoint_second(group):
        top, act_set, back_set, decay_set, matrix = group
        return sweep_back(top, act_set, back_set, decay_set) - transform(top, matrix.T)

    back_offsets = lax.map(adjoint_second, (top_states, acts, flipped_all, decays, matrices))

    def back_step(carried, group):
        matrix, offset = group
        following = transform(carried, matrix.T) + offset
        return following, (carried, following)

    _, (adjoint_tops, adjoint_out) = lax.scan(back_step, cotangent, (matrices, back_offsets), reverse=True)

    def third_back(group):
        top, act_set, input_set, back_set, decay_set = group
        adjoint = top
        grad_list = [None] * SLAB
        for layer_id in reversed(range(SLAB)):
            adjoint, scaled = retreat(adjoint, act_set[layer_id], back_set[layer_id], decay_set[layer_id])
            grad_list[layer_id] = lax.dot_general(patches(input_set[layer_id]), scaled.reshape(-1, channels), (((0,), (0,)), ((), ())), preferred_element_type=jnp.float32)
        return adjoint, jnp.stack(grad_list)

    starts_adjoint, grad_all = lax.map(third_back, (adjoint_tops, acts, inputs, flipped_all, decays))
    return finals, coarse_out, starts_adjoint, adjoint_out, grad_all.reshape(slab_count * SLAB, 9 * channels, channels)
```

```python
import functools

import jax
import jax.numpy as jnp
from jax import lax
from jax.experimental import pallas as pl
from jax.experimental.pallas import tpu as pltpu
from jax.sharding import PartitionSpec as P

STEP = 0.125
F32 = jnp.float32
BF16 = jnp.bfloat16
BLOCK_PAIRS = 14
GROUP = 4
TOGETHER = 1


def wide_of(side):
    return -(-(side + 1) // 16) * 16


def columns_shape(field):
    pairs, _, side, channels = field
    return (pairs + 1, 2, wide_of(side), 3 * channels)


def per_block(pairs, body, together=1):
    count = BLOCK_PAIRS if pairs % BLOCK_PAIRS == 0 else 1
    together = together if pairs // count % together == 0 else 1

    def step(block, carry):
        for number in range(together):
            body((block * together + number) * count, count)
        return carry

    lax.fori_loop(0, pairs // count // together, step, 0)


def clear_borders(columns):
    edge = jnp.zeros(columns.shape[2:], BF16)
    columns[0, 0] = edge
    columns[columns.shape[0] - 1, 1] = edge


def put_columns(columns, first, odd, rows):
    count, side, channels = rows.shape
    wide = columns.shape[2]
    here = jnp.concatenate([rows, jnp.zeros((count, wide - side, channels), F32)], axis=1)
    left = pltpu.roll(here, 1, 1)
    right = pltpu.roll(here, wide - 1, 1)
    columns[pl.ds(first + odd, count), 1 - odd] = jnp.concatenate([left, here, right], axis=2).astype(BF16)


def spread(paired, kernel):
    taps, channels = kernel.shape
    third = taps // 3
    blank = jnp.zeros((third, channels), BF16)
    paired[0:taps, 0:channels] = kernel
    paired[taps : taps + third, 0:channels] = blank
    paired[0:third, channels : 2 * channels] = blank
    paired[third : taps + third, channels : 2 * channels] = kernel


def convolve(columns, paired, first, count, side):
    _, _, wide, depth = columns.shape
    channels = depth // 3
    pieces = [
        columns[pl.ds(first, count), 0],
        columns[pl.ds(first, count), 1],
        columns[pl.ds(first + 1, count), 0],
        columns[pl.ds(first + 1, count), 1],
    ]
    left = jnp.concatenate([piece.reshape(count * wide, depth) for piece in pieces], axis=1)
    both = jnp.dot(left, paired[...], preferred_element_type=F32)
    return [
        both[:, odd * channels : (odd + 1) * channels].reshape(count, wide, channels)[:, :side]
        for odd in range(2)
    ]


def split_dot(left, matrix):
    high = left.astype(BF16)
    low = (left - high.astype(F32)).astype(BF16)
    m_high = matrix.astype(BF16)
    m_low = (matrix - m_high.astype(F32)).astype(BF16)
    return jnp.dot(
        jnp.concatenate([high, low, high], axis=1),
        jnp.concatenate([m_high, m_high, m_low], axis=0),
        preferred_element_type=F32,
    )


def transform_rows(rows, matrix):
    count, side, channels = rows.shape
    return split_dot(rows.reshape(count * side, channels), matrix).reshape(rows.shape)


def fill_forward(state, columns):
    def fill(first, count):
        for odd in range(2):
            put_columns(columns, first, odd, state[pl.ds(first, count), odd])

    per_block(state.shape[0], fill)


def forward_layer(current, columns, paired, rate, store):
    pairs, _, side, _ = current.shape
    decay = rate.reshape(1, 1, -1)

    def block(first, count):
        rows = pl.ds(first, count)
        for odd, preact in enumerate(convolve(columns, paired, first, count, side)):
            activation = jnp.tanh(preact)
            here = current[rows, odd]
            store(rows, first, odd, here + STEP * (activation - decay * here), activation)

    per_block(pairs, block, TOGETHER)


def scaled_rows(adjoint, activation):
    return STEP * (1.0 - activation * activation) * adjoint


def fill_backward(state, activation, columns):
    def fill(first, count):
        rows = pl.ds(first, count)
        for odd in range(2):
            put_columns(columns, first, odd, scaled_rows(state[rows, odd], activation[rows, odd]))

    per_block(state.shape[0], fill)


def backward_layer(current, columns, paired, rate, store):
    pairs, _, side, _ = current.shape
    decay = rate.reshape(1, 1, -1)

    def block(first, count):
        rows = pl.ds(first, count)
        for odd, back_term in enumerate(convolve(columns, paired, first, count, side)):
            here = current[rows, odd]
            store(rows, first, odd, here - STEP * decay * here + back_term)

    per_block(pairs, block, TOGETHER)


def params(mebibytes=40):
    return pltpu.CompilerParams(vmem_limit_bytes=mebibytes * 1024 * 1024)


def cost(field, products, extra=0):
    pairs, _, side, channels = field
    flops = products * 2 * pairs * 2 * side * channels * channels * 9
    return pl.CostEstimate(flops=flops, bytes_accessed=1000000 + extra, transcendentals=0)


def small_cost(shape, products):
    rows, channels = flat_of(shape)
    flops = products * 2 * rows * 3 * channels * channels
    return pl.CostEstimate(flops=flops, bytes_accessed=6 * 4 * rows * channels, transcendentals=0)


ANY = pl.BlockSpec(memory_space=pl.ANY)
VMEM = pl.BlockSpec(memory_space=pltpu.VMEM)
SMEM = pl.BlockSpec(memory_space=pltpu.SMEM)

def chunks_of(quarter):
    return (quarter,)


POSITION, FORWARD, BACKWARD, CHUNK, FORWARD_HEAD, BACKWARD_HEAD, SIZE = range(7)


def load(pairs_of_refs, sems, base):
    copies = []
    for number, (source, target) in enumerate(pairs_of_refs):
        copies.append(pltpu.make_async_copy(source, target, sems.at[base + number]))
        copies[-1].start()
    return copies


def finish(copies):
    for copy in copies:
        copy.wait()


def scratch_of(field, buffers):
    shape = columns_shape(field)
    return [pltpu.VMEM(shape, BF16)] * buffers + [pltpu.VMEM((4 * shape[3], 2 * field[3]), BF16)]


def join_halves(whole, low, high, half):
    rows = whole.shape[0] // 2
    whole[pl.ds(half * rows, rows)] = low[0:rows].astype(BF16)
    whole[pl.ds((1 - half) * rows, rows)] = high[0:rows].astype(BF16)


def layer_kernel(place, field, low, high, result, columns, paired, whole):
    half = lax.rem(place[CHUNK], 2)
    join_halves(whole, low, high, half)
    spread(paired, whole[...])
    rows = whole.shape[0] // 2
    clear_borders(columns)
    fill_forward(field, columns)

    def store(where, first, odd, following, activation):
        result[where, odd] = following

    forward_layer(field, columns, paired, low[rows : rows + 1], store)


def fetched_layer(place, field, low, high):
    rows, channels = low.shape[0] - 8, low.shape[1]
    return pl.pallas_call(
        layer_kernel,
        out_shape=jax.ShapeDtypeStruct(field.shape, F32),
        in_specs=[SMEM] + [VMEM] * 3,
        out_specs=VMEM,
        scratch_shapes=scratch_of(field.shape, 1) + [pltpu.VMEM((2 * rows, channels), BF16)],
        compiler_params=params(),
        cost_estimate=cost(field.shape, 1),
    )(place, field, low, high)


def piece_refs(member, group, chunks, field, shift, chunk, forward_shift):
    quarter = field.shape[0] // group
    offset = sum(chunks[:chunk])
    turn = member + shift if forward_shift else member - shift + group
    return field.at[pl.ds(lax.rem(turn, group) * quarter + offset, chunks[chunk])]


def send_out(member, group, chunks, field, outs, sems, base):
    copies = []
    for chunk in range(len(chunks)):
        for shift in range(group):
            number = chunk * group + shift
            source = piece_refs(member, group, chunks, field, shift, chunk, True)
            copies.append(pltpu.make_async_copy(source, outs[number], sems.at[base + number]))
            copies[-1].start()
    return copies


def bring_in(member, group, chunks, pieces, field, sems, base):
    copies = []
    for chunk in range(len(chunks)):
        for shift in range(group):
            number = chunk * group + shift
            target = piece_refs(member, group, chunks, field, shift, chunk, False)
            copies.append(pltpu.make_async_copy(pieces[number], target, sems.at[base + number]))
            copies[-1].start()
    return copies


def piece_shapes(field, group, chunks):
    return [jax.ShapeDtypeStruct((count,) + field[1:], F32) for count in chunks for _ in range(group)]


def offset_kernel(layers, group, chunks, place, images_hbm, field, low, high, kernels_hbm, decay, matrix, *refs):
    count_pieces = group * len(chunks)
    out, pieces = refs[0], refs[1 : 1 + count_pieces]
    images, kernels, starts, offset, now, later, paired, whole, sems = refs[1 + count_pieces :]
    pairs = offset.shape[0]
    loads = load([(images_hbm, images), (kernels_hbm, kernels)], sems, 0)
    half = lax.rem(place[CHUNK], 2)
    first_slab = place[POSITION] == 0
    join_halves(whole, low, high, half)
    spread(paired, whole[...])
    rows = whole.shape[0] // 2
    clear_borders(now)
    clear_borders(later)
    fill_forward(field, now)
    loads[0].wait()

    def store_start(where, first, odd, following, activation):
        begin = jnp.where(first_slab, images[where, odd], following)
        starts[where, odd] = begin
        put_columns(later, first, odd, begin)

    forward_layer(field, now, paired, low[rows : rows + 1], store_start)
    loads[1].wait()
    for layer in range(layers):
        now, later = later, now
        spread(paired, kernels[layer])

        def store(where, first, odd, following, activation, last=layer == layers - 1, target=later):
            if last:
                following = following - transform_rows(starts[where, odd], matrix[...])
            else:
                put_columns(target, first, odd, following)
            offset[where, odd] = following

        forward_layer(starts if layer == 0 else offset, now, paired, decay[layer : layer + 1], store)

    copies = send_out(place[FORWARD], group, chunks, offset, pieces, sems, 3)
    copies += load([(offset, out)], sems, 2)
    finish(copies)


def slab_offset(place, images, field, low, high, kernels, decay, matrix, group, chunks):
    layers, taps, channels = kernels.shape
    shape = images.shape
    count = group * len(chunks)
    results = pl.pallas_call(
        functools.partial(offset_kernel, layers, group, chunks),
        out_shape=[jax.ShapeDtypeStruct(shape, F32)] + piece_shapes(shape, group, chunks),
        in_specs=[SMEM, ANY, VMEM, VMEM, VMEM, ANY, VMEM, VMEM],
        out_specs=[ANY] * (1 + count),
        scratch_shapes=[pltpu.VMEM(shape, F32), pltpu.VMEM(kernels.shape, BF16)]
        + [pltpu.VMEM(shape, F32)] * 2
        + scratch_of(shape, 2)
        + [pltpu.VMEM((taps, channels), BF16), pltpu.SemaphoreType.DMA((3 + count,))],
        compiler_params=params(),
        cost_estimate=cost(shape, layers + 1),
    )(place, images, field, low, high, kernels, decay, matrix)
    return results[0], results[1:]


def split_matrix(matrix):
    high = matrix.astype(BF16)
    low = (matrix - high.astype(F32)).astype(BF16)
    return jnp.concatenate([high, high, low], axis=0)


def split_rows(rows):
    high = rows.astype(BF16)
    low = (rows - high.astype(F32)).astype(BF16)
    return jnp.concatenate([high, low, high], axis=1)


def identity(channels):
    rows = lax.broadcasted_iota(jnp.int32, (channels, channels), 0)
    columns = lax.broadcasted_iota(jnp.int32, (channels, channels), 1)
    return (rows == columns).astype(F32)


def prelude_kernel(place, kernels, damping, *outs):
    layers, taps, channels = kernels.shape
    parts, (quarter, matrix, turned) = outs[:layers], outs[layers:]
    half_rows, quarter_rows = taps // 2, taps // 4
    half, chunk = lax.rem(place[CHUNK], 2), lax.rem(place[CHUNK], 4)
    for layer in range(layers):
        rate = jnp.broadcast_to(damping[layer : layer + 1], (8, channels))
        parts[layer][0:half_rows] = kernels[layer, pl.ds(half * half_rows, half_rows)].astype(F32)
        parts[layer][half_rows : half_rows + 8] = rate
        quarter[layer, 0:quarter_rows] = kernels[layer, pl.ds(chunk * quarter_rows, quarter_rows)].astype(F32)
        quarter[layer, quarter_rows : quarter_rows + 8] = rate
    total = kernels[0, 0:channels].astype(F32)
    for tap in range(1, taps // channels):
        total += kernels[0, tap * channels : (tap + 1) * channels].astype(F32)
    diagonal = identity(channels) * (1.0 - layers * STEP * damping[0:1])
    coarse = diagonal + layers * STEP * total
    matrix[...] = coarse
    turned[...] = coarse.T


def prelude(place, kernels, damping):
    layers, taps, channels = kernels.shape
    part = jax.ShapeDtypeStruct((taps // 2 + 8, channels), F32)
    quarter = jax.ShapeDtypeStruct((layers, taps // 4 + 8, channels), F32)
    square = jax.ShapeDtypeStruct((channels, channels), F32)
    results = pl.pallas_call(
        prelude_kernel,
        out_shape=[part] * layers + [quarter, square, square],
        in_specs=[SMEM] + [VMEM] * 2,
        out_specs=[VMEM] * (layers + 3),
        compiler_params=params(16),
    )(place, kernels, damping)
    return results[:layers], *results[layers:]


def step_at(group, index):
    return index


def before_at(group, index):
    return group + index


def after_at(group, index):
    return 2 * group + index


def whole_at(group):
    return 3 * group


def matrices_kernel(group, place, *refs):
    pieces, (out, held) = refs[:group], refs[group:]
    channels = held.shape[1]
    for shift in range(group):
        held[lax.rem(place[FORWARD] - shift + group, group)] = pieces[shift][...]
    for backward in range(2):
        ordered = [held[group - 1 - step].T if backward else held[step] for step in range(group)]
        product = identity(channels)
        for step in range(group):
            split = split_matrix(ordered[step])
            out[backward, step_at(group, step)] = split
            out[backward, before_at(group, step)] = split_matrix(product)
            product = ordered[0] if step == 0 else jnp.dot(split_rows(product), split, preferred_element_type=F32)
        out[backward, whole_at(group)] = split_matrix(product)
        product = identity(channels)
        for step in reversed(range(group)):
            out[backward, after_at(group, step)] = split_matrix(product)
            if step == group - 1:
                product = ordered[step]
            else:
                product = jnp.dot(split_rows(ordered[step]), split_matrix(product), preferred_element_type=F32)


def group_matrices(place, pieces):
    group = len(pieces)
    channels = pieces[0].shape[0]
    return pl.pallas_call(
        functools.partial(matrices_kernel, group),
        out_shape=jax.ShapeDtypeStruct((2, 3 * group + 1, 3 * channels, channels), BF16),
        in_specs=[SMEM] + [VMEM] * group,
        out_specs=VMEM,
        scratch_shapes=[pltpu.VMEM((group, channels, channels), F32)],
        compiler_params=params(16),
    )(place, *pieces)


def flat_of(shape):
    return (shape[0] * shape[1] * shape[2], shape[3])


def carry_kernel(group, chunks, chunk, backward, place, seed, matrices, *refs):
    pieces, (carry, start, right, sems) = refs[:group], refs[group:]
    member = place[BACKWARD if backward else FORWARD]
    leads = place[BACKWARD_HEAD if backward else FORWARD_HEAD] == 1
    depth = right.shape[0] // (group + 1)
    source = piece_refs(member, group, chunks, seed, 0, chunk, True)
    loads = [(source, start), (matrices.at[backward, whole_at(group)], right.at[pl.ds(group * depth, depth)])]
    for shift in range(group):
        slab = lax.rem(member - shift + group, group)
        loads.append((matrices.at[backward, after_at(group, slab)], right.at[pl.ds(shift * depth, depth)]))
    loads = load(loads, sems, 0)
    flat = flat_of(start.shape)
    left = [split_rows(pieces[shift][...].reshape(flat)) for shift in range(group)]
    finish(loads)
    left.append(split_rows(jnp.where(leads, start[...], 0.0).reshape(flat)))
    total = jnp.dot(jnp.concatenate(left, axis=1), right[...], preferred_element_type=F32)
    carry[...] = total.reshape(start.shape)


def group_carry(place, seed, matrices, pieces, group, chunks, chunk, backward):
    shape = pieces[0].shape
    depth, channels = matrices.shape[2:]
    return pl.pallas_call(
        functools.partial(carry_kernel, group, chunks, chunk, int(backward)),
        out_shape=jax.ShapeDtypeStruct(shape, F32),
        in_specs=[SMEM, ANY, ANY] + [VMEM] * group,
        out_specs=VMEM,
        scratch_shapes=[
            pltpu.VMEM(shape, F32),
            pltpu.VMEM(((group + 1) * depth, channels), BF16),
            pltpu.SemaphoreType.DMA((group + 2,)),
        ],
        compiler_params=params(24),
        cost_estimate=small_cost(shape, 5),
    )(place, seed, matrices, *pieces)


def partial_kernel(group, chunks, chunk, backward, place, seed, matrices, *refs):
    pieces, (begun, products, full, held, start, sets, sems) = refs[:group], refs[group:]
    member = place[BACKWARD if backward else FORWARD]
    leads = place[BACKWARD_HEAD if backward else FORWARD_HEAD] == 1
    source = piece_refs(member, group, chunks, seed, 0, chunk, True)
    loads = load([(source, start), (matrices.at[backward, pl.ds(0, 2 * group)], sets)], sems, 0)
    for shift in range(group):
        held[lax.rem(member - shift + group, group)] = pieces[shift][...]
    finish(loads)
    shape = start.shape
    flat = flat_of(shape)
    state = jnp.where(leads, start[...], 0.0).reshape(flat)
    full[0] = state.reshape(shape)
    for slab in range(group - 1):
        step = sets[step_at(group, slab)]
        state = jnp.dot(split_rows(state), step, preferred_element_type=F32) + held[slab].reshape(flat)
        full[slab + 1] = state.reshape(shape)
    channels = shape[3]
    for shift in range(group):
        slab = lax.rem(member + shift, group)
        begun[shift] = full[slab]
        products[:, shift * channels : (shift + 1) * channels] = sets[before_at(group, slab)]


def partial_chain(place, seed, matrices, pieces, group, chunks, chunk, backward):
    shape = pieces[0].shape
    depth, channels = matrices.shape[2:]
    stack = (group,) + shape
    return pl.pallas_call(
        functools.partial(partial_kernel, group, chunks, chunk, int(backward)),
        out_shape=[jax.ShapeDtypeStruct(stack, F32), jax.ShapeDtypeStruct((depth, group * channels), BF16)],
        in_specs=[SMEM, ANY, ANY] + [VMEM] * group,
        out_specs=[VMEM] * 2,
        scratch_shapes=[
            pltpu.VMEM(stack, F32),
            pltpu.VMEM(stack, F32),
            pltpu.VMEM(shape, F32),
            pltpu.VMEM((2 * group, depth, channels), BF16),
            pltpu.SemaphoreType.DMA((2,)),
        ],
        compiler_params=params(24),
        cost_estimate=small_cost(shape, 12),
    )(place, seed, matrices, *pieces)


def hop_kernel(carry, whole, own, result):
    shape = own.shape
    moved = jnp.dot(split_rows(carry[...].reshape(flat_of(shape))), whole[...], preferred_element_type=F32)
    result[...] = own[...] + moved.reshape(shape)


def hop(carry, whole, own):
    return pl.pallas_call(
        hop_kernel,
        out_shape=jax.ShapeDtypeStruct(own.shape, F32),
        in_specs=[VMEM] * 3,
        out_specs=VMEM,
        compiler_params=params(24),
        cost_estimate=small_cost(own.shape, 2),
    )(carry, whole, own)


def complete_kernel(group, carry, products, begun, *outs):
    shape = carry.shape
    channels = shape[3]
    moved = jnp.dot(split_rows(carry[...].reshape(flat_of(shape))), products[...], preferred_element_type=F32)
    for shift in range(group):
        part = moved[:, shift * channels : (shift + 1) * channels]
        outs[shift][...] = begun[shift] + part.reshape(shape)


def complete_chain(carry, products, begun, group):
    shape = carry.shape
    return pl.pallas_call(
        functools.partial(complete_kernel, group),
        out_shape=[jax.ShapeDtypeStruct(shape, F32)] * group,
        in_specs=[VMEM] * 3,
        out_specs=[VMEM] * group,
        compiler_params=params(24),
        cost_estimate=small_cost(shape, 4),
    )(carry, products, begun)


def middle_kernel(layers, group, chunks, place, *refs):
    count_pieces = group * len(chunks)
    pieces, refs = refs[:count_pieces], refs[count_pieces:]
    (offset_hbm, cotangent_hbm, next_k_hbm, next_f_hbm, own_k_hbm, own_f_hbm, own_decay, next_decay, matrix, turned) = refs[:10]
    refs = refs[10:]
    (slab_end, coarse_end, back_offset), refs = refs[:3], refs[3:]
    state_outs, refs = refs[:layers], refs[layers:]
    act_outs, refs = refs[:layers], refs[layers:]
    back_pieces, refs = refs[:count_pieces], refs[count_pieces:]
    (begins, states, acts, offset, cotangent, tops, adjoint, first_columns, second_columns, paired) = refs[:10]
    kernels, turned_kernels, decays, sems = refs[10:]
    pairs = offset.shape[0]
    last_slab = place[POSITION] == place[SIZE] - 1

    brought = bring_in(place[FORWARD], group, chunks, pieces, begins, sems, 0)
    base = count_pieces
    loads = load(
        [
            (offset_hbm, offset),
            (next_k_hbm, kernels.at[0]),
            (cotangent_hbm, tops),
            (next_f_hbm, turned_kernels.at[0]),
            (own_k_hbm, kernels.at[1]),
            (own_f_hbm, turned_kernels.at[1]),
            (cotangent_hbm, cotangent),
        ],
        sems,
        base,
    )
    base += len(loads)
    decays[0] = next_decay[...]
    decays[1] = own_decay[...]
    clear_borders(first_columns)
    clear_borders(second_columns)
    finish(brought)
    loads[0].wait()

    def coarse_rows(first, count):
        rows = pl.ds(first, count)
        for odd in range(2):
            fresh = transform_rows(begins[rows, odd], matrix[...]) + offset[rows, odd]
            states[0, rows, odd] = fresh
            put_columns(first_columns, first, odd, fresh)

    per_block(pairs, coarse_rows)
    out_coarse = pltpu.make_async_copy(states.at[0], coarse_end, sems.at[base])
    out_coarse.start()
    base += 1
    finish(loads[1:])
    late = [(states.at[layers], slab_end)]
    late += [(states.at[n], state_outs[n]) for n in range(layers)]
    late += [(acts.at[n], act_outs[n]) for n in range(layers)]

    def both_sweeps(index, carry):
        now, later = first_columns, second_columns
        for layer in range(layers):
            spread(paired, kernels[index, layer])

            def store(rows, first, odd, following, activation, layer=layer, target=later):
                states[layer + 1, rows, odd] = following
                acts[layer, rows, odd] = activation
                if layer < layers - 1:
                    put_columns(target, first, odd, following)
                else:
                    put_columns(target, first, odd, scaled_rows(tops[rows, odd], activation))

            forward_layer(states.at[layer], now, paired, decays[index, layer : layer + 1], store)
            now, later = later, now

        @pl.when(index == 1)
        def _():
            load(late, sems, base)

        for layer in reversed(range(layers)):
            spread(paired, turned_kernels[index, layer])

            def store_back(rows, first, odd, following, layer=layer, target=later):
                adjoint[rows, odd] = following
                if layer > 0:
                    put_columns(target, first, odd, scaled_rows(following, acts[layer - 1, rows, odd]))

            source = tops if layer == layers - 1 else adjoint
            backward_layer(source, now, paired, decays[index, layer : layer + 1], store_back)
            now, later = later, now

        @pl.when(index == 0)
        def _():
            out_coarse.wait()

            def again(first, count):
                rows = pl.ds(first, count)
                tops[rows] = jnp.where(last_slab, cotangent[rows], adjoint[rows])
                for odd in range(2):
                    begin = begins[rows, odd]
                    states[0, rows, odd] = begin
                    put_columns(first_columns, first, odd, begin)

            per_block(pairs, again)

        return carry

    lax.fori_loop(0, 2, both_sweeps, 0)

    def subtract(first, count):
        rows = pl.ds(first, count)
        for odd in range(2):
            adjoint[rows, odd] = adjoint[rows, odd] - transform_rows(tops[rows, odd], turned[...])

    per_block(pairs, subtract)
    outs = send_out(place[BACKWARD], group, chunks, adjoint, back_pieces, sems, 0)
    outs += load([(adjoint, back_offset)], sems, count_pieces)
    finish(outs)
    for number, (source, target) in enumerate(late):
        pltpu.make_async_copy(source, target, sems.at[base + number]).wait()


def middle(place, pieces, offset, cotangent, own, following, own_decay, next_decay, matrix, turned, group, chunks):
    layers = own[0].shape[0]
    field = offset.shape
    count = len(pieces)
    fields = [jax.ShapeDtypeStruct(field, F32)] * (3 + 2 * layers)
    results = pl.pallas_call(
        functools.partial(middle_kernel, layers, group, chunks),
        out_shape=fields + piece_shapes(field, group, chunks),
        in_specs=[SMEM] + [ANY] * (count + 6) + [VMEM] * 4,
        out_specs=[ANY] * (3 + 2 * layers + count),
        scratch_shapes=[pltpu.VMEM(field, F32)]
        + [pltpu.VMEM((layers + 1,) + field, F32), pltpu.VMEM((layers,) + field, F32)]
        + [pltpu.VMEM(field, F32)] * 4
        + scratch_of(field, 2)
        + [pltpu.VMEM((2,) + own[0].shape, BF16)] * 2
        + [pltpu.VMEM((2, layers, field[3]), F32), pltpu.SemaphoreType.DMA((count + 9 + 2 * layers,))],
        compiler_params=params(52),
        cost_estimate=cost(field, 4 * layers),
    )(place, *pieces, offset, cotangent, *following, *own, own_decay, next_decay, matrix, turned)
    return results[:3], results[3 : 3 + layers], results[3 + layers : 3 + 2 * layers], results[3 + 2 * layers :]


def turn(whole, turned):
    taps, channels = whole.shape[0] // whole.shape[1], whole.shape[1]
    for tap in range(taps):
        block = whole[tap * channels : (tap + 1) * channels]
        other = taps - 1 - tap
        turned[other * channels : (other + 1) * channels] = block.T.astype(BF16)


def own_kernel(kernels, turned, whole):
    for layer in range(kernels.shape[0]):
        whole[...] = kernels[layer].astype(F32)
        turn(whole, turned.at[layer])


def turn_own(kernels):
    return pl.pallas_call(
        own_kernel,
        out_shape=jax.ShapeDtypeStruct(kernels.shape, BF16),
        in_specs=[VMEM],
        out_specs=VMEM,
        scratch_shapes=[pltpu.VMEM(kernels.shape[1:], F32)],
        compiler_params=params(),
    )(kernels)


def next_kernel(place, *refs):
    quarters, (kernels, turned, decay, whole) = refs[:4], refs[4:]
    layers = kernels.shape[0]
    rows = whole.shape[0] // 4
    chunk = lax.rem(place[CHUNK], 4)
    at = [chunk, chunk + 2 - 4 * (chunk // 2), chunk + 1 - 2 * lax.rem(chunk, 2)]
    at.append(at[2] + 2 - 4 * (chunk // 2))
    for layer in range(layers):
        for number in range(4):
            whole[pl.ds(at[number] * rows, rows)] = quarters[number][layer, 0:rows]
        kernels[layer] = whole[...].astype(BF16)
        turn(whole, turned.at[layer])
        decay[layer : layer + 1] = quarters[0][layer, rows : rows + 1]


def join_next(place, quarters):
    layers, rows, channels = quarters[0].shape
    shape = (layers, 4 * (rows - 8), channels)
    results = pl.pallas_call(
        next_kernel,
        out_shape=[jax.ShapeDtypeStruct(shape, BF16)] * 2 + [jax.ShapeDtypeStruct((layers, channels), F32)],
        in_specs=[SMEM] + [VMEM] * 4,
        out_specs=[VMEM] * 3,
        scratch_shapes=[pltpu.VMEM(shape[1:], F32)],
        compiler_params=params(),
    )(place, *quarters)
    return results[:2], results[2]


def turned_columns_kernel(state, turned, columns):
    pairs, _, side, _ = state.shape
    wide, depth = columns.shape[2:]
    clear_borders(columns)

    def fill(first, count):
        for odd in range(2):
            put_columns(columns, first, odd, state[pl.ds(first, count), odd])

    per_block(pairs, fill)
    for pair in range(pairs + 1):
        block = columns[pair].reshape(2 * wide, depth).astype(F32)
        turned[:, pair * 2 * wide : (pair + 1) * 2 * wide] = block.T.astype(BF16)


def turned_columns(state):
    shape = columns_shape(state.shape)
    return pl.pallas_call(
        turned_columns_kernel,
        out_shape=jax.ShapeDtypeStruct((shape[3], shape[0] * 2 * shape[2]), BF16),
        in_specs=[VMEM],
        out_specs=VMEM,
        scratch_shapes=[pltpu.VMEM(shape, BF16)],
        compiler_params=params(),
        cost_estimate=cost(state.shape, 1),
    )(state)


def gradient_body(adjoint, activation, turned, ready, shifted, gradient, side):
    pairs = adjoint.shape[0]
    wide = shifted.shape[2]
    channels = adjoint.shape[3]
    edge = jnp.zeros((wide, channels), BF16)
    flat = 2 * pairs + 2
    for tap in range(3):
        for row in list(range(tap)) + list(range(flat - 2 + tap, flat)):
            shifted[row // 2, row % 2, :, tap * channels : (tap + 1) * channels] = edge

    def fill(first, count):
        rows = pl.ds(first, count)
        for odd in range(2):
            scaled = scaled_rows(adjoint[rows, odd], activation[rows, odd])
            padded = jnp.concatenate([scaled, jnp.zeros((count, wide - side, channels), F32)], axis=1).astype(BF16)
            for tap in range(3):
                row = odd + tap
                shifted[pl.ds(first + row // 2, count), row % 2, :, tap * channels : (tap + 1) * channels] = padded

    per_block(pairs, fill)
    ready()
    products = jnp.dot(
        turned[...], shifted[...].reshape(flat * wide, 3 * channels), preferred_element_type=F32
    )
    for row in range(3):
        for column in range(3):
            tap = 3 * row + column
            gradient[tap * channels : (tap + 1) * channels] = products[
                column * channels : (column + 1) * channels, row * channels : (row + 1) * channels
            ]


def halve(place, gradient, keep, send):
    half = lax.rem(place[CHUNK], 2)
    rows = keep.shape[0]
    keep[...] = gradient[pl.ds(half * rows, rows)]
    send[...] = gradient[pl.ds((1 - half) * rows, rows)]


def top_kernel(group, chunks, place, *refs):
    count_pieces = group * len(chunks)
    pieces, refs = refs[:count_pieces], refs[count_pieces:]
    activation_hbm, turned_hbm, adjoint_out, keep, send = refs[:5]
    adjoint, activation, turned, shifted, gradient, sems = refs[5:]
    brought = bring_in(place[BACKWARD], group, chunks, pieces, adjoint, sems, 0)
    loads = load([(activation_hbm, activation), (turned_hbm, turned)], sems, count_pieces)
    finish(brought)
    out = load([(adjoint, adjoint_out)], sems, 0)
    loads[0].wait()
    gradient_body(adjoint, activation, turned, loads[1].wait, shifted, gradient, adjoint.shape[2])
    halve(place, gradient, keep, send)
    finish(out)


def top_gradient(place, pieces, activation, turned, group, chunks):
    field = activation.shape
    shape = columns_shape(field)
    taps = 9 * field[3]
    half = jax.ShapeDtypeStruct((taps // 2, field[3]), F32)
    return pl.pallas_call(
        functools.partial(top_kernel, group, chunks),
        out_shape=[jax.ShapeDtypeStruct(field, F32), half, half],
        in_specs=[SMEM] + [ANY] * (len(pieces) + 2),
        out_specs=[ANY, VMEM, VMEM],
        scratch_shapes=[
            pltpu.VMEM(field, F32),
            pltpu.VMEM(field, F32),
            pltpu.VMEM(turned.shape, BF16),
            pltpu.VMEM(shape, BF16),
            pltpu.VMEM((taps, field[3]), F32),
            pltpu.SemaphoreType.DMA((len(pieces) + 2,)),
        ],
        compiler_params=params(),
        cost_estimate=cost(field, 1),
    )(place, *pieces, activation, turned)


def retreat_body(adjoint, activation, columns, paired, rate, store):
    clear_borders(columns)
    fill_backward(adjoint, activation, columns)
    backward_layer(adjoint, columns, paired, rate, store)


def lower_kernel(layer, place, adjoint, above, kernel, decay, below_hbm, turned_hbm, *refs):
    result_out, keep, send = refs[:3]
    result, below, turned, columns, paired, shifted, gradient, sems = refs[3:]
    loads = load([(below_hbm, below), (turned_hbm, turned)], sems, 0)
    spread(paired, kernel[layer])

    def store(rows, first, odd, fresh):
        result[rows, odd] = fresh

    retreat_body(adjoint, above, columns, paired, decay[layer : layer + 1], store)
    out = load([(result, result_out)], sems, 2)
    loads[0].wait()
    gradient_body(result, below, turned, loads[1].wait, shifted, gradient, result.shape[2])
    halve(place, gradient, keep, send)
    finish(out)


def lower_gradient(place, layer, adjoint, above, kernels, decay, below, turned):
    field = adjoint.shape
    shape = columns_shape(field)
    taps = 9 * field[3]
    half = jax.ShapeDtypeStruct((taps // 2, field[3]), F32)
    return pl.pallas_call(
        functools.partial(lower_kernel, layer),
        out_shape=[jax.ShapeDtypeStruct(field, F32), half, half],
        in_specs=[SMEM] + [VMEM] * 4 + [ANY] * 2,
        out_specs=[ANY, VMEM, VMEM],
        scratch_shapes=[pltpu.VMEM(field, F32), pltpu.VMEM(field, F32), pltpu.VMEM(turned.shape, BF16)]
        + scratch_of(field, 1)
        + [pltpu.VMEM(shape, BF16), pltpu.VMEM((taps, field[3]), F32), pltpu.SemaphoreType.DMA((3,))],
        compiler_params=params(),
        cost_estimate=cost(field, 2),
    )(place, adjoint, above, kernels, decay, below, turned)


def last_kernel(adjoint, activation, kernel, decay, tops, back_offset, turned, result, adjoint_end, columns, paired):
    spread(paired, kernel[0])

    def store(rows, first, odd, fresh):
        result[rows, odd] = fresh

    retreat_body(adjoint, activation, columns, paired, decay[0:1], store)

    def coarse_rows(first, count):
        rows = pl.ds(first, count)
        for odd in range(2):
            adjoint_end[rows, odd] = transform_rows(tops[rows, odd], turned[...]) + back_offset[rows, odd]

    per_block(adjoint.shape[0], coarse_rows)


def last_retreat(adjoint, activation, kernels, decay, tops, back_offset, turned):
    field = adjoint.shape
    return pl.pallas_call(
        last_kernel,
        out_shape=[jax.ShapeDtypeStruct(field, F32)] * 2,
        in_specs=[VMEM] * 7,
        out_specs=[VMEM] * 2,
        scratch_shapes=scratch_of(field, 1),
        compiler_params=params(),
        cost_estimate=cost(field, 1),
    )(adjoint, activation, kernels, decay, tops, back_offset, turned)


def collect_kernel(layers, place, *refs):
    sources, out = refs[: 2 * layers], refs[2 * layers]
    half = lax.rem(place[CHUNK], 2)
    rows = out.shape[1] // 2
    for layer in range(layers):
        out[layer, pl.ds(half * rows, rows)] = sources[2 * layer][...]
        out[layer, pl.ds((1 - half) * rows, rows)] = sources[2 * layer + 1][...]


def collect(place, halves):
    layers = len(halves)
    rows, channels = halves[0][0].shape
    flat = [half for both in halves for half in both]
    return pl.pallas_call(
        functools.partial(collect_kernel, layers),
        out_shape=jax.ShapeDtypeStruct((layers, 2 * rows, channels), F32),
        in_specs=[SMEM] + [VMEM] * (2 * layers),
        out_specs=VMEM,
        compiler_params=params(16),
    )(place, *flat)


def from_behind(shard, axis, by):
    devices = lax.axis_size(axis)
    pairs = [(i, i + by) for i in range(devices) if 0 <= i + by < devices]
    return lax.ppermute(shard, axis, pairs)


def swap(shard, bit):
    return lax.ppermute(shard, "dp", [(i, i ^ bit) for i in range(lax.axis_size("dp"))])


def order_of(index, size, backward):
    return size - 1 - index if backward else index


def group_of(size):
    for group in (GROUP, 2, 1):
        if size % group == 0:
            return group


def exchange(pieces, group, backward):
    size = lax.axis_size("layer")
    received = [pieces[0]]
    for shift in range(1, group):
        pairs = []
        for order in range(size):
            base = order - order % group
            target = base + (order + shift) % group
            pairs.append((order_of(order, size, backward), order_of(target, size, backward)))
        received.append(lax.ppermute(pieces[shift], "layer", pairs))
    return received


def coarse_chain(place, seed, pieces, matrices, group, chunks, backward):
    size = lax.axis_size("layer")
    pairs = [(order_of(i, size, backward), order_of(i + group, size, backward)) for i in range(size - group)]
    received = [exchange(pieces[c * group : (c + 1) * group], group, backward) for c in range(len(chunks))]
    begins = []
    for chunk in range(len(chunks)):
        carry = jnp.zeros(pieces[chunk * group].shape, F32)
        if size > group:
            out = group_carry(place, seed, matrices, received[chunk], group, chunks, chunk, backward)
            carry = lax.ppermute(out, "layer", pairs)
            for _ in range(size // group - 2):
                carry = lax.ppermute(hop(carry, matrices[int(backward), whole_at(group)], out), "layer", pairs)
        begun, products = partial_chain(place, seed, matrices, received[chunk], group, chunks, chunk, backward)
        begins.append((carry, products, begun))
    result = []
    for carry, products, begun in begins:
        result += exchange(complete_chain(carry, products, begun, group), group, backward)
    return result


def sum_across(total):
    bit = 2
    while bit < lax.axis_size("dp"):
        total = total + swap(total, bit)
        bit *= 2
    return total


def per_device(images, kernels, damping, cotangent):
    layers, taps, channels = kernels.shape
    _, height, side, _ = images.shape
    size = lax.axis_size("layer")
    position = lax.axis_index("layer")
    dp_at = lax.axis_index("dp")
    field = (height // 2, 2, side, channels)
    images = images.reshape(field)
    cotangent = cotangent.reshape(field)
    group = group_of(size)
    quarter = field[0] // group
    chunks = chunks_of(quarter)
    back_order = size - 1 - position
    place = jnp.stack(
        [
            position,
            lax.rem(position, group),
            lax.rem(back_order, group),
            dp_at,
            (position < group).astype(jnp.int32),
            (back_order < group).astype(jnp.int32),
            jnp.int32(size),
            jnp.int32(0),
        ]
    ).astype(jnp.int32)

    parts, quarter_part, matrix, turned_matrix = prelude(place, kernels, damping)

    lows = [from_behind(part, "layer", 1) for part in parts]
    highs = [swap(low, 1) for low in lows]

    matrices = group_matrices(place, exchange([matrix] * group, group, False))
    own = (kernels, turn_own(kernels))

    state, matrices = lax.optimization_barrier((images, matrices))
    for layer in range(layers - 1):
        state = fetched_layer(place, state, lows[layer], highs[layer])

    quarter_part, state = lax.optimization_barrier((quarter_part, state))
    first = from_behind(quarter_part, "layer", -1)
    second = swap(first, 2)
    following, next_decay = join_next(place, [first, second, swap(first, 1), swap(second, 1)])

    offset, pieces = slab_offset(
        place, images, state, lows[-1], highs[-1], kernels, damping, matrix, group, chunks
    )
    pieces = coarse_chain(place, images, pieces, matrices, group, chunks, False)
    (slab_end, coarse_end, back_offset), states, acts, pieces = middle(
        place, pieces, offset, cotangent, own, following, damping, next_decay, matrix, turned_matrix, group, chunks
    )
    turned = [turned_columns(state) for state in states]
    pieces = coarse_chain(place, cotangent, pieces, matrices, group, chunks, True)
    tops, keep, send = top_gradient(place, pieces, acts[-1], turned[-1], group, chunks)
    adjoint = tops
    paired = [None] * layers
    halves = [None] * layers
    for layer in reversed(range(1, layers)):
        paired[layer] = (keep, send)
        adjoint, keep, send = lower_gradient(
            place, layer, adjoint, acts[layer], own[1], damping, acts[layer - 1], turned[layer - 1]
        )
        total = paired[layer][0] + swap(paired[layer][1], 1)
        adjoint, total = lax.optimization_barrier((adjoint, total))
        if layer < layers - 1:
            adjoint, summed = lax.optimization_barrier((adjoint, paired[layer + 1]))
            paired[layer + 1] = summed
        paired[layer] = sum_across(total)
    total = keep + swap(send, 1)
    adjoint, adjoint_end = last_retreat(adjoint, acts[0], own[1], damping, tops, back_offset, turned_matrix)
    adjoint, total, paired[1] = lax.optimization_barrier((adjoint, total, paired[1]))
    paired[0] = sum_across(total)
    halves = [(half, swap(half, 1)) for half in paired]
    full = (1, 1, height, side, channels)
    return (
        slab_end.reshape(full),
        coarse_end.reshape(full),
        adjoint.reshape(full),
        adjoint_end.reshape(full),
        collect(place, halves),
    )


def solution(mesh):
    in_specs = (
        P("dp", None, None, None),
        P("layer", None, None),
        P("layer", None),
        P("dp", None, None, None),
    )
    out_specs = (
        P("layer", "dp", None, None, None),
        P("layer", "dp", None, None, None),
        P("layer", "dp", None, None, None),
        P("layer", "dp", None, None, None),
        P("layer", None, None),
    )
    return jax.shard_map(
        per_device, mesh=mesh, in_specs=in_specs, out_specs=out_specs, check_vma=False
    )
```

```python
import functools
import math

import jax
import jax.numpy as jnp
from jax import lax
from jax.experimental import pallas as pl
from jax.experimental.pallas import tpu as pltpu
from jax.sharding import PartitionSpec as P

STEP = 0.125
F32 = jnp.float32
BF16 = jnp.bfloat16
BLOCK_PAIRS = 7
GROUP = 4


def wide_of(side):
    return -(-(side + 1) // 16) * 16


def columns_shape(field):
    pairs, _, side, channels = field
    return (pairs + 1, 2, wide_of(side), 3 * channels)


def block_of(pairs):
    return BLOCK_PAIRS if pairs % BLOCK_PAIRS == 0 else 1


def per_block(pairs, body, whole=False):
    block = block_of(pairs)

    def step(number, carry):
        if whole:
            body(number * block, block)
        else:
            for pair in range(block):
                body(number * block + pair, 1)
        return carry

    lax.fori_loop(0, pairs // block, step, 0)


def clear_borders(columns):
    edge = jnp.zeros(columns.shape[2:], BF16)
    columns[0, 0] = edge
    columns[columns.shape[0] - 1, 1] = edge


def put_columns(columns, first, odd, rows):
    count, side, channels = rows.shape
    wide = columns.shape[2]
    here = jnp.concatenate([rows, jnp.zeros((count, wide - side, channels), F32)], axis=1)
    left = pltpu.roll(here, 1, 1)
    right = pltpu.roll(here, wide - 1, 1)
    columns[pl.ds(first + odd, count), 1 - odd] = jnp.concatenate([left, here, right], axis=2).astype(BF16)


def spread(paired, kernel):
    taps, channels = kernel.shape
    third = taps // 3
    blank = jnp.zeros((third, channels), BF16)
    paired[0:taps, 0:channels] = kernel
    paired[taps : taps + third, 0:channels] = blank
    paired[0:third, channels : 2 * channels] = blank
    paired[third : taps + third, channels : 2 * channels] = kernel


def convolve(columns, paired, results, emit, side):
    _, _, wide, depth = columns.shape
    channels = depth // 3
    pairs = columns.shape[0] - 1
    block = block_of(pairs)

    def product(number):
        first = number * block
        pieces = [
            columns[first : first + block, 0],
            columns[first : first + block, 1],
            columns[first + 1 : first + 1 + block, 0],
            columns[first + 1 : first + 1 + block, 1],
        ]
        left = jnp.concatenate([piece.reshape(block * wide, depth) for piece in pieces], axis=1)
        results[number % 2][...] = jnp.dot(left, paired[...], preferred_element_type=F32)

    product(0)
    for number in range(pairs // block):
        if number + 1 < pairs // block:
            product(number + 1)
        result = results[number % 2]
        for pair in range(block):
            for odd in range(2):
                preact = result[pair * wide : (pair + 1) * wide, odd * channels : (odd + 1) * channels]
                emit(number * block + pair, odd, preact.reshape(1, wide, channels)[:, :side])


def split_dot(left, matrix):
    high = left.astype(BF16)
    low = (left - high.astype(F32)).astype(BF16)
    m_high = matrix.astype(BF16)
    m_low = (matrix - m_high.astype(F32)).astype(BF16)
    return jnp.dot(
        jnp.concatenate([high, low, high], axis=1),
        jnp.concatenate([m_high, m_high, m_low], axis=0),
        preferred_element_type=F32,
    )


def transform_rows(rows, matrix):
    count, side, channels = rows.shape
    return split_dot(rows.reshape(count * side, channels), matrix).reshape(rows.shape)


def fill_forward(state, columns):
    def fill(first, count):
        for odd in range(2):
            put_columns(columns, first, odd, state[pl.ds(first, count), odd])

    per_block(state.shape[0], fill)


def forward_layer(current, columns, tools, rate, store):
    decay = rate.reshape(1, 1, -1)

    def emit(first, odd, preact):
        rows = pl.ds(first, 1)
        activation = jnp.tanh(preact)
        here = current[rows, odd]
        store(rows, first, odd, here + STEP * (activation - decay * here), activation)

    convolve(columns, tools[0], tools[1:], emit, current.shape[2])


def scaled_rows(adjoint, activation):
    return STEP * (1.0 - activation * activation) * adjoint


def fill_backward(state, activation, columns):
    def fill(first, count):
        rows = pl.ds(first, count)
        for odd in range(2):
            put_columns(columns, first, odd, scaled_rows(state[rows, odd], activation[rows, odd]))

    per_block(state.shape[0], fill)


def backward_layer(current, columns, tools, rate, store):
    decay = rate.reshape(1, 1, -1)

    def emit(first, odd, back_term):
        rows = pl.ds(first, 1)
        here = current[rows, odd]
        store(rows, first, odd, here - STEP * decay * here + back_term)

    convolve(columns, tools[0], tools[1:], emit, current.shape[2])


def params(mebibytes=40):
    return pltpu.CompilerParams(vmem_limit_bytes=mebibytes * 1024 * 1024)


def cost(share, shape):
    flops = 8 * share * math.prod(shape) * shape[-1] * 9
    return pl.CostEstimate(flops=int(flops), bytes_accessed=8 * math.prod(shape), transcendentals=0)


ANY = pl.BlockSpec(memory_space=pl.ANY)
VMEM = pl.BlockSpec(memory_space=pltpu.VMEM)
SMEM = pl.BlockSpec(memory_space=pltpu.SMEM)

def chunks_of(quarter):
    return (quarter - quarter // 2, quarter // 2) if quarter > 1 else (quarter,)


POSITION, FORWARD, BACKWARD, CHUNK, FORWARD_HEAD, BACKWARD_HEAD, SIZE = range(7)


def load(pairs_of_refs, sems, base):
    copies = []
    for number, (source, target) in enumerate(pairs_of_refs):
        copies.append(pltpu.make_async_copy(source, target, sems.at[base + number]))
        copies[-1].start()
    return copies


def finish(copies):
    for copy in copies:
        copy.wait()


def scratch_of(field, buffers):
    shape = columns_shape(field)
    products = pltpu.VMEM((block_of(field[0]) * shape[2], 2 * field[3]), F32)
    return [pltpu.VMEM(shape, BF16)] * buffers + [pltpu.VMEM((4 * shape[3], 2 * field[3]), BF16), products, products]


def join_halves(whole, low, high, half):
    rows = whole.shape[0] // 2
    whole[pl.ds(half * rows, rows)] = low[0:rows].astype(BF16)
    whole[pl.ds((1 - half) * rows, rows)] = high[0:rows].astype(BF16)


def layer_kernel(place, field, low, high, result, columns, paired, even, uneven, whole):
    half = lax.rem(place[CHUNK], 2)
    join_halves(whole, low, high, half)
    spread(paired, whole[...])
    rows = whole.shape[0] // 2
    clear_borders(columns)
    fill_forward(field, columns)

    def store(where, first, odd, following, activation):
        result[where, odd] = following

    forward_layer(field, columns, (paired, even, uneven), low[rows : rows + 1], store)


def fetched_layer(place, field, low, high):
    rows, channels = low.shape[0] - 8, low.shape[1]
    return pl.pallas_call(
        layer_kernel,
        out_shape=jax.ShapeDtypeStruct(field.shape, F32),
        in_specs=[SMEM] + [VMEM] * 3,
        out_specs=VMEM,
        scratch_shapes=scratch_of(field.shape, 1) + [pltpu.VMEM((2 * rows, channels), BF16)],
        compiler_params=params(),
        cost_estimate=cost(1.0, field.shape),
    )(place, field, low, high)


def piece_refs(member, group, chunks, field, shift, chunk, forward_shift):
    quarter = field.shape[0] // group
    offset = sum(chunks[:chunk])
    turn = member + shift if forward_shift else member - shift + group
    return field.at[pl.ds(lax.rem(turn, group) * quarter + offset, chunks[chunk])]


def send_out(member, group, chunks, field, outs, sems, base):
    copies = []
    for chunk in range(len(chunks)):
        for shift in range(group):
            number = chunk * group + shift
            source = piece_refs(member, group, chunks, field, shift, chunk, True)
            copies.append(pltpu.make_async_copy(source, outs[number], sems.at[base + number]))
            copies[-1].start()
    return copies


def bring_in(member, group, chunks, pieces, field, sems, base):
    copies = []
    for chunk in range(len(chunks)):
        for shift in range(group):
            number = chunk * group + shift
            target = piece_refs(member, group, chunks, field, shift, chunk, False)
            copies.append(pltpu.make_async_copy(pieces[number], target, sems.at[base + number]))
            copies[-1].start()
    return copies


def piece_shapes(field, group, chunks):
    return [jax.ShapeDtypeStruct((count,) + field[1:], F32) for count in chunks for _ in range(group)]


def offset_kernel(layers, group, chunks, place, images_hbm, field, low, high, kernels_hbm, decay, matrix, *refs):
    count_pieces = group * len(chunks)
    out, pieces = refs[0], refs[1 : 1 + count_pieces]
    images, kernels, starts, offset, now, later, paired, even, uneven, whole, sems = refs[1 + count_pieces :]
    tools = (paired, even, uneven)
    pairs = offset.shape[0]
    loads = load([(images_hbm, images), (kernels_hbm, kernels)], sems, 0)
    half = lax.rem(place[CHUNK], 2)
    first_slab = place[POSITION] == 0
    join_halves(whole, low, high, half)
    spread(paired, whole[...])
    rows = whole.shape[0] // 2
    clear_borders(now)
    clear_borders(later)
    fill_forward(field, now)
    loads[0].wait()

    def store_start(where, first, odd, following, activation):
        begin = jnp.where(first_slab, images[where, odd], following)
        starts[where, odd] = begin
        put_columns(later, first, odd, begin)

    forward_layer(field, now, tools, low[rows : rows + 1], store_start)
    loads[1].wait()
    for layer in range(layers):
        now, later = later, now
        spread(paired, kernels[layer])

        def store(where, first, odd, following, activation, last=layer == layers - 1, target=later):
            if not last:
                put_columns(target, first, odd, following)
            offset[where, odd] = following

        forward_layer(starts if layer == 0 else offset, now, tools, decay[layer : layer + 1], store)

    def subtract(first, count):
        where = pl.ds(first, count)
        for odd in range(2):
            offset[where, odd] = offset[where, odd] - transform_rows(starts[where, odd], matrix[...])

    per_block(pairs, subtract, whole=True)

    copies = send_out(place[FORWARD], group, chunks, offset, pieces, sems, 3)
    copies += load([(offset, out)], sems, 2)
    finish(copies)


def slab_offset(place, images, field, low, high, kernels, decay, matrix, group, chunks):
    layers, taps, channels = kernels.shape
    shape = images.shape
    count = group * len(chunks)
    results = pl.pallas_call(
        functools.partial(offset_kernel, layers, group, chunks),
        out_shape=[jax.ShapeDtypeStruct(shape, F32)] + piece_shapes(shape, group, chunks),
        in_specs=[SMEM, ANY, VMEM, VMEM, VMEM, ANY, VMEM, VMEM],
        out_specs=[ANY] * (1 + count),
        scratch_shapes=[pltpu.VMEM(shape, F32), pltpu.VMEM(kernels.shape, BF16)]
        + [pltpu.VMEM(shape, F32)] * 2
        + scratch_of(shape, 2)
        + [pltpu.VMEM((taps, channels), BF16), pltpu.SemaphoreType.DMA((3 + count,))],
        compiler_params=params(),
        cost_estimate=cost(layers + 1.0, shape),
    )(place, images, field, low, high, kernels, decay, matrix)
    return results[0], results[1:]


def split_matrix(matrix):
    high = matrix.astype(BF16)
    low = (matrix - high.astype(F32)).astype(BF16)
    return jnp.concatenate([high, high, low], axis=0)


def split_rows(rows):
    high = rows.astype(BF16)
    low = (rows - high.astype(F32)).astype(BF16)
    return jnp.concatenate([high, low, high], axis=1)


def identity(channels):
    rows = lax.broadcasted_iota(jnp.int32, (channels, channels), 0)
    columns = lax.broadcasted_iota(jnp.int32, (channels, channels), 1)
    return (rows == columns).astype(F32)


def prelude_kernel(place, kernels, damping, *outs):
    layers, taps, channels = kernels.shape
    parts, (quarter, matrix, turned) = outs[:layers], outs[layers:]
    half_rows, quarter_rows = taps // 2, taps // 4
    half, chunk = lax.rem(place[CHUNK], 2), lax.rem(place[CHUNK], 4)
    for layer in range(layers):
        rate = jnp.broadcast_to(damping[layer : layer + 1], (8, channels))
        parts[layer][0:half_rows] = kernels[layer, pl.ds(half * half_rows, half_rows)].astype(F32)
        parts[layer][half_rows : half_rows + 8] = rate
        quarter[layer, 0:quarter_rows] = kernels[layer, pl.ds(chunk * quarter_rows, quarter_rows)].astype(F32)
        quarter[layer, quarter_rows : quarter_rows + 8] = rate
    total = kernels[0, 0:channels].astype(F32)
    for tap in range(1, taps // channels):
        total += kernels[0, tap * channels : (tap + 1) * channels].astype(F32)
    diagonal = identity(channels) * (1.0 - layers * STEP * damping[0:1])
    coarse = diagonal + layers * STEP * total
    for member in range(matrix.shape[0]):
        matrix[member] = coarse
    turned[...] = coarse.T


def prelude(place, kernels, damping, group):
    layers, taps, channels = kernels.shape
    part = jax.ShapeDtypeStruct((taps // 2 + 8, channels), F32)
    quarter = jax.ShapeDtypeStruct((layers, taps // 4 + 8, channels), F32)
    square = jax.ShapeDtypeStruct((channels, channels), F32)
    results = pl.pallas_call(
        prelude_kernel,
        out_shape=[part] * layers + [quarter, jax.ShapeDtypeStruct((group, channels, channels), F32), square],
        in_specs=[SMEM] + [VMEM] * 2,
        out_specs=[VMEM] * (layers + 3),
        compiler_params=params(16),
    )(place, kernels, damping)
    return results[:layers], *results[layers:]


def step_at(group, index):
    return index


def before_at(group, index):
    return group + index


def after_at(group, index):
    return 2 * group + index


def whole_at(group):
    return 3 * group


def matrices_kernel(group, held, out):
    channels = held.shape[1]
    for backward in range(2):
        ordered = [held[group - 1 - step].T if backward else held[step] for step in range(group)]
        product = identity(channels)
        for step in range(group):
            split = split_matrix(ordered[step])
            out[backward, step_at(group, step)] = split
            out[backward, before_at(group, step)] = split_matrix(product)
            product = ordered[0] if step == 0 else jnp.dot(split_rows(product), split, preferred_element_type=F32)
        out[backward, whole_at(group)] = split_matrix(product)
        product = identity(channels)
        for step in reversed(range(group)):
            out[backward, after_at(group, step)] = split_matrix(product)
            if step == group - 1:
                product = ordered[step]
            else:
                product = jnp.dot(split_rows(ordered[step]), split_matrix(product), preferred_element_type=F32)


def group_matrices(steps):
    group, channels, _ = steps.shape
    return pl.pallas_call(
        functools.partial(matrices_kernel, group),
        out_shape=jax.ShapeDtypeStruct((2, 3 * group + 1, 3 * channels, channels), BF16),
        in_specs=[VMEM],
        out_specs=VMEM,
        compiler_params=params(16),
    )(steps)


def flat_of(shape):
    return (shape[0] * shape[1] * shape[2], shape[3])


def carry_kernel(group, chunks, chunk, backward, place, seed, matrices, *refs):
    pieces, (carry, start, right, sems) = refs[:group], refs[group:]
    member = place[BACKWARD if backward else FORWARD]
    leads = place[BACKWARD_HEAD if backward else FORWARD_HEAD] == 1
    depth = right.shape[0] // (group + 1)
    source = piece_refs(member, group, chunks, seed, 0, chunk, True)
    loads = [(source, start), (matrices.at[backward, whole_at(group)], right.at[pl.ds(group * depth, depth)])]
    for shift in range(group):
        slab = lax.rem(member - shift + group, group)
        loads.append((matrices.at[backward, after_at(group, slab)], right.at[pl.ds(shift * depth, depth)]))
    loads = load(loads, sems, 0)
    flat = flat_of(start.shape)
    left = [split_rows(pieces[shift][...].reshape(flat)) for shift in range(group)]
    finish(loads)
    left.append(split_rows(jnp.where(leads, start[...], 0.0).reshape(flat)))
    total = jnp.dot(jnp.concatenate(left, axis=1), right[...], preferred_element_type=F32)
    carry[...] = total.reshape(start.shape)


def group_carry(place, seed, matrices, pieces, group, chunks, chunk, backward):
    shape = pieces[0].shape
    depth, channels = matrices.shape[2:]
    return pl.pallas_call(
        functools.partial(carry_kernel, group, chunks, chunk, int(backward)),
        out_shape=jax.ShapeDtypeStruct(shape, F32),
        in_specs=[SMEM, ANY, ANY] + [VMEM] * group,
        out_specs=VMEM,
        scratch_shapes=[
            pltpu.VMEM(shape, F32),
            pltpu.VMEM(((group + 1) * depth, channels), BF16),
            pltpu.SemaphoreType.DMA((group + 2,)),
        ],
        compiler_params=params(24),
        cost_estimate=cost(1.0 * group, shape),
    )(place, seed, matrices, *pieces)


def partial_kernel(group, chunks, chunk, backward, place, seed, matrices, *refs):
    pieces, (begun, products, full, held, start, sets, sems) = refs[:group], refs[group:]
    member = place[BACKWARD if backward else FORWARD]
    leads = place[BACKWARD_HEAD if backward else FORWARD_HEAD] == 1
    source = piece_refs(member, group, chunks, seed, 0, chunk, True)
    loads = load([(source, start), (matrices.at[backward, pl.ds(0, 2 * group)], sets)], sems, 0)
    for shift in range(group):
        held[lax.rem(member - shift + group, group)] = pieces[shift][...]
    finish(loads)
    shape = start.shape
    flat = flat_of(shape)
    state = jnp.where(leads, start[...], 0.0).reshape(flat)
    full[0] = state.reshape(shape)
    for slab in range(group - 1):
        step = sets[step_at(group, slab)]
        state = jnp.dot(split_rows(state), step, preferred_element_type=F32) + held[slab].reshape(flat)
        full[slab + 1] = state.reshape(shape)
    channels = shape[3]
    for shift in range(group):
        slab = lax.rem(member + shift, group)
        begun[shift] = full[slab]
        products[:, shift * channels : (shift + 1) * channels] = sets[before_at(group, slab)]


def partial_chain(place, seed, matrices, pieces, group, chunks, chunk, backward):
    shape = pieces[0].shape
    depth, channels = matrices.shape[2:]
    stack = (group,) + shape
    return pl.pallas_call(
        functools.partial(partial_kernel, group, chunks, chunk, int(backward)),
        out_shape=[jax.ShapeDtypeStruct(stack, F32), jax.ShapeDtypeStruct((depth, group * channels), BF16)],
        in_specs=[SMEM, ANY, ANY] + [VMEM] * group,
        out_specs=[VMEM] * 2,
        scratch_shapes=[
            pltpu.VMEM(stack, F32),
            pltpu.VMEM(stack, F32),
            pltpu.VMEM(shape, F32),
            pltpu.VMEM((2 * group, depth, channels), BF16),
            pltpu.SemaphoreType.DMA((2,)),
        ],
        compiler_params=params(24),
        cost_estimate=cost(0.8 * group, shape),
    )(place, seed, matrices, *pieces)


def hop_kernel(carry, whole, own, result):
    shape = own.shape
    moved = jnp.dot(split_rows(carry[...].reshape(flat_of(shape))), whole[...], preferred_element_type=F32)
    result[...] = own[...] + moved.reshape(shape)


def hop(carry, whole, own):
    return pl.pallas_call(
        hop_kernel,
        out_shape=jax.ShapeDtypeStruct(own.shape, F32),
        in_specs=[VMEM] * 3,
        out_specs=VMEM,
        compiler_params=params(24),
        cost_estimate=cost(0.8, own.shape),
    )(carry, whole, own)


def complete_kernel(group, carry, products, begun, *outs):
    shape = carry.shape
    channels = shape[3]
    moved = jnp.dot(split_rows(carry[...].reshape(flat_of(shape))), products[...], preferred_element_type=F32)
    for shift in range(group):
        part = moved[:, shift * channels : (shift + 1) * channels]
        outs[shift][...] = begun[shift] + part.reshape(shape)


def complete_chain(carry, products, begun, group):
    shape = carry.shape
    return pl.pallas_call(
        functools.partial(complete_kernel, group),
        out_shape=[jax.ShapeDtypeStruct(shape, F32)] * group,
        in_specs=[VMEM] * 3,
        out_specs=[VMEM] * group,
        compiler_params=params(24),
        cost_estimate=cost(0.2 * group, shape),
    )(carry, products, begun)


def middle_kernel(layers, group, chunks, place, *refs):
    count_pieces = group * len(chunks)
    pieces, refs = refs[:count_pieces], refs[count_pieces:]
    (offset_hbm, cotangent_hbm, next_k_hbm, next_f_hbm, own_k_hbm, own_f_hbm, own_decay, next_decay, matrix, turned) = refs[:10]
    refs = refs[10:]
    (slab_end, coarse_end, back_offset), refs = refs[:3], refs[3:]
    state_outs, refs = refs[:layers], refs[layers:]
    act_outs, refs = refs[:layers], refs[layers:]
    back_pieces, refs = refs[:count_pieces], refs[count_pieces:]
    (begins, states, acts, offset, cotangent, tops, adjoint, first_columns, second_columns) = refs[:9]
    tools, (kernels, turned_kernels, decays, sems) = refs[9:12], refs[12:]
    paired = tools[0]
    pairs = offset.shape[0]
    last_slab = place[POSITION] == place[SIZE] - 1

    brought = bring_in(place[FORWARD], group, chunks, pieces, begins, sems, 0)
    base = count_pieces
    loads = load(
        [
            (offset_hbm, offset),
            (next_k_hbm, kernels.at[0]),
            (cotangent_hbm, tops),
            (next_f_hbm, turned_kernels.at[0]),
            (own_k_hbm, kernels.at[1]),
            (own_f_hbm, turned_kernels.at[1]),
            (cotangent_hbm, cotangent),
        ],
        sems,
        base,
    )
    base += len(loads)
    decays[0] = next_decay[...]
    decays[1] = own_decay[...]
    clear_borders(first_columns)
    clear_borders(second_columns)
    finish(brought)
    loads[0].wait()

    def coarse_rows(first, count):
        rows = pl.ds(first, count)
        for odd in range(2):
            states[0, rows, odd] = transform_rows(begins[rows, odd], matrix[...]) + offset[rows, odd]

    per_block(pairs, coarse_rows, whole=True)
    fill_forward(states.at[0], first_columns)
    out_coarse = pltpu.make_async_copy(states.at[0], coarse_end, sems.at[base])
    out_coarse.start()
    base += 1
    finish(loads[1:])
    late = [(states.at[layers], slab_end)]
    late += [(states.at[n], state_outs[n]) for n in range(layers)]
    late += [(acts.at[n], act_outs[n]) for n in range(layers)]

    def both_sweeps(index, carry):
        now, later = first_columns, second_columns
        for layer in range(layers):
            spread(paired, kernels[index, layer])

            def store(rows, first, odd, following, activation, layer=layer, target=later):
                states[layer + 1, rows, odd] = following
                acts[layer, rows, odd] = activation
                if layer < layers - 1:
                    put_columns(target, first, odd, following)
                else:
                    put_columns(target, first, odd, scaled_rows(tops[rows, odd], activation))

            forward_layer(states.at[layer], now, tools, decays[index, layer : layer + 1], store)
            now, later = later, now

        @pl.when(index == 1)
        def _():
            load(late, sems, base)

        for layer in reversed(range(layers)):
            spread(paired, turned_kernels[index, layer])

            def store_back(rows, first, odd, following, layer=layer, target=later):
                adjoint[rows, odd] = following
                if layer > 0:
                    put_columns(target, first, odd, scaled_rows(following, acts[layer - 1, rows, odd]))

            source = tops if layer == layers - 1 else adjoint
            backward_layer(source, now, tools, decays[index, layer : layer + 1], store_back)
            now, later = later, now

        @pl.when(index == 0)
        def _():
            out_coarse.wait()

            def again(first, count):
                rows = pl.ds(first, count)
                tops[rows] = jnp.where(last_slab, cotangent[rows], adjoint[rows])
                for odd in range(2):
                    begin = begins[rows, odd]
                    states[0, rows, odd] = begin
                    put_columns(first_columns, first, odd, begin)

            per_block(pairs, again)

        return carry

    lax.fori_loop(0, 2, both_sweeps, 0)

    def subtract(first, count):
        rows = pl.ds(first, count)
        for odd in range(2):
            adjoint[rows, odd] = adjoint[rows, odd] - transform_rows(tops[rows, odd], turned[...])

    per_block(pairs, subtract, whole=True)
    outs = send_out(place[BACKWARD], group, chunks, adjoint, back_pieces, sems, 0)
    outs += load([(adjoint, back_offset)], sems, count_pieces)
    finish(outs)
    for number, (source, target) in enumerate(late):
        pltpu.make_async_copy(source, target, sems.at[base + number]).wait()


def middle(place, pieces, offset, cotangent, own, following, own_decay, next_decay, matrix, turned, group, chunks):
    layers = own[0].shape[0]
    field = offset.shape
    count = len(pieces)
    fields = [jax.ShapeDtypeStruct(field, F32)] * (3 + 2 * layers)
    results = pl.pallas_call(
        functools.partial(middle_kernel, layers, group, chunks),
        out_shape=fields + piece_shapes(field, group, chunks),
        in_specs=[SMEM] + [ANY] * (count + 6) + [VMEM] * 4,
        out_specs=[ANY] * (3 + 2 * layers + count),
        scratch_shapes=[pltpu.VMEM(field, F32)]
        + [pltpu.VMEM((layers + 1,) + field, F32), pltpu.VMEM((layers,) + field, F32)]
        + [pltpu.VMEM(field, F32)] * 4
        + scratch_of(field, 2)
        + [pltpu.VMEM((2,) + own[0].shape, BF16)] * 2
        + [pltpu.VMEM((2, layers, field[3]), F32), pltpu.SemaphoreType.DMA((count + 9 + 2 * layers,))],
        compiler_params=params(52),
        cost_estimate=cost(4.0 * layers, field),
    )(place, *pieces, offset, cotangent, *following, *own, own_decay, next_decay, matrix, turned)
    return results[:3], results[3 : 3 + layers], results[3 + layers : 3 + 2 * layers], results[3 + 2 * layers :]


def turn(whole, turned):
    taps, channels = whole.shape[0] // whole.shape[1], whole.shape[1]
    for tap in range(taps):
        block = whole[tap * channels : (tap + 1) * channels]
        other = taps - 1 - tap
        turned[other * channels : (other + 1) * channels] = block.T.astype(BF16)


def own_kernel(kernels, turned, whole):
    for layer in range(kernels.shape[0]):
        whole[...] = kernels[layer].astype(F32)
        turn(whole, turned.at[layer])


def turn_own(kernels):
    return pl.pallas_call(
        own_kernel,
        out_shape=jax.ShapeDtypeStruct(kernels.shape, BF16),
        in_specs=[VMEM],
        out_specs=VMEM,
        scratch_shapes=[pltpu.VMEM(kernels.shape[1:], F32)],
        compiler_params=params(),
    )(kernels)


def next_kernel(place, *refs):
    quarters, (kernels, turned, decay, whole) = refs[:4], refs[4:]
    layers = kernels.shape[0]
    rows = whole.shape[0] // 4
    chunk = lax.rem(place[CHUNK], 4)
    at = [chunk, chunk + 2 - 4 * (chunk // 2), chunk + 1 - 2 * lax.rem(chunk, 2)]
    at.append(at[2] + 2 - 4 * (chunk // 2))
    for layer in range(layers):
        for number in range(4):
            whole[pl.ds(at[number] * rows, rows)] = quarters[number][layer, 0:rows]
        kernels[layer] = whole[...].astype(BF16)
        turn(whole, turned.at[layer])
        decay[layer : layer + 1] = quarters[0][layer, rows : rows + 1]


def join_next(place, quarters):
    layers, rows, channels = quarters[0].shape
    shape = (layers, 4 * (rows - 8), channels)
    results = pl.pallas_call(
        next_kernel,
        out_shape=[jax.ShapeDtypeStruct(shape, BF16)] * 2 + [jax.ShapeDtypeStruct((layers, channels), F32)],
        in_specs=[SMEM] + [VMEM] * 4,
        out_specs=[VMEM] * 3,
        scratch_shapes=[pltpu.VMEM(shape[1:], F32)],
        compiler_params=params(),
    )(place, *quarters)
    return results[:2], results[2]


def turned_columns_kernel(state, turned, columns):
    pairs, _, side, _ = state.shape
    wide, depth = columns.shape[2:]
    clear_borders(columns)

    def fill(first, count):
        for odd in range(2):
            put_columns(columns, first, odd, state[pl.ds(first, count), odd])

    per_block(pairs, fill)
    for pair in range(pairs + 1):
        block = columns[pair].reshape(2 * wide, depth).astype(F32)
        turned[:, pair * 2 * wide : (pair + 1) * 2 * wide] = block.T.astype(BF16)


def turned_columns(state):
    shape = columns_shape(state.shape)
    return pl.pallas_call(
        turned_columns_kernel,
        out_shape=jax.ShapeDtypeStruct((shape[3], shape[0] * 2 * shape[2]), BF16),
        in_specs=[VMEM],
        out_specs=VMEM,
        scratch_shapes=[pltpu.VMEM(shape, BF16)],
        compiler_params=params(),
        cost_estimate=cost(0.4, state.shape),
    )(state)


def gradient_body(adjoint, activation, turned, ready, scaled, gradient, side):
    pairs = adjoint.shape[0]
    wide, channels = scaled.shape[2:]
    edge = jnp.zeros((2, wide, channels), BF16)
    scaled[0] = edge
    scaled[pairs + 1] = edge

    def fill(first, count):
        rows = pl.ds(first, count)
        for odd in range(2):
            own = scaled_rows(adjoint[rows, odd], activation[rows, odd])
            padded = jnp.concatenate([own, jnp.zeros((count, wide - side, channels), F32)], axis=1)
            scaled[pl.ds(first + 1, count), odd] = padded.astype(BF16)

    per_block(pairs, fill)
    ready()
    flat = scaled[...].reshape((2 * pairs + 4) * wide, channels)
    rows = (2 * pairs + 2) * wide
    shifted = [flat[(2 - tap) * wide : (2 - tap) * wide + rows] for tap in range(3)]
    products = jnp.dot(turned[...], jnp.concatenate(shifted, axis=1), preferred_element_type=F32)
    for row in range(3):
        for column in range(3):
            tap = 3 * row + column
            gradient[tap * channels : (tap + 1) * channels] = products[
                column * channels : (column + 1) * channels, row * channels : (row + 1) * channels
            ]


def scaled_shape(field):
    pairs, _, side, channels = field
    return (pairs + 2, 2, wide_of(side), channels)


def halve(place, gradient, keep, send):
    half = lax.rem(place[CHUNK], 2)
    rows = keep.shape[0]
    keep[...] = gradient[pl.ds(half * rows, rows)]
    send[...] = gradient[pl.ds((1 - half) * rows, rows)]


def top_kernel(group, chunks, place, *refs):
    count_pieces = group * len(chunks)
    pieces, refs = refs[:count_pieces], refs[count_pieces:]
    activation_hbm, turned_hbm, adjoint_out, keep, send = refs[:5]
    adjoint, activation, turned, shifted, gradient, sems = refs[5:]
    brought = bring_in(place[BACKWARD], group, chunks, pieces, adjoint, sems, 0)
    loads = load([(activation_hbm, activation), (turned_hbm, turned)], sems, count_pieces)
    finish(brought)
    out = load([(adjoint, adjoint_out)], sems, 0)
    loads[0].wait()
    gradient_body(adjoint, activation, turned, loads[1].wait, shifted, gradient, adjoint.shape[2])
    halve(place, gradient, keep, send)
    finish(out)


def top_gradient(place, pieces, activation, turned, group, chunks):
    field = activation.shape
    shape = columns_shape(field)
    taps = 9 * field[3]
    half = jax.ShapeDtypeStruct((taps // 2, field[3]), F32)
    return pl.pallas_call(
        functools.partial(top_kernel, group, chunks),
        out_shape=[jax.ShapeDtypeStruct(field, F32), half, half],
        in_specs=[SMEM] + [ANY] * (len(pieces) + 2),
        out_specs=[ANY, VMEM, VMEM],
        scratch_shapes=[
            pltpu.VMEM(field, F32),
            pltpu.VMEM(field, F32),
            pltpu.VMEM(turned.shape, BF16),
            pltpu.VMEM(scaled_shape(field), BF16),
            pltpu.VMEM((taps, field[3]), F32),
            pltpu.SemaphoreType.DMA((len(pieces) + 2,)),
        ],
        compiler_params=params(),
        cost_estimate=cost(1.5, field),
    )(place, *pieces, activation, turned)


def retreat_body(adjoint, activation, columns, tools, rate, store):
    clear_borders(columns)
    fill_backward(adjoint, activation, columns)
    backward_layer(adjoint, columns, tools, rate, store)


def lower_kernel(layer, place, adjoint, above, kernel, decay, below_hbm, turned_hbm, *refs):
    result_out, keep, send = refs[:3]
    result, below, turned, columns, paired, even, uneven, shifted, gradient, sems = refs[3:]
    loads = load([(below_hbm, below), (turned_hbm, turned)], sems, 0)
    spread(paired, kernel[layer])

    def store(rows, first, odd, fresh):
        result[rows, odd] = fresh

    retreat_body(adjoint, above, columns, (paired, even, uneven), decay[layer : layer + 1], store)
    out = load([(result, result_out)], sems, 2)
    loads[0].wait()
    gradient_body(result, below, turned, loads[1].wait, shifted, gradient, result.shape[2])
    halve(place, gradient, keep, send)
    finish(out)


def lower_gradient(place, layer, adjoint, above, kernels, decay, below, turned):
    field = adjoint.shape
    shape = columns_shape(field)
    taps = 9 * field[3]
    half = jax.ShapeDtypeStruct((taps // 2, field[3]), F32)
    return pl.pallas_call(
        functools.partial(lower_kernel, layer),
        out_shape=[jax.ShapeDtypeStruct(field, F32), half, half],
        in_specs=[SMEM] + [VMEM] * 4 + [ANY] * 2,
        out_specs=[ANY, VMEM, VMEM],
        scratch_shapes=[pltpu.VMEM(field, F32), pltpu.VMEM(field, F32), pltpu.VMEM(turned.shape, BF16)]
        + scratch_of(field, 1)
        + [pltpu.VMEM(scaled_shape(field), BF16), pltpu.VMEM((taps, field[3]), F32), pltpu.SemaphoreType.DMA((3,))],
        compiler_params=params(),
        cost_estimate=cost(2.0, field),
    )(place, adjoint, above, kernels, decay, below, turned)


def last_kernel(adjoint, activation, kernel, decay, tops, back_offset, turned, result, adjoint_end, columns, *tools):
    spread(tools[0], kernel[0])

    def store(rows, first, odd, fresh):
        result[rows, odd] = fresh

    retreat_body(adjoint, activation, columns, tools, decay[0:1], store)

    def coarse_rows(first, count):
        rows = pl.ds(first, count)
        for odd in range(2):
            adjoint_end[rows, odd] = transform_rows(tops[rows, odd], turned[...]) + back_offset[rows, odd]

    per_block(adjoint.shape[0], coarse_rows, whole=True)


def last_retreat(adjoint, activation, kernels, decay, tops, back_offset, turned):
    field = adjoint.shape
    return pl.pallas_call(
        last_kernel,
        out_shape=[jax.ShapeDtypeStruct(field, F32)] * 2,
        in_specs=[VMEM] * 7,
        out_specs=[VMEM] * 2,
        scratch_shapes=scratch_of(field, 1),
        compiler_params=params(),
        cost_estimate=cost(1.6, field),
    )(adjoint, activation, kernels, decay, tops, back_offset, turned)


def collect_kernel(layers, place, *refs):
    sources, out = refs[: 2 * layers], refs[2 * layers]
    half = lax.rem(place[CHUNK], 2)
    rows = out.shape[1] // 2
    for layer in range(layers):
        out[layer, pl.ds(half * rows, rows)] = sources[2 * layer][...]
        out[layer, pl.ds((1 - half) * rows, rows)] = sources[2 * layer + 1][...]


def collect(place, halves):
    layers = len(halves)
    rows, channels = halves[0][0].shape
    flat = [half for both in halves for half in both]
    return pl.pallas_call(
        functools.partial(collect_kernel, layers),
        out_shape=jax.ShapeDtypeStruct((layers, 2 * rows, channels), F32),
        in_specs=[SMEM] + [VMEM] * (2 * layers),
        out_specs=VMEM,
        compiler_params=params(16),
    )(place, *flat)


def from_behind(shard, axis, by):
    devices = lax.axis_size(axis)
    pairs = [(i, i + by) for i in range(devices) if 0 <= i + by < devices]
    return lax.ppermute(shard, axis, pairs)


def swap(shard, bit):
    return lax.ppermute(shard, "dp", [(i, i ^ bit) for i in range(lax.axis_size("dp"))])


def order_of(index, size, backward):
    return size - 1 - index if backward else index


def group_of(size):
    for group in (GROUP, 2, 1):
        if size % group == 0:
            return group


def exchange(pieces, group, backward):
    size = lax.axis_size("layer")
    received = [pieces[0]]
    for shift in range(1, group):
        pairs = []
        for order in range(size):
            base = order - order % group
            target = base + (order + shift) % group
            pairs.append((order_of(order, size, backward), order_of(target, size, backward)))
        received.append(lax.ppermute(pieces[shift], "layer", pairs))
    return received


def coarse_chain(place, seed, pieces, matrices, group, chunks, backward, beside=()):
    size = lax.axis_size("layer")
    pairs = [(order_of(i, size, backward), order_of(i + group, size, backward)) for i in range(size - group)]
    received = []
    for chunk in range(len(chunks)):
        sent = pieces[chunk * group : (chunk + 1) * group]
        if chunk > 0:
            received[-1][1], *sent = lax.optimization_barrier((received[-1][1], *sent))
        received.append(exchange(sent, group, backward))
    begins = []
    for chunk in range(len(chunks)):
        carry = jnp.zeros(pieces[chunk * group].shape, F32)
        if size > group:
            out = group_carry(place, seed, matrices, received[chunk], group, chunks, chunk, backward)
            carry = lax.ppermute(out, "layer", pairs)
            for _ in range(size // group - 2):
                carry = lax.ppermute(hop(carry, matrices[int(backward), whole_at(group)], out), "layer", pairs)
        begun, products = partial_chain(place, seed, matrices, received[chunk], group, chunks, chunk, backward)
        if chunk == len(chunks) - 1:
            begun, *beside = lax.optimization_barrier((begun, *beside))
        begins.append((carry, products, begun))
    result = []
    for carry, products, begun in begins:
        result += exchange(complete_chain(carry, products, begun, group), group, backward)
    return result, beside


def sum_across(total):
    bit = 2
    while bit < lax.axis_size("dp"):
        total = total + swap(total, bit)
        bit *= 2
    return total


def per_device(images, kernels, damping, cotangent):
    layers, taps, channels = kernels.shape
    _, height, side, _ = images.shape
    size = lax.axis_size("layer")
    position = lax.axis_index("layer")
    dp_at = lax.axis_index("dp")
    field = (height // 2, 2, side, channels)
    images = images.reshape(field)
    cotangent = cotangent.reshape(field)
    group = group_of(size)
    quarter = field[0] // group
    chunks = chunks_of(quarter)
    back_order = size - 1 - position
    place = jnp.stack(
        [
            position,
            lax.rem(position, group),
            lax.rem(back_order, group),
            dp_at,
            (position < group).astype(jnp.int32),
            (back_order < group).astype(jnp.int32),
            jnp.int32(size),
            jnp.int32(0),
        ]
    ).astype(jnp.int32)

    parts, quarter_part, copies, turned_matrix = prelude(place, kernels, damping, group)
    matrix = copies[0]

    lows = [from_behind(part, "layer", 1) for part in parts]
    highs = [swap(low, 1) for low in lows]

    groups = [list(range(at, at + group)) for at in range(0, size, group)]
    steps = lax.all_to_all(copies, "layer", 0, 0, axis_index_groups=groups, tiled=True)
    own = (kernels, turn_own(kernels))

    state = images
    for layer in range(layers - 1):
        state = fetched_layer(place, state, lows[layer], highs[layer])

    quarter_part, state = lax.optimization_barrier((quarter_part, state))
    first = from_behind(quarter_part, "layer", -1)

    offset, pieces = slab_offset(
        place, images, state, lows[-1], highs[-1], kernels, damping, matrix, group, chunks
    )
    first, pieces, steps = lax.optimization_barrier((first, pieces, steps))
    second = swap(first, 2)
    following, next_decay = join_next(place, [first, second, swap(first, 1), swap(second, 1)])
    matrices = group_matrices(steps)
    pieces, _ = coarse_chain(place, images, pieces, matrices, group, chunks, False)
    (slab_end, coarse_end, back_offset), states, acts, pieces = middle(
        place, pieces, offset, cotangent, own, following, damping, next_decay, matrix, turned_matrix, group, chunks
    )
    turned = [turned_columns(state) for state in states]
    pieces, turned = coarse_chain(place, cotangent, pieces, matrices, group, chunks, True, turned)
    tops, keep, send = top_gradient(place, pieces, acts[-1], turned[-1], group, chunks)
    adjoint = tops
    paired = [None] * layers
    halves = [None] * layers
    for layer in reversed(range(1, layers)):
        paired[layer] = (keep, send)
        adjoint, keep, send = lower_gradient(
            place, layer, adjoint, acts[layer], own[1], damping, acts[layer - 1], turned[layer - 1]
        )
        total = paired[layer][0] + swap(paired[layer][1], 1)
        adjoint, total = lax.optimization_barrier((adjoint, total))
        if layer < layers - 1:
            adjoint, summed = lax.optimization_barrier((adjoint, paired[layer + 1]))
            paired[layer + 1] = summed
        paired[layer] = sum_across(total)
    total = keep + swap(send, 1)
    adjoint, adjoint_end = last_retreat(adjoint, acts[0], own[1], damping, tops, back_offset, turned_matrix)
    adjoint, total = lax.optimization_barrier((adjoint, total))
    paired[0] = sum_across(total)
    halves = [(half, swap(half, 1)) for half in paired]
    full = (1, 1, height, side, channels)
    return (
        slab_end.reshape(full),
        coarse_end.reshape(full),
        adjoint.reshape(full),
        adjoint_end.reshape(full),
        collect(place, halves),
    )


def solution(mesh):
    in_specs = (
        P("dp", None, None, None),
        P("layer", None, None),
        P("layer", None),
        P("dp", None, None, None),
    )
    out_specs = (
        P("layer", "dp", None, None, None),
        P("layer", "dp", None, None, None),
        P("layer", "dp", None, None, None),
        P("layer", "dp", None, None, None),
        P("layer", None, None),
    )
    return jax.shard_map(
        per_device, mesh=mesh, in_specs=in_specs, out_specs=out_specs, check_vma=False
    )
```

```python
import functools
import math

import jax
import jax.numpy as jnp
from jax import lax
from jax.experimental import pallas as pl
from jax.experimental.pallas import tpu as pltpu
from jax.sharding import PartitionSpec as P

STEP = 0.125
F32 = jnp.float32
BF16 = jnp.bfloat16
BLOCK_PAIRS = 7
GROUP = 4


def wide_of(side):
    return -(-(side + 1) // 16) * 16


def columns_shape(field):
    pairs, _, side, channels = field
    return (pairs + 1, 2, wide_of(side), 3 * channels)


def block_of(pairs):
    return BLOCK_PAIRS if pairs % BLOCK_PAIRS == 0 else 1


def per_block(pairs, body, whole=False):
    block = block_of(pairs)

    def step(number, carry):
        if whole:
            body(number * block, block)
        else:
            for pair in range(block):
                body(number * block + pair, 1)
        return carry

    lax.fori_loop(0, pairs // block, step, 0)


def clear_borders(columns):
    edge = jnp.zeros(columns.shape[2:], BF16)
    columns[0, 0] = edge
    columns[columns.shape[0] - 1, 1] = edge


def put_columns(columns, first, odd, rows):
    count, side, channels = rows.shape
    wide = columns.shape[2]
    here = jnp.concatenate([rows, jnp.zeros((count, wide - side, channels), F32)], axis=1)
    left = pltpu.roll(here, 1, 1)
    right = pltpu.roll(here, wide - 1, 1)
    columns[pl.ds(first + odd, count), 1 - odd] = jnp.concatenate([left, here, right], axis=2).astype(BF16)


def spread(paired, kernel):
    taps, channels = kernel.shape
    third = taps // 3
    blank = jnp.zeros((third, channels), BF16)
    paired[0:taps, 0:channels] = kernel
    paired[taps : taps + third, 0:channels] = blank
    paired[0:third, channels : 2 * channels] = blank
    paired[third : taps + third, channels : 2 * channels] = kernel


def convolve(columns, paired, results, emit, side, ahead=None):
    _, _, wide, depth = columns.shape
    channels = depth // 3
    pairs = columns.shape[0] - 1
    block = block_of(pairs)

    def product(number):
        first = number * block
        pieces = [
            columns[first : first + block, 0],
            columns[first : first + block, 1],
            columns[first + 1 : first + 1 + block, 0],
            columns[first + 1 : first + 1 + block, 1],
        ]
        left = jnp.concatenate([piece.reshape(block * wide, depth) for piece in pieces], axis=1)
        results[number % 2][...] = jnp.dot(left, paired[...], preferred_element_type=F32)

    product(0)
    if ahead is not None:
        ahead()
    for number in range(pairs // block):
        if number + 1 < pairs // block:
            product(number + 1)
        result = results[number % 2]
        for pair in range(block):
            for odd in range(2):
                preact = result[pair * wide : (pair + 1) * wide, odd * channels : (odd + 1) * channels]
                emit(number * block + pair, odd, preact.reshape(1, wide, channels)[:, :side])


def split_dot(left, matrix):
    high = left.astype(BF16)
    low = (left - high.astype(F32)).astype(BF16)
    m_high = matrix.astype(BF16)
    m_low = (matrix - m_high.astype(F32)).astype(BF16)
    return jnp.dot(
        jnp.concatenate([high, low, high], axis=1),
        jnp.concatenate([m_high, m_high, m_low], axis=0),
        preferred_element_type=F32,
    )


def transform_rows(rows, matrix):
    count, side, channels = rows.shape
    return split_dot(rows.reshape(count * side, channels), matrix).reshape(rows.shape)


def fill_forward(state, columns):
    def fill(first, count):
        for odd in range(2):
            put_columns(columns, first, odd, state[pl.ds(first, count), odd])

    per_block(state.shape[0], fill)


def forward_layer(current, columns, tools, rate, store, ahead=None):
    decay = rate.reshape(1, 1, -1)

    def emit(first, odd, preact):
        rows = pl.ds(first, 1)
        activation = jnp.tanh(preact)
        here = current[rows, odd]
        store(rows, first, odd, here + STEP * (activation - decay * here), activation)

    convolve(columns, tools[0], tools[1:], emit, current.shape[2], ahead)


def scaled_rows(adjoint, activation):
    return STEP * (1.0 - activation * activation) * adjoint


def fill_backward(state, activation, columns):
    def fill(first, count):
        rows = pl.ds(first, count)
        for odd in range(2):
            put_columns(columns, first, odd, scaled_rows(state[rows, odd], activation[rows, odd]))

    per_block(state.shape[0], fill)


def backward_layer(current, columns, tools, rate, store, ahead=None):
    decay = rate.reshape(1, 1, -1)

    def emit(first, odd, back_term):
        rows = pl.ds(first, 1)
        here = current[rows, odd]
        store(rows, first, odd, here - STEP * decay * here + back_term)

    convolve(columns, tools[0], tools[1:], emit, current.shape[2], ahead)


def params(mebibytes=40):
    return pltpu.CompilerParams(vmem_limit_bytes=mebibytes * 1024 * 1024)


def cost(share, shape):
    flops = 8 * share * math.prod(shape) * shape[-1] * 9
    return pl.CostEstimate(flops=int(flops), bytes_accessed=int(8 * share * math.prod(shape)), transcendentals=0)


ANY = pl.BlockSpec(memory_space=pl.ANY)
VMEM = pl.BlockSpec(memory_space=pltpu.VMEM)
SMEM = pl.BlockSpec(memory_space=pltpu.SMEM)

def chunks_of(quarter):
    return (quarter - quarter // 2, quarter // 2) if quarter > 1 else (quarter,)


POSITION, FORWARD, BACKWARD, CHUNK, FORWARD_HEAD, BACKWARD_HEAD, SIZE = range(7)


def load(pairs_of_refs, sems, base):
    copies = []
    for number, (source, target) in enumerate(pairs_of_refs):
        copies.append(pltpu.make_async_copy(source, target, sems.at[base + number]))
        copies[-1].start()
    return copies


def finish(copies):
    for copy in copies:
        copy.wait()


def scratch_of(field, buffers):
    shape = columns_shape(field)
    products = pltpu.VMEM((block_of(field[0]) * shape[2], 2 * field[3]), F32)
    return [pltpu.VMEM(shape, BF16)] * buffers + [pltpu.VMEM((4 * shape[3], 2 * field[3]), BF16), products, products]


def join_halves(whole, low, high, half):
    rows = whole.shape[0] // 2
    whole[pl.ds(half * rows, rows)] = low[0:rows].astype(BF16)
    whole[pl.ds((1 - half) * rows, rows)] = high[0:rows].astype(BF16)


def layer_kernel(place, field, low, high, result, columns, paired, even, uneven, whole):
    half = lax.rem(place[CHUNK], 2)
    join_halves(whole, low, high, half)
    spread(paired, whole[...])
    rows = whole.shape[0] // 2
    clear_borders(columns)
    fill_forward(field, columns)

    def store(where, first, odd, following, activation):
        result[where, odd] = following

    forward_layer(field, columns, (paired, even, uneven), low[rows : rows + 1], store)


def fetched_layer(place, field, low, high):
    rows, channels = low.shape[0] - 8, low.shape[1]
    return pl.pallas_call(
        layer_kernel,
        out_shape=jax.ShapeDtypeStruct(field.shape, F32),
        in_specs=[SMEM] + [VMEM] * 3,
        out_specs=VMEM,
        scratch_shapes=scratch_of(field.shape, 1) + [pltpu.VMEM((2 * rows, channels), BF16)],
        compiler_params=params(),
        cost_estimate=cost(1.0, field.shape),
    )(place, field, low, high)


def piece_refs(member, group, chunks, field, shift, chunk, forward_shift):
    quarter = field.shape[0] // group
    offset = sum(chunks[:chunk])
    turn = member + shift if forward_shift else member - shift + group
    return field.at[pl.ds(lax.rem(turn, group) * quarter + offset, chunks[chunk])]


def send_out(member, group, chunks, field, outs, sems, base):
    copies = []
    for chunk in range(len(chunks)):
        for shift in range(group):
            number = chunk * group + shift
            source = piece_refs(member, group, chunks, field, shift, chunk, True)
            copies.append(pltpu.make_async_copy(source, outs[number], sems.at[base + number]))
            copies[-1].start()
    return copies


def bring_in(member, group, chunks, pieces, field, sems, base):
    copies = []
    for chunk in range(len(chunks)):
        for shift in range(group):
            number = chunk * group + shift
            target = piece_refs(member, group, chunks, field, shift, chunk, False)
            copies.append(pltpu.make_async_copy(pieces[number], target, sems.at[base + number]))
            copies[-1].start()
    return copies


def piece_shapes(field, group, chunks):
    return [jax.ShapeDtypeStruct((count,) + field[1:], F32) for count in chunks for _ in range(group)]


def offset_kernel(layers, group, chunks, place, images_hbm, field, low, high, kernels_hbm, decay, matrix, *refs):
    count_pieces = group * len(chunks)
    out, pieces = refs[0], refs[1 : 1 + count_pieces]
    images, kernels, starts, offset, now, later, paired, even, uneven, spare, whole, sems = refs[1 + count_pieces :]
    pair_of = [paired, spare]
    pairs = offset.shape[0]
    loads = load([(images_hbm, images), (kernels_hbm, kernels)], sems, 0)
    half = lax.rem(place[CHUNK], 2)
    first_slab = place[POSITION] == 0
    join_halves(whole, low, high, half)
    spread(paired, whole[...])
    rows = whole.shape[0] // 2
    clear_borders(now)
    clear_borders(later)
    fill_forward(field, now)
    finish(loads)

    def store_start(where, first, odd, following, activation):
        begin = jnp.where(first_slab, images[where, odd], following)
        starts[where, odd] = begin
        put_columns(later, first, odd, begin)

    def ahead_of(layer):
        if layer >= layers:
            return None
        return lambda: spread(pair_of[(layer + 1) % 2], kernels[layer])

    forward_layer(field, now, (paired, even, uneven), low[rows : rows + 1], store_start, ahead_of(0))
    for layer in range(layers):
        now, later = later, now
        tools = (pair_of[(layer + 1) % 2], even, uneven)

        def store(where, first, odd, following, activation, last=layer == layers - 1, target=later):
            if not last:
                put_columns(target, first, odd, following)
            offset[where, odd] = following

        source = starts if layer == 0 else offset
        forward_layer(source, now, tools, decay[layer : layer + 1], store, ahead_of(layer + 1))

    def subtract(first, count):
        where = pl.ds(first, count)
        for odd in range(2):
            offset[where, odd] = offset[where, odd] - transform_rows(starts[where, odd], matrix[...])

    per_block(pairs, subtract, whole=True)

    copies = send_out(place[FORWARD], group, chunks, offset, pieces, sems, 3)
    copies += load([(offset, out)], sems, 2)
    finish(copies)


def slab_offset(place, images, field, low, high, kernels, decay, matrix, group, chunks):
    layers, taps, channels = kernels.shape
    shape = images.shape
    count = group * len(chunks)
    results = pl.pallas_call(
        functools.partial(offset_kernel, layers, group, chunks),
        out_shape=[jax.ShapeDtypeStruct(shape, F32)] + piece_shapes(shape, group, chunks),
        in_specs=[SMEM, ANY, VMEM, VMEM, VMEM, ANY, VMEM, VMEM],
        out_specs=[ANY] * (1 + count),
        scratch_shapes=[pltpu.VMEM(shape, F32), pltpu.VMEM(kernels.shape, BF16)]
        + [pltpu.VMEM(shape, F32)] * 2
        + scratch_of(shape, 2)
        + scratch_of(shape, 0)[:1]
        + [pltpu.VMEM((taps, channels), BF16), pltpu.SemaphoreType.DMA((3 + count,))],
        compiler_params=params(60),
        cost_estimate=cost(layers + 1.0, shape),
    )(place, images, field, low, high, kernels, decay, matrix)
    return results[0], results[1:]


def split_matrix(matrix):
    high = matrix.astype(BF16)
    low = (matrix - high.astype(F32)).astype(BF16)
    return jnp.concatenate([high, high, low], axis=0)


def split_rows(rows):
    high = rows.astype(BF16)
    low = (rows - high.astype(F32)).astype(BF16)
    return jnp.concatenate([high, low, high], axis=1)


def identity(channels):
    rows = lax.broadcasted_iota(jnp.int32, (channels, channels), 0)
    columns = lax.broadcasted_iota(jnp.int32, (channels, channels), 1)
    return (rows == columns).astype(F32)


def prelude_kernel(place, kernels, damping, *outs):
    layers, taps, channels = kernels.shape
    parts, (quarter, matrix, turned) = outs[:layers], outs[layers:]
    half_rows, quarter_rows = taps // 2, taps // 4
    half, chunk = lax.rem(place[CHUNK], 2), lax.rem(place[CHUNK], 4)
    for layer in range(layers):
        rate = jnp.broadcast_to(damping[layer : layer + 1], (8, channels))
        parts[layer][0:half_rows] = kernels[layer, pl.ds(half * half_rows, half_rows)].astype(F32)
        parts[layer][half_rows : half_rows + 8] = rate
        quarter[layer, 0:quarter_rows] = kernels[layer, pl.ds(chunk * quarter_rows, quarter_rows)].astype(F32)
        quarter[layer, quarter_rows : quarter_rows + 8] = rate
    total = kernels[0, 0:channels].astype(F32)
    for tap in range(1, taps // channels):
        total += kernels[0, tap * channels : (tap + 1) * channels].astype(F32)
    diagonal = identity(channels) * (1.0 - layers * STEP * damping[0:1])
    coarse = diagonal + layers * STEP * total
    for member in range(matrix.shape[0]):
        matrix[member] = coarse
    turned[...] = coarse.T


def prelude(place, kernels, damping, group):
    layers, taps, channels = kernels.shape
    part = jax.ShapeDtypeStruct((taps // 2 + 8, channels), F32)
    quarter = jax.ShapeDtypeStruct((layers, taps // 4 + 8, channels), F32)
    square = jax.ShapeDtypeStruct((channels, channels), F32)
    results = pl.pallas_call(
        prelude_kernel,
        out_shape=[part] * layers + [quarter, jax.ShapeDtypeStruct((group, channels, channels), F32), square],
        in_specs=[SMEM] + [VMEM] * 2,
        out_specs=[VMEM] * (layers + 3),
        compiler_params=params(60),
    )(place, kernels, damping)
    return results[:layers], *results[layers:]


def step_at(group, index):
    return index


def before_at(group, index):
    return group + index


def after_at(group, index):
    return 2 * group + index


def whole_at(group):
    return 3 * group


def matrices_kernel(group, held, out):
    channels = held.shape[1]
    for backward in range(2):
        ordered = [held[group - 1 - step].T if backward else held[step] for step in range(group)]
        product = identity(channels)
        for step in range(group):
            split = split_matrix(ordered[step])
            out[backward, step_at(group, step)] = split
            out[backward, before_at(group, step)] = split_matrix(product)
            product = ordered[0] if step == 0 else jnp.dot(split_rows(product), split, preferred_element_type=F32)
        out[backward, whole_at(group)] = split_matrix(product)
        product = identity(channels)
        for step in reversed(range(group)):
            out[backward, after_at(group, step)] = split_matrix(product)
            if step == group - 1:
                product = ordered[step]
            else:
                product = jnp.dot(split_rows(ordered[step]), split_matrix(product), preferred_element_type=F32)


def group_matrices(steps):
    group, channels, _ = steps.shape
    return pl.pallas_call(
        functools.partial(matrices_kernel, group),
        out_shape=jax.ShapeDtypeStruct((2, 3 * group + 1, 3 * channels, channels), BF16),
        in_specs=[VMEM],
        out_specs=VMEM,
        compiler_params=params(16),
    )(steps)


def flat_of(shape):
    return (shape[0] * shape[1] * shape[2], shape[3])


def carry_kernel(group, chunks, chunk, backward, place, seed, matrices, *refs):
    pieces, (carry, start, right, sems) = refs[:group], refs[group:]
    member = place[BACKWARD if backward else FORWARD]
    leads = place[BACKWARD_HEAD if backward else FORWARD_HEAD] == 1
    depth = right.shape[0] // (group + 1)
    source = piece_refs(member, group, chunks, seed, 0, chunk, True)
    loads = [(source, start), (matrices.at[backward, whole_at(group)], right.at[pl.ds(group * depth, depth)])]
    for shift in range(group):
        slab = lax.rem(member - shift + group, group)
        loads.append((matrices.at[backward, after_at(group, slab)], right.at[pl.ds(shift * depth, depth)]))
    loads = load(loads, sems, 0)
    flat = flat_of(start.shape)
    left = [split_rows(pieces[shift][...].reshape(flat)) for shift in range(group)]
    finish(loads)
    left.append(split_rows(jnp.where(leads, start[...], 0.0).reshape(flat)))
    total = jnp.dot(jnp.concatenate(left, axis=1), right[...], preferred_element_type=F32)
    carry[...] = total.reshape(start.shape)


def group_carry(place, seed, matrices, pieces, group, chunks, chunk, backward):
    shape = pieces[0].shape
    depth, channels = matrices.shape[2:]
    return pl.pallas_call(
        functools.partial(carry_kernel, group, chunks, chunk, int(backward)),
        out_shape=jax.ShapeDtypeStruct(shape, F32),
        in_specs=[SMEM, ANY, ANY] + [VMEM] * group,
        out_specs=VMEM,
        scratch_shapes=[
            pltpu.VMEM(shape, F32),
            pltpu.VMEM(((group + 1) * depth, channels), BF16),
            pltpu.SemaphoreType.DMA((group + 2,)),
        ],
        compiler_params=params(24),
        cost_estimate=cost(1.0 * group, shape),
    )(place, seed, matrices, *pieces)


def partial_kernel(group, chunks, chunk, backward, place, seed, matrices, *refs):
    pieces, (begun, products, full, held, start, sets, sems) = refs[:group], refs[group:]
    member = place[BACKWARD if backward else FORWARD]
    leads = place[BACKWARD_HEAD if backward else FORWARD_HEAD] == 1
    source = piece_refs(member, group, chunks, seed, 0, chunk, True)
    loads = load([(source, start), (matrices.at[backward, pl.ds(0, 2 * group)], sets)], sems, 0)
    for shift in range(group):
        held[lax.rem(member - shift + group, group)] = pieces[shift][...]
    finish(loads)
    shape = start.shape
    flat = flat_of(shape)
    state = jnp.where(leads, start[...], 0.0).reshape(flat)
    full[0] = state.reshape(shape)
    for slab in range(group - 1):
        step = sets[step_at(group, slab)]
        state = jnp.dot(split_rows(state), step, preferred_element_type=F32) + held[slab].reshape(flat)
        full[slab + 1] = state.reshape(shape)
    channels = shape[3]
    for shift in range(group):
        slab = lax.rem(member + shift, group)
        begun[shift] = full[slab]
        products[:, shift * channels : (shift + 1) * channels] = sets[before_at(group, slab)]


def partial_chain(place, seed, matrices, pieces, group, chunks, chunk, backward):
    shape = pieces[0].shape
    depth, channels = matrices.shape[2:]
    stack = (group,) + shape
    return pl.pallas_call(
        functools.partial(partial_kernel, group, chunks, chunk, int(backward)),
        out_shape=[jax.ShapeDtypeStruct(stack, F32), jax.ShapeDtypeStruct((depth, group * channels), BF16)],
        in_specs=[SMEM, ANY, ANY] + [VMEM] * group,
        out_specs=[VMEM] * 2,
        scratch_shapes=[
            pltpu.VMEM(stack, F32),
            pltpu.VMEM(stack, F32),
            pltpu.VMEM(shape, F32),
            pltpu.VMEM((2 * group, depth, channels), BF16),
            pltpu.SemaphoreType.DMA((2,)),
        ],
        compiler_params=params(24),
        cost_estimate=cost(0.0, shape),
    )(place, seed, matrices, *pieces)


def hop_kernel(carry, whole, own, result):
    shape = own.shape
    moved = jnp.dot(split_rows(carry[...].reshape(flat_of(shape))), whole[...], preferred_element_type=F32)
    result[...] = own[...] + moved.reshape(shape)


def hop(carry, whole, own):
    return pl.pallas_call(
        hop_kernel,
        out_shape=jax.ShapeDtypeStruct(own.shape, F32),
        in_specs=[VMEM] * 3,
        out_specs=VMEM,
        compiler_params=params(24),
        cost_estimate=cost(0.8, own.shape),
    )(carry, whole, own)


def complete_kernel(group, carry, products, begun, *outs):
    shape = carry.shape
    channels = shape[3]
    moved = jnp.dot(split_rows(carry[...].reshape(flat_of(shape))), products[...], preferred_element_type=F32)
    for shift in range(group):
        part = moved[:, shift * channels : (shift + 1) * channels]
        outs[shift][...] = begun[shift] + part.reshape(shape)


def complete_chain(carry, products, begun, group):
    shape = carry.shape
    return pl.pallas_call(
        functools.partial(complete_kernel, group),
        out_shape=[jax.ShapeDtypeStruct(shape, F32)] * group,
        in_specs=[VMEM] * 3,
        out_specs=[VMEM] * group,
        compiler_params=params(24),
        cost_estimate=cost(0.0, shape),
    )(carry, products, begun)


def middle_kernel(layers, group, chunks, place, *refs):
    count_pieces = group * len(chunks)
    pieces, refs = refs[:count_pieces], refs[count_pieces:]
    (offset_hbm, cotangent_hbm, next_k_hbm, next_f_hbm, own_k_hbm, own_f_hbm, own_decay, next_decay, matrix, turned) = refs[:10]
    refs = refs[10:]
    (slab_end, coarse_end, back_offset), refs = refs[:3], refs[3:]
    state_outs, refs = refs[:layers], refs[layers:]
    act_outs, refs = refs[:layers], refs[layers:]
    back_pieces, refs = refs[:count_pieces], refs[count_pieces:]
    (begins, states, acts, offset, cotangent, tops, adjoint, first_columns, second_columns) = refs[:9]
    pair_of, blocks = (refs[9], refs[12]), refs[10:12]
    kernels, turned_kernels, decays, sems = refs[13:]
    pairs = offset.shape[0]
    last_slab = place[POSITION] == place[SIZE] - 1

    brought = bring_in(place[FORWARD], group, chunks, pieces, begins, sems, 0)
    base = count_pieces
    loads = load(
        [
            (offset_hbm, offset),
            (next_k_hbm, kernels.at[0]),
            (cotangent_hbm, tops),
            (next_f_hbm, turned_kernels.at[0]),
            (own_k_hbm, kernels.at[1]),
            (own_f_hbm, turned_kernels.at[1]),
            (cotangent_hbm, cotangent),
        ],
        sems,
        base,
    )
    base += len(loads)
    decays[0] = next_decay[...]
    decays[1] = own_decay[...]
    clear_borders(first_columns)
    clear_borders(second_columns)
    finish(brought)
    loads[0].wait()

    def coarse_rows(first, count):
        rows = pl.ds(first, count)
        for odd in range(2):
            states[0, rows, odd] = transform_rows(begins[rows, odd], matrix[...]) + offset[rows, odd]

    per_block(pairs, coarse_rows, whole=True)
    fill_forward(states.at[0], first_columns)
    out_coarse = pltpu.make_async_copy(states.at[0], coarse_end, sems.at[base])
    out_coarse.start()
    base += 1
    finish(loads[1:])
    late = [(states.at[layers], slab_end)]
    late += [(states.at[n], state_outs[n]) for n in range(layers)]
    late += [(acts.at[n], act_outs[n]) for n in range(layers)]

    def both_sweeps(index, carry):
        now, later = first_columns, second_columns
        order = [(kernels, layer) for layer in range(layers)]
        order += [(turned_kernels, layer) for layer in reversed(range(layers))]

        def ahead_of(number):
            if number >= len(order):
                return None
            source, layer = order[number]
            return lambda: spread(pair_of[number % 2], source[index, layer])

        ahead_of(0)()
        for layer in range(layers):
            number = layer

            def store(rows, first, odd, following, activation, layer=layer, target=later):
                states[layer + 1, rows, odd] = following
                acts[layer, rows, odd] = activation
                if layer < layers - 1:
                    put_columns(target, first, odd, following)
                else:
                    put_columns(target, first, odd, scaled_rows(tops[rows, odd], activation))

            tools = (pair_of[number % 2], *blocks)
            rate = decays[index, layer : layer + 1]
            forward_layer(states.at[layer], now, tools, rate, store, ahead_of(number + 1))
            now, later = later, now

        @pl.when(index == 1)
        def _():
            load(late, sems, base)

        for layer in reversed(range(layers)):
            number += 1

            def store_back(rows, first, odd, following, layer=layer, target=later):
                adjoint[rows, odd] = following
                if layer > 0:
                    put_columns(target, first, odd, scaled_rows(following, acts[layer - 1, rows, odd]))

            source = tops if layer == layers - 1 else adjoint
            tools = (pair_of[number % 2], *blocks)
            rate = decays[index, layer : layer + 1]
            backward_layer(source, now, tools, rate, store_back, ahead_of(number + 1))
            now, later = later, now

        @pl.when(index == 0)
        def _():
            out_coarse.wait()

            def again(first, count):
                rows = pl.ds(first, count)
                tops[rows] = jnp.where(last_slab, cotangent[rows], adjoint[rows])
                for odd in range(2):
                    begin = begins[rows, odd]
                    states[0, rows, odd] = begin
                    put_columns(first_columns, first, odd, begin)

            per_block(pairs, again)

        return carry

    lax.fori_loop(0, 2, both_sweeps, 0)

    def subtract(first, count):
        rows = pl.ds(first, count)
        for odd in range(2):
            adjoint[rows, odd] = adjoint[rows, odd] - transform_rows(tops[rows, odd], turned[...])

    per_block(pairs, subtract, whole=True)
    outs = send_out(place[BACKWARD], group, chunks, adjoint, back_pieces, sems, 0)
    outs += load([(adjoint, back_offset)], sems, count_pieces)
    finish(outs)
    for number, (source, target) in enumerate(late):
        pltpu.make_async_copy(source, target, sems.at[base + number]).wait()


def middle(place, pieces, offset, cotangent, own, following, own_decay, next_decay, matrix, turned, group, chunks):
    layers = own[0].shape[0]
    field = offset.shape
    count = len(pieces)
    fields = [jax.ShapeDtypeStruct(field, F32)] * (3 + 2 * layers)
    results = pl.pallas_call(
        functools.partial(middle_kernel, layers, group, chunks),
        out_shape=fields + piece_shapes(field, group, chunks),
        in_specs=[SMEM] + [ANY] * (count + 6) + [VMEM] * 4,
        out_specs=[ANY] * (3 + 2 * layers + count),
        scratch_shapes=[pltpu.VMEM(field, F32)]
        + [pltpu.VMEM((layers + 1,) + field, F32), pltpu.VMEM((layers,) + field, F32)]
        + [pltpu.VMEM(field, F32)] * 4
        + scratch_of(field, 2)
        + scratch_of(field, 0)[:1]
        + [pltpu.VMEM((2,) + own[0].shape, BF16)] * 2
        + [pltpu.VMEM((2, layers, field[3]), F32), pltpu.SemaphoreType.DMA((count + 9 + 2 * layers,))],
        compiler_params=params(52),
        cost_estimate=cost(4.0 * layers, field),
    )(place, *pieces, offset, cotangent, *following, *own, own_decay, next_decay, matrix, turned)
    return results[:3], results[3 : 3 + layers], results[3 + layers : 3 + 2 * layers], results[3 + 2 * layers :]


def turn(whole, turned):
    taps, channels = whole.shape[0] // whole.shape[1], whole.shape[1]
    for tap in range(taps):
        block = whole[tap * channels : (tap + 1) * channels]
        other = taps - 1 - tap
        turned[other * channels : (other + 1) * channels] = block.T.astype(BF16)


def own_kernel(kernels, turned, whole):
    for layer in range(kernels.shape[0]):
        whole[...] = kernels[layer].astype(F32)
        turn(whole, turned.at[layer])


def turn_own(kernels):
    return pl.pallas_call(
        own_kernel,
        out_shape=jax.ShapeDtypeStruct(kernels.shape, BF16),
        in_specs=[VMEM],
        out_specs=VMEM,
        scratch_shapes=[pltpu.VMEM(kernels.shape[1:], F32)],
        compiler_params=params(),
    )(kernels)


def next_kernel(place, *refs):
    quarters, (kernels, turned, decay, whole) = refs[:4], refs[4:]
    layers = kernels.shape[0]
    rows = whole.shape[0] // 4
    chunk = lax.rem(place[CHUNK], 4)
    at = [chunk, chunk + 2 - 4 * (chunk // 2), chunk + 1 - 2 * lax.rem(chunk, 2)]
    at.append(at[2] + 2 - 4 * (chunk // 2))
    for layer in range(layers):
        for number in range(4):
            whole[pl.ds(at[number] * rows, rows)] = quarters[number][layer, 0:rows]
        kernels[layer] = whole[...].astype(BF16)
        turn(whole, turned.at[layer])
        decay[layer : layer + 1] = quarters[0][layer, rows : rows + 1]


def join_next(place, quarters):
    layers, rows, channels = quarters[0].shape
    shape = (layers, 4 * (rows - 8), channels)
    results = pl.pallas_call(
        next_kernel,
        out_shape=[jax.ShapeDtypeStruct(shape, BF16)] * 2 + [jax.ShapeDtypeStruct((layers, channels), F32)],
        in_specs=[SMEM] + [VMEM] * 4,
        out_specs=[VMEM] * 3,
        scratch_shapes=[pltpu.VMEM(shape[1:], F32)],
        compiler_params=params(),
    )(place, *quarters)
    return results[:2], results[2]


def turned_columns_kernel(state, turned, columns):
    pairs, _, side, _ = state.shape
    wide, depth = columns.shape[2:]
    clear_borders(columns)

    def fill(first, count):
        for odd in range(2):
            put_columns(columns, first, odd, state[pl.ds(first, count), odd])

    per_block(pairs, fill)
    for pair in range(pairs + 1):
        block = columns[pair].reshape(2 * wide, depth).astype(F32)
        turned[:, pair * 2 * wide : (pair + 1) * 2 * wide] = block.T.astype(BF16)


def turned_columns(state):
    shape = columns_shape(state.shape)
    return pl.pallas_call(
        turned_columns_kernel,
        out_shape=jax.ShapeDtypeStruct((shape[3], shape[0] * 2 * shape[2]), BF16),
        in_specs=[VMEM],
        out_specs=VMEM,
        scratch_shapes=[pltpu.VMEM(shape, BF16)],
        compiler_params=params(),
        cost_estimate=cost(0.0, state.shape),
    )(state)


def gradient_body(adjoint, activation, turned, ready, scaled, gradient, side):
    pairs = adjoint.shape[0]
    wide, channels = scaled.shape[2:]
    edge = jnp.zeros((2, wide, channels), BF16)
    scaled[0] = edge
    scaled[pairs + 1] = edge

    def fill(first, count):
        rows = pl.ds(first, count)
        for odd in range(2):
            own = scaled_rows(adjoint[rows, odd], activation[rows, odd])
            padded = jnp.concatenate([own, jnp.zeros((count, wide - side, channels), F32)], axis=1)
            scaled[pl.ds(first + 1, count), odd] = padded.astype(BF16)

    per_block(pairs, fill)
    ready()
    flat = scaled[...].reshape((2 * pairs + 4) * wide, channels)
    rows = (2 * pairs + 2) * wide
    shifted = [flat[(2 - tap) * wide : (2 - tap) * wide + rows] for tap in range(3)]
    products = jnp.dot(turned[...], jnp.concatenate(shifted, axis=1), preferred_element_type=F32)
    for row in range(3):
        for column in range(3):
            tap = 3 * row + column
            gradient[tap * channels : (tap + 1) * channels] = products[
                column * channels : (column + 1) * channels, row * channels : (row + 1) * channels
            ]


def scaled_shape(field):
    pairs, _, side, channels = field
    return (pairs + 2, 2, wide_of(side), channels)


def halve(place, gradient, keep, send):
    half = lax.rem(place[CHUNK], 2)
    rows = keep.shape[0]
    keep[...] = gradient[pl.ds(half * rows, rows)]
    send[...] = gradient[pl.ds((1 - half) * rows, rows)]


def top_kernel(group, chunks, place, *refs):
    count_pieces = group * len(chunks)
    pieces, refs = refs[:count_pieces], refs[count_pieces:]
    activation_hbm, turned_hbm, adjoint_out, keep, send = refs[:5]
    adjoint, activation, turned, shifted, gradient, sems = refs[5:]
    brought = bring_in(place[BACKWARD], group, chunks, pieces, adjoint, sems, 0)
    loads = load([(activation_hbm, activation), (turned_hbm, turned)], sems, count_pieces)
    finish(brought)
    out = load([(adjoint, adjoint_out)], sems, 0)
    loads[0].wait()
    gradient_body(adjoint, activation, turned, loads[1].wait, shifted, gradient, adjoint.shape[2])
    halve(place, gradient, keep, send)
    finish(out)


def top_gradient(place, pieces, activation, turned, group, chunks):
    field = activation.shape
    shape = columns_shape(field)
    taps = 9 * field[3]
    half = jax.ShapeDtypeStruct((taps // 2, field[3]), F32)
    return pl.pallas_call(
        functools.partial(top_kernel, group, chunks),
        out_shape=[jax.ShapeDtypeStruct(field, F32), half, half],
        in_specs=[SMEM] + [ANY] * (len(pieces) + 2),
        out_specs=[ANY, VMEM, VMEM],
        scratch_shapes=[
            pltpu.VMEM(field, F32),
            pltpu.VMEM(field, F32),
            pltpu.VMEM(turned.shape, BF16),
            pltpu.VMEM(scaled_shape(field), BF16),
            pltpu.VMEM((taps, field[3]), F32),
            pltpu.SemaphoreType.DMA((len(pieces) + 2,)),
        ],
        compiler_params=params(),
        cost_estimate=cost(1.5, field),
    )(place, *pieces, activation, turned)


def retreat_body(adjoint, activation, columns, tools, rate, store):
    clear_borders(columns)
    fill_backward(adjoint, activation, columns)
    backward_layer(adjoint, columns, tools, rate, store)


def lower_kernel(layer, place, adjoint, above, kernel, decay, below_hbm, turned_hbm, *refs):
    result_out, keep, send = refs[:3]
    result, below, turned, columns, paired, even, uneven, shifted, gradient, sems = refs[3:]
    loads = load([(below_hbm, below), (turned_hbm, turned)], sems, 0)
    spread(paired, kernel[layer])

    def store(rows, first, odd, fresh):
        result[rows, odd] = fresh

    retreat_body(adjoint, above, columns, (paired, even, uneven), decay[layer : layer + 1], store)
    out = load([(result, result_out)], sems, 2)
    loads[0].wait()
    gradient_body(result, below, turned, loads[1].wait, shifted, gradient, result.shape[2])
    halve(place, gradient, keep, send)
    finish(out)


def lower_gradient(place, layer, adjoint, above, kernels, decay, below, turned):
    field = adjoint.shape
    shape = columns_shape(field)
    taps = 9 * field[3]
    half = jax.ShapeDtypeStruct((taps // 2, field[3]), F32)
    return pl.pallas_call(
        functools.partial(lower_kernel, layer),
        out_shape=[jax.ShapeDtypeStruct(field, F32), half, half],
        in_specs=[SMEM] + [VMEM] * 4 + [ANY] * 2,
        out_specs=[ANY, VMEM, VMEM],
        scratch_shapes=[pltpu.VMEM(field, F32), pltpu.VMEM(field, F32), pltpu.VMEM(turned.shape, BF16)]
        + scratch_of(field, 1)
        + [pltpu.VMEM(scaled_shape(field), BF16), pltpu.VMEM((taps, field[3]), F32), pltpu.SemaphoreType.DMA((3,))],
        compiler_params=params(),
        cost_estimate=cost(2.0, field),
    )(place, adjoint, above, kernels, decay, below, turned)


def last_kernel(adjoint, activation, kernel, decay, tops, back_offset, turned, result, adjoint_end, columns, *tools):
    spread(tools[0], kernel[0])

    def store(rows, first, odd, fresh):
        result[rows, odd] = fresh

    retreat_body(adjoint, activation, columns, tools, decay[0:1], store)

    def coarse_rows(first, count):
        rows = pl.ds(first, count)
        for odd in range(2):
            adjoint_end[rows, odd] = transform_rows(tops[rows, odd], turned[...]) + back_offset[rows, odd]

    per_block(adjoint.shape[0], coarse_rows, whole=True)


def last_retreat(adjoint, activation, kernels, decay, tops, back_offset, turned):
    field = adjoint.shape
    return pl.pallas_call(
        last_kernel,
        out_shape=[jax.ShapeDtypeStruct(field, F32)] * 2,
        in_specs=[VMEM] * 7,
        out_specs=[VMEM] * 2,
        scratch_shapes=scratch_of(field, 1),
        compiler_params=params(),
        cost_estimate=cost(1.6, field),
    )(adjoint, activation, kernels, decay, tops, back_offset, turned)


def collect_kernel(layers, place, *refs):
    sources, out, held, sems = refs[:-3], refs[-3], refs[-2], refs[-1]
    half = lax.rem(place[CHUNK], 2)
    rows = out.shape[1] // 2
    if layers > 0:
        number = 0
        copies = []
        for layer in range(layers):
            for part in [half, 1 - half][: 1 if layer == 0 else 2]:
                copies.append((sources[number], out.at[layer, pl.ds(part * rows, rows)]))
                number += 1
        finish(load(copies, sems, 0))
    else:
        finish(load([(sources[0], out.at[0, pl.ds((1 - half) * rows, rows)])], sems, 0))


def collect(place, halves):
    layers = len(halves)
    rows, channels = halves[0][0].shape
    shape = jax.ShapeDtypeStruct((layers, 2 * rows, channels), F32)
    most = [half for both in halves for half in both]
    last = most.pop(1)
    scratch = [pltpu.VMEM((8, channels), F32), pltpu.SemaphoreType.DMA((2 * layers,))]
    out = pl.pallas_call(
        functools.partial(collect_kernel, layers),
        out_shape=shape,
        in_specs=[SMEM] + [VMEM] * len(most),
        out_specs=ANY,
        scratch_shapes=scratch,
        compiler_params=params(16),
        cost_estimate=cost(0.4, (rows, 2 * layers, channels)),
    )(place, *most)
    return pl.pallas_call(
        functools.partial(collect_kernel, 0),
        out_shape=shape,
        in_specs=[SMEM, VMEM, ANY],
        out_specs=ANY,
        scratch_shapes=scratch,
        input_output_aliases={2: 0},
        compiler_params=params(16),
    )(place, last, out)


def from_behind(shard, axis, by):
    devices = lax.axis_size(axis)
    pairs = [(i, i + by) for i in range(devices) if 0 <= i + by < devices]
    return lax.ppermute(shard, axis, pairs)


def swap(shard, bit):
    return lax.ppermute(shard, "dp", [(i, i ^ bit) for i in range(lax.axis_size("dp"))])


def order_of(index, size, backward):
    return size - 1 - index if backward else index


def group_of(size):
    for group in (GROUP, 2, 1):
        if size % group == 0:
            return group


def exchange(pieces, group, backward):
    size = lax.axis_size("layer")
    received = [pieces[0]]
    for shift in range(1, group):
        pairs = []
        for order in range(size):
            base = order - order % group
            target = base + (order + shift) % group
            pairs.append((order_of(order, size, backward), order_of(target, size, backward)))
        received.append(lax.ppermute(pieces[shift], "layer", pairs))
    return received


def coarse_chain(place, seed, pieces, matrices, group, chunks, backward, beside=()):
    size = lax.axis_size("layer")
    pairs = [(order_of(i, size, backward), order_of(i + group, size, backward)) for i in range(size - group)]
    received = []
    for chunk in range(len(chunks)):
        sent = pieces[chunk * group : (chunk + 1) * group]
        if chunk > 0:
            received[-1][1], *sent = lax.optimization_barrier((received[-1][1], *sent))
        received.append(exchange(sent, group, backward))
    carries = [jnp.zeros(pieces[chunk * group].shape, F32) for chunk in range(len(chunks))]
    if size > group:
        for chunk in range(len(chunks)):
            out = group_carry(place, seed, matrices, received[chunk], group, chunks, chunk, backward)
            carry = lax.ppermute(out, "layer", pairs)
            for _ in range(size // group - 2):
                carry = lax.ppermute(hop(carry, matrices[int(backward), whole_at(group)], out), "layer", pairs)
            carries[chunk] = carry
        received, out = lax.optimization_barrier((received, out))
    partials = [
        partial_chain(place, seed, matrices, received[chunk], group, chunks, chunk, backward)
        for chunk in range(len(chunks))
    ]
    partials, beside = lax.optimization_barrier((partials, beside))
    begins = [(carry, products, begun) for carry, (begun, products) in zip(carries, partials)]
    result = []
    for carry, products, begun in begins:
        result += exchange(complete_chain(carry, products, begun, group), group, backward)
    return result, beside


def sum_across(total):
    bit = 2
    while bit < lax.axis_size("dp"):
        total = total + swap(total, bit)
        bit *= 2
    return total


def per_device(images, kernels, damping, cotangent):
    layers, taps, channels = kernels.shape
    _, height, side, _ = images.shape
    size = lax.axis_size("layer")
    position = lax.axis_index("layer")
    dp_at = lax.axis_index("dp")
    field = (height // 2, 2, side, channels)
    images = images.reshape(field)
    cotangent = cotangent.reshape(field)
    group = group_of(size)
    quarter = field[0] // group
    chunks = chunks_of(quarter)
    back_order = size - 1 - position
    place = jnp.stack(
        [
            position,
            lax.rem(position, group),
            lax.rem(back_order, group),
            dp_at,
            (position < group).astype(jnp.int32),
            (back_order < group).astype(jnp.int32),
            jnp.int32(size),
            jnp.int32(0),
        ]
    ).astype(jnp.int32)

    parts, quarter_part, copies, turned_matrix = prelude(place, kernels, damping, group)
    matrix = copies[0]

    lows = [from_behind(part, "layer", 1) for part in parts]
    highs = [swap(low, 1) for low in lows]

    groups = [list(range(at, at + group)) for at in range(0, size, group)]
    steps = lax.all_to_all(copies, "layer", 0, 0, axis_index_groups=groups, tiled=True)
    own = (kernels, turn_own(kernels))

    state = images
    for layer in range(layers - 1):
        state = fetched_layer(place, state, lows[layer], highs[layer])

    quarter_part, state = lax.optimization_barrier((quarter_part, state))
    first = from_behind(quarter_part, "layer", -1)

    offset, pieces = slab_offset(
        place, images, state, lows[-1], highs[-1], kernels, damping, matrix, group, chunks
    )
    first, pieces, steps = lax.optimization_barrier((first, pieces, steps))
    second = swap(first, 2)
    following, next_decay = join_next(place, [first, second, swap(first, 1), swap(second, 1)])
    matrices = group_matrices(steps)
    pieces, _ = coarse_chain(place, images, pieces, matrices, group, chunks, False)
    (slab_end, coarse_end, back_offset), states, acts, pieces = middle(
        place, pieces, offset, cotangent, own, following, damping, next_decay, matrix, turned_matrix, group, chunks
    )
    turned = [turned_columns(state) for state in states]
    pieces, turned = coarse_chain(place, cotangent, pieces, matrices, group, chunks, True, turned)
    tops, keep, send = top_gradient(place, pieces, acts[-1], turned[-1], group, chunks)
    adjoint = tops
    paired = [None] * layers
    halves = [None] * layers
    for layer in reversed(range(1, layers)):
        paired[layer] = (keep, send)
        adjoint, keep, send = lower_gradient(
            place, layer, adjoint, acts[layer], own[1], damping, acts[layer - 1], turned[layer - 1]
        )
        total = paired[layer][0] + swap(paired[layer][1], 1)
        adjoint, total = lax.optimization_barrier((adjoint, total))
        if layer < layers - 1:
            adjoint, summed = lax.optimization_barrier((adjoint, paired[layer + 1]))
            paired[layer + 1] = summed
        paired[layer] = sum_across(total)
    total = keep + swap(send, 1)
    adjoint, adjoint_end = last_retreat(adjoint, acts[0], own[1], damping, tops, back_offset, turned_matrix)
    adjoint, total = lax.optimization_barrier((adjoint, total))
    paired[0] = sum_across(total)
    halves = [(half, swap(half, 1)) for half in paired]
    full = (1, 1, height, side, channels)
    return (
        slab_end.reshape(full),
        coarse_end.reshape(full),
        adjoint.reshape(full),
        adjoint_end.reshape(full),
        collect(place, halves),
    )


def solution(mesh):
    in_specs = (
        P("dp", None, None, None),
        P("layer", None, None),
        P("layer", None),
        P("dp", None, None, None),
    )
    out_specs = (
        P("layer", "dp", None, None, None),
        P("layer", "dp", None, None, None),
        P("layer", "dp", None, None, None),
        P("layer", "dp", None, None, None),
        P("layer", None, None),
    )
    return jax.shard_map(
        per_device, mesh=mesh, in_specs=in_specs, out_specs=out_specs, check_vma=False
    )
```

```python
import functools
import math

import jax
import jax.numpy as jnp
from jax import lax
from jax.experimental import pallas as pl
from jax.experimental.pallas import tpu as pltpu
from jax.sharding import PartitionSpec as P

STEP = 0.125
F32 = jnp.float32
BF16 = jnp.bfloat16
BLOCK_PAIRS = 7
PRODUCT_PAIRS = 14
GROUP = 4


def wide_of(side):
    return -(-(side + 1) // 16) * 16


def columns_shape(field):
    pairs, _, side, channels = field
    return (pairs + 1, 2, wide_of(side), 3 * channels)


def block_of(pairs):
    return BLOCK_PAIRS if pairs % BLOCK_PAIRS == 0 else 1


def product_block(pairs):
    return PRODUCT_PAIRS if pairs % PRODUCT_PAIRS == 0 else block_of(pairs)


def per_block(pairs, body, whole=False):
    block = block_of(pairs)

    def step(number, carry):
        if whole:
            body(number * block, block)
        else:
            for pair in range(block):
                body(number * block + pair, 1)
        return carry

    lax.fori_loop(0, pairs // block, step, 0)


def clear_borders(columns):
    edge = jnp.zeros(columns.shape[2:], BF16)
    columns[0, 0] = edge
    columns[columns.shape[0] - 1, 1] = edge


def put_columns(columns, first, odd, rows):
    count, side, channels = rows.shape
    wide = columns.shape[2]
    here = jnp.concatenate([rows, jnp.zeros((count, wide - side, channels), F32)], axis=1)
    left = pltpu.roll(here, 1, 1)
    right = pltpu.roll(here, wide - 1, 1)
    columns[pl.ds(first + odd, count), 1 - odd] = jnp.concatenate([left, here, right], axis=2).astype(BF16)


def spread(paired, kernel):
    taps, channels = kernel.shape
    third = taps // 3
    blank = jnp.zeros((third, channels), BF16)
    paired[0:taps, 0:channels] = kernel
    paired[taps : taps + third, 0:channels] = blank
    paired[0:third, channels : 2 * channels] = blank
    paired[third : taps + third, channels : 2 * channels] = kernel


def convolve(columns, paired, results, emit, side):
    _, _, wide, depth = columns.shape
    channels = depth // 3
    pairs = columns.shape[0] - 1
    block = product_block(pairs)

    def product(number):
        first = number * block
        pieces = [
            columns[first : first + block, 0],
            columns[first : first + block, 1],
            columns[first + 1 : first + 1 + block, 0],
            columns[first + 1 : first + 1 + block, 1],
        ]
        left = jnp.concatenate([piece.reshape(block * wide, depth) for piece in pieces], axis=1)
        results[number % 2][...] = jnp.dot(left, paired[...], preferred_element_type=F32)

    product(0)
    for number in range(pairs // block):
        if number + 1 < pairs // block:
            product(number + 1)
        result = results[number % 2]
        for pair in range(block):
            for odd in range(2):
                preact = result[pair * wide : (pair + 1) * wide, odd * channels : (odd + 1) * channels]
                emit(number * block + pair, odd, preact.reshape(1, wide, channels)[:, :side])


def split_dot(left, matrix):
    high = left.astype(BF16)
    low = (left - high.astype(F32)).astype(BF16)
    m_high = matrix.astype(BF16)
    m_low = (matrix - m_high.astype(F32)).astype(BF16)
    return jnp.dot(
        jnp.concatenate([high, low, high], axis=1),
        jnp.concatenate([m_high, m_high, m_low], axis=0),
        preferred_element_type=F32,
    )


def transform_rows(rows, matrix):
    count, side, channels = rows.shape
    return split_dot(rows.reshape(count * side, channels), matrix).reshape(rows.shape)


def fill_forward(state, columns):
    def fill(first, count):
        for odd in range(2):
            put_columns(columns, first, odd, state[pl.ds(first, count), odd])

    per_block(state.shape[0], fill)


def forward_layer(current, columns, tools, rate, store):
    decay = rate.reshape(1, 1, -1)

    def emit(first, odd, preact):
        rows = pl.ds(first, 1)
        activation = jnp.tanh(preact)
        here = current[rows, odd]
        store(rows, first, odd, here + STEP * (activation - decay * here), activation)

    convolve(columns, tools[0], tools[1:], emit, current.shape[2])


def scaled_rows(adjoint, activation):
    return STEP * (1.0 - activation * activation) * adjoint


def fill_backward(state, activation, columns):
    def fill(first, count):
        rows = pl.ds(first, count)
        for odd in range(2):
            put_columns(columns, first, odd, scaled_rows(state[rows, odd], activation[rows, odd]))

    per_block(state.shape[0], fill)


def backward_layer(current, columns, tools, rate, store):
    decay = rate.reshape(1, 1, -1)

    def emit(first, odd, back_term):
        rows = pl.ds(first, 1)
        here = current[rows, odd]
        store(rows, first, odd, here - STEP * decay * here + back_term)

    convolve(columns, tools[0], tools[1:], emit, current.shape[2])


def params(mebibytes=40):
    return pltpu.CompilerParams(vmem_limit_bytes=mebibytes * 1024 * 1024)


def cost(share, shape, free=False):
    share = 0.0 if free else share
    flops = 8 * share * math.prod(shape) * shape[-1] * 9
    return pl.CostEstimate(flops=int(flops), bytes_accessed=int(8 * share * math.prod(shape)), transcendentals=0)


ANY = pl.BlockSpec(memory_space=pl.ANY)
VMEM = pl.BlockSpec(memory_space=pltpu.VMEM)
SMEM = pl.BlockSpec(memory_space=pltpu.SMEM)

def chunks_of(quarter):
    return (quarter - quarter // 2, quarter // 2) if quarter > 1 else (quarter,)


POSITION, FORWARD, BACKWARD, CHUNK, FORWARD_HEAD, BACKWARD_HEAD, SIZE = range(7)


def load(pairs_of_refs, sems, base):
    copies = []
    for number, (source, target) in enumerate(pairs_of_refs):
        copies.append(pltpu.make_async_copy(source, target, sems.at[base + number]))
        copies[-1].start()
    return copies


def finish(copies):
    for copy in copies:
        copy.wait()


def scratch_of(field, buffers):
    shape = columns_shape(field)
    products = pltpu.VMEM((product_block(field[0]) * shape[2], 2 * field[3]), F32)
    return [pltpu.VMEM(shape, BF16)] * buffers + [pltpu.VMEM((4 * shape[3], 2 * field[3]), BF16), products, products]


def join_halves(whole, low, high, half):
    rows = whole.shape[0] // 2
    whole[pl.ds(half * rows, rows)] = low[0:rows].astype(BF16)
    whole[pl.ds((1 - half) * rows, rows)] = high[0:rows].astype(BF16)


def layer_kernel(place, field, low, high, result, columns, paired, even, uneven, whole):
    half = (place[CHUNK] & 1)
    join_halves(whole, low, high, half)
    spread(paired, whole[...])
    rows = whole.shape[0] // 2
    clear_borders(columns)
    fill_forward(field, columns)

    def store(where, first, odd, following, activation):
        result[where, odd] = following

    forward_layer(field, columns, (paired, even, uneven), low[rows : rows + 1], store)


def fetched_layer(place, field, low, high):
    rows, channels = low.shape[0] - 8, low.shape[1]
    return pl.pallas_call(
        layer_kernel,
        out_shape=jax.ShapeDtypeStruct(field.shape, F32),
        in_specs=[SMEM] + [VMEM] * 3,
        out_specs=VMEM,
        scratch_shapes=scratch_of(field.shape, 1) + [pltpu.VMEM((2 * rows, channels), BF16)],
        compiler_params=params(),
        cost_estimate=cost(1.0, field.shape),
    )(place, field, low, high)


def wrapped(index, group):
    return index & (group - 1)


def piece_refs(member, group, chunks, field, shift, chunk, forward_shift):
    quarter = field.shape[0] // group
    offset = sum(chunks[:chunk])
    turn = member + shift if forward_shift else member - shift + group
    return field.at[pl.ds(wrapped(turn, group) * quarter + offset, chunks[chunk])]


def subtract_and_send(member, group, chunks, field, tops, matrix, outs, sems, base):
    quarter = field.shape[0] // group
    copies = []
    for shift in [*range(1, group), 0]:
        rows = pl.ds(wrapped(member + shift, group) * quarter, quarter)
        for odd in range(2):
            field[rows, odd] = field[rows, odd] - transform_rows(tops[rows, odd], matrix[...])
        for chunk in range(len(chunks)):
            number = chunk * group + shift
            source = piece_refs(member, group, chunks, field, shift, chunk, True)
            copies.append(pltpu.make_async_copy(source, outs[number], sems.at[base + number]))
            copies[-1].start()
    return copies


def bring_in(member, group, chunks, pieces, field, sems, base):
    copies = []
    for chunk in range(len(chunks)):
        for shift in range(group):
            number = chunk * group + shift
            target = piece_refs(member, group, chunks, field, shift, chunk, False)
            copies.append(pltpu.make_async_copy(pieces[number], target, sems.at[base + number]))
            copies[-1].start()
    return copies


def piece_shapes(field, group, chunks):
    return [jax.ShapeDtypeStruct((count,) + field[1:], F32) for count in chunks for _ in range(group)]


def offset_kernel(layers, group, chunks, place, images_hbm, field, low, high, kernels_hbm, decay, matrix, *refs):
    count_pieces = group * len(chunks)
    out, pieces = refs[0], refs[1 : 1 + count_pieces]
    images, kernels, starts, offset, now, later, paired, even, uneven, whole, sems = refs[1 + count_pieces :]
    tools = (paired, even, uneven)
    pairs = offset.shape[0]
    loads = load([(images_hbm, images), (kernels_hbm, kernels)], sems, 0)
    half = (place[CHUNK] & 1)
    first_slab = place[POSITION] == 0
    join_halves(whole, low, high, half)
    spread(paired, whole[...])
    rows = whole.shape[0] // 2
    clear_borders(now)
    clear_borders(later)
    fill_forward(field, now)
    loads[0].wait()

    def store_start(where, first, odd, following, activation):
        begin = jnp.where(first_slab, images[where, odd], following)
        starts[where, odd] = begin
        put_columns(later, first, odd, begin)

    forward_layer(field, now, tools, low[rows : rows + 1], store_start)
    loads[1].wait()
    for layer in range(layers):
        now, later = later, now
        spread(paired, kernels[layer])

        def store(where, first, odd, following, activation, last=layer == layers - 1, target=later):
            if not last:
                put_columns(target, first, odd, following)
            offset[where, odd] = following

        source = starts if layer == 0 else offset
        forward_layer(source, now, tools, decay[layer : layer + 1], store)

    copies = subtract_and_send(place[FORWARD], group, chunks, offset, starts, matrix, pieces, sems, 3)
    copies += load([(offset, out)], sems, 2)
    finish(copies)


def slab_offset(place, images, field, low, high, kernels, decay, matrix, group, chunks):
    layers, taps, channels = kernels.shape
    shape = images.shape
    count = group * len(chunks)
    results = pl.pallas_call(
        functools.partial(offset_kernel, layers, group, chunks),
        out_shape=[jax.ShapeDtypeStruct(shape, F32)] + piece_shapes(shape, group, chunks),
        in_specs=[SMEM, ANY, VMEM, VMEM, VMEM, ANY, VMEM, VMEM],
        out_specs=[ANY] * (1 + count),
        scratch_shapes=[pltpu.VMEM(shape, F32), pltpu.VMEM(kernels.shape, BF16)]
        + [pltpu.VMEM(shape, F32)] * 2
        + scratch_of(shape, 2)
        + [pltpu.VMEM((taps, channels), BF16), pltpu.SemaphoreType.DMA((3 + count,))],
        compiler_params=params(60),
        cost_estimate=cost(layers + 1.0, shape),
    )(place, images, field, low, high, kernels, decay, matrix)
    return results[0], results[1:]


def split_matrix(matrix):
    high = matrix.astype(BF16)
    low = (matrix - high.astype(F32)).astype(BF16)
    return jnp.concatenate([high, high, low], axis=0)


def split_rows(rows):
    high = rows.astype(BF16)
    low = (rows - high.astype(F32)).astype(BF16)
    return jnp.concatenate([high, low, high], axis=1)


def identity(channels):
    rows = lax.broadcasted_iota(jnp.int32, (channels, channels), 0)
    columns = lax.broadcasted_iota(jnp.int32, (channels, channels), 1)
    return (rows == columns).astype(F32)


def prelude_kernel(place, kernels, damping, *outs):
    layers, taps, channels = kernels.shape
    parts, (quarter, copies, matrix, turned) = outs[:layers], outs[layers:]
    half_rows, quarter_rows = taps // 2, taps // 4
    half, chunk = (place[CHUNK] & 1), (place[CHUNK] & 3)
    for layer in range(layers):
        rate = jnp.broadcast_to(damping[layer : layer + 1], (8, channels))
        parts[layer][0:half_rows] = kernels[layer, pl.ds(half * half_rows, half_rows)].astype(F32)
        parts[layer][half_rows : half_rows + 8] = rate
        quarter[layer, 0:quarter_rows] = kernels[layer, pl.ds(chunk * quarter_rows, quarter_rows)].astype(F32)
        quarter[layer, quarter_rows : quarter_rows + 8] = rate
    total = kernels[0, 0:channels].astype(F32)
    for tap in range(1, taps // channels):
        total += kernels[0, tap * channels : (tap + 1) * channels].astype(F32)
    diagonal = identity(channels) * (1.0 - layers * STEP * damping[0:1])
    coarse = diagonal + layers * STEP * total
    for member in range(copies.shape[0]):
        copies[member] = coarse
    matrix[...] = coarse
    turned[...] = coarse.T


def prelude(place, kernels, damping, group):
    layers, taps, channels = kernels.shape
    part = jax.ShapeDtypeStruct((taps // 2 + 8, channels), F32)
    quarter = jax.ShapeDtypeStruct((layers, taps // 4 + 8, channels), F32)
    square = jax.ShapeDtypeStruct((channels, channels), F32)
    results = pl.pallas_call(
        prelude_kernel,
        out_shape=[part] * layers + [quarter, jax.ShapeDtypeStruct((group, channels, channels), F32), square, square],
        in_specs=[SMEM] + [VMEM] * 2,
        out_specs=[VMEM] * (layers + 4),
        compiler_params=params(60),
    )(place, kernels, damping)
    return results[:layers], *results[layers:]


def step_at(group, index):
    return index


def before_at(group, index):
    return group + index


def after_at(group, index):
    return 2 * group + index


def whole_at(group):
    return 3 * group


def matrices_kernel(group, held, out):
    channels = held.shape[1]
    for backward in range(2):
        ordered = [held[group - 1 - step].T if backward else held[step] for step in range(group)]
        product = identity(channels)
        for step in range(group):
            split = split_matrix(ordered[step])
            out[backward, step_at(group, step)] = split
            out[backward, before_at(group, step)] = split_matrix(product)
            product = ordered[0] if step == 0 else jnp.dot(split_rows(product), split, preferred_element_type=F32)
        out[backward, whole_at(group)] = split_matrix(product)
        product = identity(channels)
        for step in reversed(range(group)):
            out[backward, after_at(group, step)] = split_matrix(product)
            if step == group - 1:
                product = ordered[step]
            else:
                product = jnp.dot(split_rows(ordered[step]), split_matrix(product), preferred_element_type=F32)


def group_matrices(steps):
    group, channels, _ = steps.shape
    return pl.pallas_call(
        functools.partial(matrices_kernel, group),
        out_shape=jax.ShapeDtypeStruct((2, 3 * group + 1, 3 * channels, channels), BF16),
        in_specs=[VMEM],
        out_specs=VMEM,
        compiler_params=params(16),
    )(steps)


def flat_of(shape):
    return (shape[0] * shape[1] * shape[2], shape[3])


def carry_kernel(group, chunks, chunk, backward, place, seed, matrices, *refs):
    pieces, (carry, start, right, sems) = refs[:group], refs[group:]
    member = place[BACKWARD if backward else FORWARD]
    leads = place[BACKWARD_HEAD if backward else FORWARD_HEAD] == 1
    depth = right.shape[0] // (group + 1)
    source = piece_refs(member, group, chunks, seed, 0, chunk, True)
    loads = [(source, start), (matrices.at[backward, whole_at(group)], right.at[pl.ds(group * depth, depth)])]
    for shift in range(group):
        slab = wrapped(member - shift + group, group)
        loads.append((matrices.at[backward, after_at(group, slab)], right.at[pl.ds(shift * depth, depth)]))
    loads = load(loads, sems, 0)
    flat = flat_of(start.shape)
    left = [split_rows(pieces[shift][...].reshape(flat)) for shift in range(group)]
    finish(loads)
    left.append(split_rows(jnp.where(leads, start[...], 0.0).reshape(flat)))
    total = jnp.dot(jnp.concatenate(left, axis=1), right[...], preferred_element_type=F32)
    carry[...] = total.reshape(start.shape)


def group_carry(place, seed, matrices, pieces, group, chunks, chunk, backward):
    shape = pieces[0].shape
    depth, channels = matrices.shape[2:]
    return pl.pallas_call(
        functools.partial(carry_kernel, group, chunks, chunk, int(backward)),
        out_shape=jax.ShapeDtypeStruct(shape, F32),
        in_specs=[SMEM, ANY, ANY] + [VMEM] * group,
        out_specs=VMEM,
        scratch_shapes=[
            pltpu.VMEM(shape, F32),
            pltpu.VMEM(((group + 1) * depth, channels), BF16),
            pltpu.SemaphoreType.DMA((group + 2,)),
        ],
        compiler_params=params(24),
        cost_estimate=cost(1.0 * group, shape),
    )(place, seed, matrices, *pieces)


def partial_kernel(group, chunks, chunk, backward, place, seed, matrices, *refs):
    pieces, (begun, products, full, held, start, sets, sems) = refs[:group], refs[group:]
    member = place[BACKWARD if backward else FORWARD]
    leads = place[BACKWARD_HEAD if backward else FORWARD_HEAD] == 1
    source = piece_refs(member, group, chunks, seed, 0, chunk, True)
    loads = load([(source, start), (matrices.at[backward, pl.ds(0, 2 * group)], sets)], sems, 0)
    for shift in range(group):
        held[wrapped(member - shift + group, group)] = pieces[shift][...]
    finish(loads)
    shape = start.shape
    flat = flat_of(shape)
    state = jnp.where(leads, start[...], 0.0).reshape(flat)
    full[0] = state.reshape(shape)
    for slab in range(group - 1):
        step = sets[step_at(group, slab)]
        state = jnp.dot(split_rows(state), step, preferred_element_type=F32) + held[slab].reshape(flat)
        full[slab + 1] = state.reshape(shape)
    channels = shape[3]
    for shift in range(group):
        slab = wrapped(member + shift, group)
        begun[shift] = full[slab]
        products[:, shift * channels : (shift + 1) * channels] = sets[before_at(group, slab)]


def partial_chain(place, seed, matrices, pieces, group, chunks, chunk, backward):
    shape = pieces[0].shape
    depth, channels = matrices.shape[2:]
    stack = (group,) + shape
    return pl.pallas_call(
        functools.partial(partial_kernel, group, chunks, chunk, int(backward)),
        out_shape=[jax.ShapeDtypeStruct(stack, F32), jax.ShapeDtypeStruct((depth, group * channels), BF16)],
        in_specs=[SMEM, ANY, ANY] + [VMEM] * group,
        out_specs=[VMEM] * 2,
        scratch_shapes=[
            pltpu.VMEM(stack, F32),
            pltpu.VMEM(stack, F32),
            pltpu.VMEM(shape, F32),
            pltpu.VMEM((2 * group, depth, channels), BF16),
            pltpu.SemaphoreType.DMA((2,)),
        ],
        compiler_params=params(24),
        cost_estimate=cost(0.8 * group, shape, not backward),
    )(place, seed, matrices, *pieces)


def hop_kernel(carry, whole, own, result):
    shape = own.shape
    moved = jnp.dot(split_rows(carry[...].reshape(flat_of(shape))), whole[...], preferred_element_type=F32)
    result[...] = own[...] + moved.reshape(shape)


def hop(carry, whole, own):
    return pl.pallas_call(
        hop_kernel,
        out_shape=jax.ShapeDtypeStruct(own.shape, F32),
        in_specs=[VMEM] * 3,
        out_specs=VMEM,
        compiler_params=params(24),
        cost_estimate=cost(0.8, own.shape),
    )(carry, whole, own)


def complete_kernel(group, carry, products, begun, *outs):
    shape = carry.shape
    channels = shape[3]
    moved = jnp.dot(split_rows(carry[...].reshape(flat_of(shape))), products[...], preferred_element_type=F32)
    for shift in range(group):
        part = moved[:, shift * channels : (shift + 1) * channels]
        outs[shift][...] = begun[shift] + part.reshape(shape)


def complete_chain(carry, products, begun, group):
    shape = carry.shape
    return pl.pallas_call(
        functools.partial(complete_kernel, group),
        out_shape=[jax.ShapeDtypeStruct(shape, F32)] * group,
        in_specs=[VMEM] * 3,
        out_specs=[VMEM] * group,
        compiler_params=params(24),
        cost_estimate=cost(0.2 * group, shape),
    )(carry, products, begun)


def middle_kernel(layers, group, chunks, place, *refs):
    count_pieces = group * len(chunks)
    pieces, refs = refs[:count_pieces], refs[count_pieces:]
    (offset_hbm, cotangent_hbm, next_k_hbm, next_f_hbm, own_k_hbm, own_f_hbm, own_decay, next_decay, matrix, turned) = refs[:10]
    refs = refs[10:]
    (slab_end, coarse_end, back_offset), refs = refs[:3], refs[3:]
    state_outs, refs = refs[:layers], refs[layers:]
    act_outs, refs = refs[:layers], refs[layers:]
    back_pieces, refs = refs[:count_pieces], refs[count_pieces:]
    (begins, states, acts, offset, cotangent, tops, adjoint, first_columns, second_columns) = refs[:9]
    tools, (kernels, turned_kernels, decays, sems) = refs[9:12], refs[12:]
    paired = tools[0]
    pairs = offset.shape[0]
    last_slab = place[POSITION] == place[SIZE] - 1

    brought = bring_in(place[FORWARD], group, chunks, pieces, begins, sems, 0)
    base = count_pieces
    loads = load(
        [
            (offset_hbm, offset),
            (next_k_hbm, kernels.at[0]),
            (cotangent_hbm, tops),
            (next_f_hbm, turned_kernels.at[0]),
            (own_k_hbm, kernels.at[1]),
            (own_f_hbm, turned_kernels.at[1]),
            (cotangent_hbm, cotangent),
        ],
        sems,
        base,
    )
    base += len(loads)
    decays[0] = next_decay[...]
    decays[1] = own_decay[...]
    clear_borders(first_columns)
    clear_borders(second_columns)
    finish(brought)
    loads[0].wait()

    def coarse_rows(first, count):
        rows = pl.ds(first, count)
        for odd in range(2):
            states[0, rows, odd] = transform_rows(begins[rows, odd], matrix[...]) + offset[rows, odd]

    per_block(pairs, coarse_rows, whole=True)
    fill_forward(states.at[0], first_columns)
    out_coarse = pltpu.make_async_copy(states.at[0], coarse_end, sems.at[base])
    out_coarse.start()
    base += 1
    finish(loads[1:])
    late = [(states.at[layers], slab_end)]
    late += [(states.at[n], state_outs[n]) for n in range(layers)]
    late += [(acts.at[n], act_outs[n]) for n in range(layers)]

    def both_sweeps(index, carry):
        now, later = first_columns, second_columns
        for layer in range(layers):
            spread(paired, kernels[index, layer])

            def store(rows, first, odd, following, activation, layer=layer, target=later):
                states[layer + 1, rows, odd] = following
                acts[layer, rows, odd] = activation
                if layer < layers - 1:
                    put_columns(target, first, odd, following)
                else:
                    put_columns(target, first, odd, scaled_rows(tops[rows, odd], activation))

            forward_layer(states.at[layer], now, tools, decays[index, layer : layer + 1], store)
            now, later = later, now

        @pl.when(index == 1)
        def _():
            load(late, sems, base)

        for layer in reversed(range(layers)):
            spread(paired, turned_kernels[index, layer])

            def store_back(rows, first, odd, following, layer=layer, target=later):
                adjoint[rows, odd] = following
                if layer > 0:
                    put_columns(target, first, odd, scaled_rows(following, acts[layer - 1, rows, odd]))

            source = tops if layer == layers - 1 else adjoint
            backward_layer(source, now, tools, decays[index, layer : layer + 1], store_back)
            now, later = later, now

        @pl.when(index == 0)
        def _():
            out_coarse.wait()

            def again(first, count):
                rows = pl.ds(first, count)
                tops[rows] = jnp.where(last_slab, cotangent[rows], adjoint[rows])
                for odd in range(2):
                    begin = begins[rows, odd]
                    states[0, rows, odd] = begin
                    put_columns(first_columns, first, odd, begin)

            per_block(pairs, again)

        return carry

    lax.fori_loop(0, 2, both_sweeps, 0)

    outs = subtract_and_send(place[BACKWARD], group, chunks, adjoint, tops, turned, back_pieces, sems, 0)
    outs += load([(adjoint, back_offset)], sems, count_pieces)
    finish(outs)
    for number, (source, target) in enumerate(late):
        pltpu.make_async_copy(source, target, sems.at[base + number]).wait()


def middle(place, pieces, offset, cotangent, own, following, own_decay, next_decay, matrix, turned, group, chunks):
    layers = own[0].shape[0]
    field = offset.shape
    count = len(pieces)
    fields = [jax.ShapeDtypeStruct(field, F32)] * (3 + 2 * layers)
    results = pl.pallas_call(
        functools.partial(middle_kernel, layers, group, chunks),
        out_shape=fields + piece_shapes(field, group, chunks),
        in_specs=[SMEM] + [ANY] * (count + 6) + [VMEM] * 4,
        out_specs=[ANY] * (3 + 2 * layers + count),
        scratch_shapes=[pltpu.VMEM(field, F32)]
        + [pltpu.VMEM((layers + 1,) + field, F32), pltpu.VMEM((layers,) + field, F32)]
        + [pltpu.VMEM(field, F32)] * 4
        + scratch_of(field, 2)
        + [pltpu.VMEM((2,) + own[0].shape, BF16)] * 2
        + [pltpu.VMEM((2, layers, field[3]), F32), pltpu.SemaphoreType.DMA((count + 9 + 2 * layers,))],
        compiler_params=params(52),
        cost_estimate=cost(4.0 * layers, field),
    )(place, *pieces, offset, cotangent, *following, *own, own_decay, next_decay, matrix, turned)
    return results[:3], results[3 : 3 + layers], results[3 + layers : 3 + 2 * layers], results[3 + 2 * layers :]


def turn(whole, turned):
    taps, channels = whole.shape[0] // whole.shape[1], whole.shape[1]
    for tap in range(taps):
        block = whole[tap * channels : (tap + 1) * channels]
        other = taps - 1 - tap
        turned[other * channels : (other + 1) * channels] = block.T.astype(BF16)


def own_kernel(kernels, turned, whole):
    for layer in range(kernels.shape[0]):
        whole[...] = kernels[layer].astype(F32)
        turn(whole, turned.at[layer])


def turn_own(kernels):
    return pl.pallas_call(
        own_kernel,
        out_shape=jax.ShapeDtypeStruct(kernels.shape, BF16),
        in_specs=[VMEM],
        out_specs=VMEM,
        scratch_shapes=[pltpu.VMEM(kernels.shape[1:], F32)],
        compiler_params=params(),
    )(kernels)


def next_kernel(place, *refs):
    quarters, (kernels, turned, decay, whole) = refs[:4], refs[4:]
    layers = kernels.shape[0]
    rows = whole.shape[0] // 4
    chunk = (place[CHUNK] & 3)
    at = [chunk, chunk ^ 2, chunk ^ 1, chunk ^ 3]
    for layer in range(layers):
        for number in range(4):
            whole[pl.ds(at[number] * rows, rows)] = quarters[number][layer, 0:rows]
        kernels[layer] = whole[...].astype(BF16)
        turn(whole, turned.at[layer])
        decay[layer : layer + 1] = quarters[0][layer, rows : rows + 1]


def join_next(place, quarters):
    layers, rows, channels = quarters[0].shape
    shape = (layers, 4 * (rows - 8), channels)
    results = pl.pallas_call(
        next_kernel,
        out_shape=[jax.ShapeDtypeStruct(shape, BF16)] * 2 + [jax.ShapeDtypeStruct((layers, channels), F32)],
        in_specs=[SMEM] + [VMEM] * 4,
        out_specs=[VMEM] * 3,
        scratch_shapes=[pltpu.VMEM(shape[1:], F32)],
        compiler_params=params(),
    )(place, *quarters)
    return results[:2], results[2]


def turned_columns_kernel(state, turned, columns):
    pairs, _, side, _ = state.shape
    wide, depth = columns.shape[2:]
    clear_borders(columns)

    def fill(first, count):
        for odd in range(2):
            put_columns(columns, first, odd, state[pl.ds(first, count), odd])

    per_block(pairs, fill)
    for pair in range(pairs + 1):
        block = columns[pair].reshape(2 * wide, depth).astype(F32)
        turned[:, pair * 2 * wide : (pair + 1) * 2 * wide] = block.T.astype(BF16)


def turned_columns(state):
    shape = columns_shape(state.shape)
    return pl.pallas_call(
        turned_columns_kernel,
        out_shape=jax.ShapeDtypeStruct((shape[3], shape[0] * 2 * shape[2]), BF16),
        in_specs=[VMEM],
        out_specs=VMEM,
        scratch_shapes=[pltpu.VMEM(shape, BF16)],
        compiler_params=params(),
        cost_estimate=cost(0.4, state.shape),
    )(state)


def gradient_body(adjoint, activation, turned, ready, scaled, gradient, side):
    pairs = adjoint.shape[0]
    wide, channels = scaled.shape[2:]
    edge = jnp.zeros((2, wide, channels), BF16)
    scaled[0] = edge
    scaled[pairs + 1] = edge

    def fill(first, count):
        rows = pl.ds(first, count)
        for odd in range(2):
            own = scaled_rows(adjoint[rows, odd], activation[rows, odd])
            padded = jnp.concatenate([own, jnp.zeros((count, wide - side, channels), F32)], axis=1)
            scaled[pl.ds(first + 1, count), odd] = padded.astype(BF16)

    per_block(pairs, fill)
    ready()
    flat = scaled[...].reshape((2 * pairs + 4) * wide, channels)
    rows = (2 * pairs + 2) * wide
    shifted = [flat[(2 - tap) * wide : (2 - tap) * wide + rows] for tap in range(3)]
    products = jnp.dot(turned[...], jnp.concatenate(shifted, axis=1), preferred_element_type=F32)
    for row in range(3):
        for column in range(3):
            tap = 3 * row + column
            gradient[tap * channels : (tap + 1) * channels] = products[
                column * channels : (column + 1) * channels, row * channels : (row + 1) * channels
            ]


def scaled_shape(field):
    pairs, _, side, channels = field
    return (pairs + 2, 2, wide_of(side), channels)


def halve(place, gradient, keep, send):
    half = (place[CHUNK] & 1)
    rows = keep.shape[0]
    keep[...] = gradient[pl.ds(half * rows, rows)]
    send[...] = gradient[pl.ds((1 - half) * rows, rows)]


def top_kernel(group, chunks, place, *refs):
    count_pieces = group * len(chunks)
    pieces, refs = refs[:count_pieces], refs[count_pieces:]
    activation_hbm, turned_hbm, adjoint_out, keep, send = refs[:5]
    adjoint, activation, turned, shifted, gradient, sems = refs[5:]
    brought = bring_in(place[BACKWARD], group, chunks, pieces, adjoint, sems, 0)
    loads = load([(activation_hbm, activation), (turned_hbm, turned)], sems, count_pieces)
    finish(brought)
    out = load([(adjoint, adjoint_out)], sems, 0)
    loads[0].wait()
    gradient_body(adjoint, activation, turned, loads[1].wait, shifted, gradient, adjoint.shape[2])
    halve(place, gradient, keep, send)
    finish(out)


def top_gradient(place, pieces, activation, turned, group, chunks):
    field = activation.shape
    shape = columns_shape(field)
    taps = 9 * field[3]
    half = jax.ShapeDtypeStruct((taps // 2, field[3]), F32)
    return pl.pallas_call(
        functools.partial(top_kernel, group, chunks),
        out_shape=[jax.ShapeDtypeStruct(field, F32), half, half],
        in_specs=[SMEM] + [ANY] * (len(pieces) + 2),
        out_specs=[ANY, VMEM, VMEM],
        scratch_shapes=[
            pltpu.VMEM(field, F32),
            pltpu.VMEM(field, F32),
            pltpu.VMEM(turned.shape, BF16),
            pltpu.VMEM(scaled_shape(field), BF16),
            pltpu.VMEM((taps, field[3]), F32),
            pltpu.SemaphoreType.DMA((len(pieces) + 2,)),
        ],
        compiler_params=params(60),
        cost_estimate=cost(1.5, field),
    )(place, *pieces, activation, turned)


def retreat_body(adjoint, activation, columns, tools, rate, store):
    clear_borders(columns)
    fill_backward(adjoint, activation, columns)
    backward_layer(adjoint, columns, tools, rate, store)


def lower_kernel(layer, place, adjoint, above, kernel, decay, below_hbm, turned_hbm, *refs):
    result_out, keep, send = refs[:3]
    result, below, turned, columns, paired, even, uneven, shifted, gradient, sems = refs[3:]
    loads = load([(below_hbm, below), (turned_hbm, turned)], sems, 0)
    spread(paired, kernel[layer])

    def store(rows, first, odd, fresh):
        result[rows, odd] = fresh

    retreat_body(adjoint, above, columns, (paired, even, uneven), decay[layer : layer + 1], store)
    out = load([(result, result_out)], sems, 2)
    loads[0].wait()
    gradient_body(result, below, turned, loads[1].wait, shifted, gradient, result.shape[2])
    halve(place, gradient, keep, send)
    finish(out)


def lower_gradient(place, layer, adjoint, above, kernels, decay, below, turned):
    field = adjoint.shape
    shape = columns_shape(field)
    taps = 9 * field[3]
    half = jax.ShapeDtypeStruct((taps // 2, field[3]), F32)
    return pl.pallas_call(
        functools.partial(lower_kernel, layer),
        out_shape=[jax.ShapeDtypeStruct(field, F32), half, half],
        in_specs=[SMEM] + [VMEM] * 4 + [ANY] * 2,
        out_specs=[ANY, VMEM, VMEM],
        scratch_shapes=[pltpu.VMEM(field, F32), pltpu.VMEM(field, F32), pltpu.VMEM(turned.shape, BF16)]
        + scratch_of(field, 1)
        + [pltpu.VMEM(scaled_shape(field), BF16), pltpu.VMEM((taps, field[3]), F32), pltpu.SemaphoreType.DMA((3,))],
        compiler_params=params(),
        cost_estimate=cost(2.0, field),
    )(place, adjoint, above, kernels, decay, below, turned)


def last_kernel(adjoint, activation, kernel, decay, tops, back_offset, turned, result, adjoint_end, columns, *tools):
    spread(tools[0], kernel[0])

    def store(rows, first, odd, fresh):
        result[rows, odd] = fresh

    retreat_body(adjoint, activation, columns, tools, decay[0:1], store)

    def coarse_rows(first, count):
        rows = pl.ds(first, count)
        for odd in range(2):
            adjoint_end[rows, odd] = transform_rows(tops[rows, odd], turned[...]) + back_offset[rows, odd]

    per_block(adjoint.shape[0], coarse_rows, whole=True)


def last_retreat(adjoint, activation, kernels, decay, tops, back_offset, turned):
    field = adjoint.shape
    return pl.pallas_call(
        last_kernel,
        out_shape=[jax.ShapeDtypeStruct(field, F32)] * 2,
        in_specs=[VMEM] * 7,
        out_specs=[VMEM] * 2,
        scratch_shapes=scratch_of(field, 1),
        compiler_params=params(),
        cost_estimate=cost(1.6, field),
    )(adjoint, activation, kernels, decay, tops, back_offset, turned)


def collect_kernel(layers, place, *refs):
    sources, out, held, sems = refs[:-3], refs[-3], refs[-2], refs[-1]
    half = (place[CHUNK] & 1)
    rows = out.shape[1] // 2
    if layers > 0:
        number = 0
        copies = []
        for layer in range(layers):
            for part in [half, 1 - half][: 1 if layer == 0 else 2]:
                copies.append((sources[number], out.at[layer, pl.ds(part * rows, rows)]))
                number += 1
        finish(load(copies, sems, 0))
    else:
        finish(load([(sources[0], out.at[0, pl.ds((1 - half) * rows, rows)])], sems, 0))


def collect(place, halves):
    layers = len(halves)
    rows, channels = halves[0][0].shape
    shape = jax.ShapeDtypeStruct((layers, 2 * rows, channels), F32)
    most = [half for both in halves for half in both]
    last = most.pop(1)
    scratch = [pltpu.VMEM((8, channels), F32), pltpu.SemaphoreType.DMA((2 * layers,))]
    out = pl.pallas_call(
        functools.partial(collect_kernel, layers),
        out_shape=shape,
        in_specs=[SMEM] + [VMEM] * len(most),
        out_specs=ANY,
        scratch_shapes=scratch,
        compiler_params=params(16),
        cost_estimate=cost(0.4, (rows, 2 * layers, channels)),
    )(place, *most)
    return pl.pallas_call(
        functools.partial(collect_kernel, 0),
        out_shape=shape,
        in_specs=[SMEM, VMEM, ANY],
        out_specs=ANY,
        scratch_shapes=scratch,
        input_output_aliases={2: 0},
        compiler_params=params(16),
    )(place, last, out)


def from_behind(shard, axis, by):
    devices = lax.axis_size(axis)
    pairs = [(i, i + by) for i in range(devices) if 0 <= i + by < devices]
    return lax.ppermute(shard, axis, pairs)


def swap(shard, bit):
    return lax.ppermute(shard, "dp", [(i, i ^ bit) for i in range(lax.axis_size("dp"))])


def order_of(index, size, backward):
    return size - 1 - index if backward else index


def group_of(size):
    for group in (GROUP, 2, 1):
        if size % group == 0:
            return group


def exchange(pieces, group, backward):
    size = lax.axis_size("layer")
    received = [pieces[0]]
    for shift in range(1, group):
        pairs = []
        for order in range(size):
            base = order - order % group
            target = base + (order + shift) % group
            pairs.append((order_of(order, size, backward), order_of(target, size, backward)))
        received.append(lax.ppermute(pieces[shift], "layer", pairs))
    return received


def coarse_chain(place, seed, pieces, matrices, group, chunks, backward, beside=()):
    size = lax.axis_size("layer")
    pairs = [(order_of(i, size, backward), order_of(i + group, size, backward)) for i in range(size - group)]
    received = []
    for chunk in range(len(chunks)):
        sent = pieces[chunk * group : (chunk + 1) * group]
        if chunk > 0:
            received[-1][1], *sent = lax.optimization_barrier((received[-1][1], *sent))
        received.append(exchange(sent, group, backward))
    carries = [jnp.zeros(pieces[chunk * group].shape, F32) for chunk in range(len(chunks))]
    partials = [None] * len(chunks)

    def partial_of(chunk):
        return partial_chain(place, seed, matrices, received[chunk], group, chunks, chunk, backward)

    for chunk in range(len(chunks)):
        if size > group:
            out = group_carry(place, seed, matrices, received[chunk], group, chunks, chunk, backward)
            carry = lax.ppermute(out, "layer", pairs)
            for _ in range(size // group - 2):
                carry = lax.ppermute(hop(carry, matrices[int(backward), whole_at(group)], out), "layer", pairs)
            carries[chunk] = carry
        if backward:
            partials[chunk] = partial_of(chunk)
    if backward:
        partials[-1], beside = lax.optimization_barrier((partials[-1], beside))
    else:
        if size > group:
            received, out = lax.optimization_barrier((received, out))
        partials = lax.optimization_barrier([partial_of(chunk) for chunk in range(len(chunks))])
    begins = [(carry, products, begun) for carry, (begun, products) in zip(carries, partials)]
    result = []
    for carry, products, begun in begins:
        result += exchange(complete_chain(carry, products, begun, group), group, backward)
    return result, beside


def sum_across(total):
    bit = 2
    while bit < lax.axis_size("dp"):
        total = total + swap(total, bit)
        bit *= 2
    return total


def per_device(images, kernels, damping, cotangent):
    layers, taps, channels = kernels.shape
    _, height, side, _ = images.shape
    size = lax.axis_size("layer")
    position = lax.axis_index("layer")
    dp_at = lax.axis_index("dp")
    field = (height // 2, 2, side, channels)
    images = images.reshape(field)
    cotangent = cotangent.reshape(field)
    group = group_of(size)
    quarter = field[0] // group
    chunks = chunks_of(quarter)
    back_order = size - 1 - position
    place = jnp.stack(
        [
            position,
            lax.rem(position, group),
            lax.rem(back_order, group),
            dp_at,
            (position < group).astype(jnp.int32),
            (back_order < group).astype(jnp.int32),
            jnp.int32(size),
            jnp.int32(0),
        ]
    ).astype(jnp.int32)

    parts, quarter_part, copies, matrix, turned_matrix = prelude(place, kernels, damping, group)

    lows = [from_behind(part, "layer", 1) for part in parts]
    highs = [swap(low, 1) for low in lows[:-1]]

    groups = [list(range(at, at + group)) for at in range(0, size, group)]
    steps = lax.all_to_all(copies, "layer", 0, 0, axis_index_groups=groups, tiled=True)
    own = (kernels, turn_own(kernels))

    state, steps = lax.optimization_barrier((images, steps))
    for layer in range(layers - 1):
        state = fetched_layer(place, state, lows[layer], highs[layer])
    lows[-1], state = lax.optimization_barrier((lows[-1], state))
    highs.append(swap(lows[-1], 1))

    quarter_part, state = lax.optimization_barrier((quarter_part, state))
    first = from_behind(quarter_part, "layer", -1)

    offset, pieces = slab_offset(
        place, images, state, lows[-1], highs[-1], kernels, damping, matrix, group, chunks
    )
    first, pieces = lax.optimization_barrier((first, pieces))
    second = swap(first, 2)
    following, next_decay = join_next(place, [first, second, swap(first, 1), swap(second, 1)])
    matrices = group_matrices(steps)
    pieces, _ = coarse_chain(place, images, pieces, matrices, group, chunks, False)
    (slab_end, coarse_end, back_offset), states, acts, pieces = middle(
        place, pieces, offset, cotangent, own, following, damping, next_decay, matrix, turned_matrix, group, chunks
    )
    turned = [turned_columns(state) for state in states]
    pieces, turned = coarse_chain(place, cotangent, pieces, matrices, group, chunks, True, turned)
    tops, keep, send = top_gradient(place, pieces, acts[-1], turned[-1], group, chunks)
    adjoint = tops
    paired = [None] * layers
    halves = [None] * layers
    for layer in reversed(range(1, layers)):
        paired[layer] = (keep, send)
        adjoint, keep, send = lower_gradient(
            place, layer, adjoint, acts[layer], own[1], damping, acts[layer - 1], turned[layer - 1]
        )
        total = paired[layer][0] + swap(paired[layer][1], 1)
        adjoint, total = lax.optimization_barrier((adjoint, total))
        if layer < layers - 1:
            adjoint, summed = lax.optimization_barrier((adjoint, paired[layer + 1]))
            paired[layer + 1] = summed
        paired[layer] = sum_across(total)
    total = keep + swap(send, 1)
    adjoint, adjoint_end = last_retreat(adjoint, acts[0], own[1], damping, tops, back_offset, turned_matrix)
    adjoint, total = lax.optimization_barrier((adjoint, total))
    paired[0] = sum_across(total)
    halves = [(half, swap(half, 1)) for half in paired]
    full = (1, 1, height, side, channels)
    return (
        slab_end.reshape(full),
        coarse_end.reshape(full),
        adjoint.reshape(full),
        adjoint_end.reshape(full),
        collect(place, halves),
    )


def solution(mesh):
    in_specs = (
        P("dp", None, None, None),
        P("layer", None, None),
        P("layer", None),
        P("dp", None, None, None),
    )
    out_specs = (
        P("layer", "dp", None, None, None),
        P("layer", "dp", None, None, None),
        P("layer", "dp", None, None, None),
        P("layer", "dp", None, None, None),
        P("layer", None, None),
    )
    return jax.shard_map(
        per_device, mesh=mesh, in_specs=in_specs, out_specs=out_specs, check_vma=False
    )
```

```python
import functools
import math

import jax
import jax.numpy as jnp
from jax import lax
from jax.experimental import pallas as pl
from jax.experimental.pallas import tpu as pltpu
from jax.sharding import PartitionSpec as P

STEP = 0.125
F32 = jnp.float32
BF16 = jnp.bfloat16
BLOCK_PAIRS = 7
PRODUCT_PAIRS = 14
GROUP = 4


def wide_of(side):
    return -(-(side + 1) // 16) * 16


def columns_shape(field):
    pairs, _, side, channels = field
    return (pairs + 1, 2, wide_of(side), 3 * channels)


def block_of(pairs):
    return BLOCK_PAIRS if pairs % BLOCK_PAIRS == 0 else 1


def product_block(pairs):
    return PRODUCT_PAIRS if pairs % PRODUCT_PAIRS == 0 else block_of(pairs)


def per_block(pairs, body, whole=False):
    block = block_of(pairs)

    def step(number, carry):
        if whole:
            body(number * block, block)
        else:
            for pair in range(block):
                body(number * block + pair, 1)
        return carry

    lax.fori_loop(0, pairs // block, step, 0)


def clear_borders(columns):
    edge = jnp.zeros(columns.shape[2:], BF16)
    columns[0, 0] = edge
    columns[columns.shape[0] - 1, 1] = edge


def put_columns(columns, first, odd, rows):
    count, side, channels = rows.shape
    wide = columns.shape[2]
    here = jnp.concatenate([rows, jnp.zeros((count, wide - side, channels), F32)], axis=1)
    left = pltpu.roll(here, 1, 1)
    right = pltpu.roll(here, wide - 1, 1)
    columns[pl.ds(first + odd, count), 1 - odd] = jnp.concatenate([left, here, right], axis=2).astype(BF16)


def spread(paired, kernel):
    taps, channels = kernel.shape
    third = taps // 3
    blank = jnp.zeros((third, channels), BF16)
    paired[0:taps, 0:channels] = kernel
    paired[taps : taps + third, 0:channels] = blank
    paired[0:third, channels : 2 * channels] = blank
    paired[third : taps + third, channels : 2 * channels] = kernel


def convolve(columns, paired, results, emit, side):
    _, _, wide, depth = columns.shape
    channels = depth // 3
    pairs = columns.shape[0] - 1
    block = product_block(pairs)

    def product(number):
        first = number * block
        pieces = [
            columns[first : first + block, 0],
            columns[first : first + block, 1],
            columns[first + 1 : first + 1 + block, 0],
            columns[first + 1 : first + 1 + block, 1],
        ]
        left = jnp.concatenate([piece.reshape(block * wide, depth) for piece in pieces], axis=1)
        results[number % 2][...] = jnp.dot(left, paired[...], preferred_element_type=F32)

    product(0)
    for number in range(pairs // block):
        if number + 1 < pairs // block:
            product(number + 1)
        result = results[number % 2]
        for pair in range(block):
            for odd in range(2):
                preact = result[pair * wide : (pair + 1) * wide, odd * channels : (odd + 1) * channels]
                emit(number * block + pair, odd, preact.reshape(1, wide, channels)[:, :side])


def split_dot(left, matrix):
    high = left.astype(BF16)
    low = (left - high.astype(F32)).astype(BF16)
    m_high = matrix.astype(BF16)
    m_low = (matrix - m_high.astype(F32)).astype(BF16)
    return jnp.dot(
        jnp.concatenate([high, low, high], axis=1),
        jnp.concatenate([m_high, m_high, m_low], axis=0),
        preferred_element_type=F32,
    )


def transform_rows(rows, matrix):
    count, side, channels = rows.shape
    return split_dot(rows.reshape(count * side, channels), matrix).reshape(rows.shape)


def fill_forward(state, columns):
    def fill(first, count):
        for odd in range(2):
            put_columns(columns, first, odd, state[pl.ds(first, count), odd])

    per_block(state.shape[0], fill)


def forward_layer(current, columns, tools, rate, store):
    decay = rate.reshape(1, 1, -1)

    def emit(first, odd, preact):
        rows = pl.ds(first, 1)
        activation = jnp.tanh(preact)
        here = current[rows, odd]
        store(rows, first, odd, here + STEP * (activation - decay * here), activation)

    convolve(columns, tools[0], tools[1:], emit, current.shape[2])


def scaled_rows(adjoint, activation):
    return STEP * (1.0 - activation * activation) * adjoint


def fill_backward(state, activation, columns):
    def fill(first, count):
        rows = pl.ds(first, count)
        for odd in range(2):
            put_columns(columns, first, odd, scaled_rows(state[rows, odd], activation[rows, odd]))

    per_block(state.shape[0], fill)


def backward_layer(current, columns, tools, rate, store):
    decay = rate.reshape(1, 1, -1)

    def emit(first, odd, back_term):
        rows = pl.ds(first, 1)
        here = current[rows, odd]
        store(rows, first, odd, here - STEP * decay * here + back_term)

    convolve(columns, tools[0], tools[1:], emit, current.shape[2])


def params(mebibytes=40):
    return pltpu.CompilerParams(vmem_limit_bytes=mebibytes * 1024 * 1024)


def cost(share, shape, free=False):
    share = 0.0 if free else share
    flops = 8 * share * math.prod(shape) * shape[-1] * 9
    return pl.CostEstimate(flops=int(flops), bytes_accessed=int(8 * share * math.prod(shape)), transcendentals=0)


ANY = pl.BlockSpec(memory_space=pl.ANY)
VMEM = pl.BlockSpec(memory_space=pltpu.VMEM)
SMEM = pl.BlockSpec(memory_space=pltpu.SMEM)

def chunks_of(quarter):
    return (quarter - quarter // 2, quarter // 2) if quarter > 1 else (quarter,)


POSITION, FORWARD, BACKWARD, CHUNK, FORWARD_HEAD, BACKWARD_HEAD, SIZE = range(7)


def load(pairs_of_refs, sems, base):
    copies = []
    for number, (source, target) in enumerate(pairs_of_refs):
        copies.append(pltpu.make_async_copy(source, target, sems.at[base + number]))
        copies[-1].start()
    return copies


def finish(copies):
    for copy in copies:
        copy.wait()


def scratch_of(field, buffers):
    shape = columns_shape(field)
    products = pltpu.VMEM((product_block(field[0]) * shape[2], 2 * field[3]), F32)
    return [pltpu.VMEM(shape, BF16)] * buffers + [pltpu.VMEM((4 * shape[3], 2 * field[3]), BF16), products, products]


def join_halves(whole, low, high, half):
    rows = whole.shape[0] // 2
    whole[pl.ds(half * rows, rows)] = low[0:rows].astype(BF16)
    whole[pl.ds((1 - half) * rows, rows)] = high[0:rows].astype(BF16)


def layer_kernel(place, field, low, high, result, columns, paired, even, uneven, whole):
    half = (place[CHUNK] & 1)
    join_halves(whole, low, high, half)
    spread(paired, whole[...])
    rows = whole.shape[0] // 2
    clear_borders(columns)
    fill_forward(field, columns)

    def store(where, first, odd, following, activation):
        result[where, odd] = following

    forward_layer(field, columns, (paired, even, uneven), low[rows : rows + 1], store)


def fetched_layer(place, field, low, high):
    rows, channels = low.shape[0] - 8, low.shape[1]
    return pl.pallas_call(
        layer_kernel,
        out_shape=jax.ShapeDtypeStruct(field.shape, F32),
        in_specs=[SMEM] + [VMEM] * 3,
        out_specs=VMEM,
        scratch_shapes=scratch_of(field.shape, 1) + [pltpu.VMEM((2 * rows, channels), BF16)],
        compiler_params=params(),
        cost_estimate=cost(1.0, field.shape),
    )(place, field, low, high)


def wrapped(index, group):
    return index & (group - 1)


def piece_refs(member, group, chunks, field, shift, chunk, forward_shift):
    quarter = field.shape[0] // group
    offset = sum(chunks[:chunk])
    turn = member + shift if forward_shift else member - shift + group
    return field.at[pl.ds(wrapped(turn, group) * quarter + offset, chunks[chunk])]


def subtract_and_send(member, group, chunks, field, tops, matrix, outs, sems, base):
    quarter = field.shape[0] // group
    copies = []
    for shift in [*range(1, group), 0]:
        rows = pl.ds(wrapped(member + shift, group) * quarter, quarter)
        for odd in range(2):
            field[rows, odd] = field[rows, odd] - transform_rows(tops[rows, odd], matrix[...])
        for chunk in range(len(chunks)):
            number = chunk * group + shift
            source = piece_refs(member, group, chunks, field, shift, chunk, True)
            copies.append(pltpu.make_async_copy(source, outs[number], sems.at[base + number]))
            copies[-1].start()
    return copies


def bring_in(member, group, chunks, pieces, field, sems, base):
    copies = []
    for chunk in range(len(chunks)):
        for shift in range(group):
            number = chunk * group + shift
            target = piece_refs(member, group, chunks, field, shift, chunk, False)
            copies.append(pltpu.make_async_copy(pieces[number], target, sems.at[base + number]))
            copies[-1].start()
    return copies


def piece_shapes(field, group, chunks):
    return [jax.ShapeDtypeStruct((count,) + field[1:], F32) for count in chunks for _ in range(group)]


def offset_kernel(layers, group, chunks, place, images_hbm, field, low, high, kernels_hbm, decay, matrix, *refs):
    count_pieces = group * len(chunks)
    out, pieces = refs[0], refs[1 : 1 + count_pieces]
    images, kernels, starts, offset, now, later, paired, even, uneven, whole, sems = refs[1 + count_pieces :]
    tools = (paired, even, uneven)
    pairs = offset.shape[0]
    loads = load([(images_hbm, images), (kernels_hbm, kernels)], sems, 0)
    half = (place[CHUNK] & 1)
    first_slab = place[POSITION] == 0
    join_halves(whole, low, high, half)
    spread(paired, whole[...])
    rows = whole.shape[0] // 2
    clear_borders(now)
    clear_borders(later)
    fill_forward(field, now)
    loads[0].wait()

    def store_start(where, first, odd, following, activation):
        begin = jnp.where(first_slab, images[where, odd], following)
        starts[where, odd] = begin
        put_columns(later, first, odd, begin)

    forward_layer(field, now, tools, low[rows : rows + 1], store_start)
    loads[1].wait()
    for layer in range(layers):
        now, later = later, now
        spread(paired, kernels[layer])

        def store(where, first, odd, following, activation, last=layer == layers - 1, target=later):
            if not last:
                put_columns(target, first, odd, following)
            offset[where, odd] = following

        source = starts if layer == 0 else offset
        forward_layer(source, now, tools, decay[layer : layer + 1], store)

    copies = subtract_and_send(place[FORWARD], group, chunks, offset, starts, matrix, pieces, sems, 3)
    copies += load([(offset, out)], sems, 2)
    finish(copies)


def slab_offset(place, images, field, low, high, kernels, decay, matrix, group, chunks):
    layers, taps, channels = kernels.shape
    shape = images.shape
    count = group * len(chunks)
    results = pl.pallas_call(
        functools.partial(offset_kernel, layers, group, chunks),
        out_shape=[jax.ShapeDtypeStruct(shape, F32)] + piece_shapes(shape, group, chunks),
        in_specs=[SMEM, ANY, VMEM, VMEM, VMEM, ANY, VMEM, VMEM],
        out_specs=[ANY] * (1 + count),
        scratch_shapes=[pltpu.VMEM(shape, F32), pltpu.VMEM(kernels.shape, BF16)]
        + [pltpu.VMEM(shape, F32)] * 2
        + scratch_of(shape, 2)
        + [pltpu.VMEM((taps, channels), BF16), pltpu.SemaphoreType.DMA((3 + count,))],
        compiler_params=params(60),
        cost_estimate=cost(layers + 1.0, shape),
    )(place, images, field, low, high, kernels, decay, matrix)
    return results[0], results[1:]


def split_matrix(matrix):
    high = matrix.astype(BF16)
    low = (matrix - high.astype(F32)).astype(BF16)
    return jnp.concatenate([high, high, low], axis=0)


def split_rows(rows):
    high = rows.astype(BF16)
    low = (rows - high.astype(F32)).astype(BF16)
    return jnp.concatenate([high, low, high], axis=1)


def identity(channels):
    rows = lax.broadcasted_iota(jnp.int32, (channels, channels), 0)
    columns = lax.broadcasted_iota(jnp.int32, (channels, channels), 1)
    return (rows == columns).astype(F32)


def prelude_kernel(place, kernels, damping, *outs):
    layers, taps, channels = kernels.shape
    parts, (quarter, copies, matrix, turned) = outs[:layers], outs[layers:]
    half_rows, quarter_rows = taps // 2, taps // 4
    half, chunk = (place[CHUNK] & 1), (place[CHUNK] & 3)
    for layer in range(layers):
        rate = jnp.broadcast_to(damping[layer : layer + 1], (8, channels))
        parts[layer][0:half_rows] = kernels[layer, pl.ds(half * half_rows, half_rows)].astype(F32)
        parts[layer][half_rows : half_rows + 8] = rate
        quarter[layer, 0:quarter_rows] = kernels[layer, pl.ds(chunk * quarter_rows, quarter_rows)].astype(F32)
        quarter[layer, quarter_rows : quarter_rows + 8] = rate
    total = kernels[0, 0:channels].astype(F32)
    for tap in range(1, taps // channels):
        total += kernels[0, tap * channels : (tap + 1) * channels].astype(F32)
    diagonal = identity(channels) * (1.0 - layers * STEP * damping[0:1])
    coarse = diagonal + layers * STEP * total
    for member in range(copies.shape[0]):
        copies[member] = coarse
    matrix[...] = coarse
    turned[...] = coarse.T


def prelude(place, kernels, damping, group):
    layers, taps, channels = kernels.shape
    part = jax.ShapeDtypeStruct((taps // 2 + 8, channels), F32)
    quarter = jax.ShapeDtypeStruct((layers, taps // 4 + 8, channels), F32)
    square = jax.ShapeDtypeStruct((channels, channels), F32)
    results = pl.pallas_call(
        prelude_kernel,
        out_shape=[part] * layers + [quarter, jax.ShapeDtypeStruct((group, channels, channels), F32), square, square],
        in_specs=[SMEM] + [VMEM] * 2,
        out_specs=[VMEM] * (layers + 4),
        compiler_params=params(60),
    )(place, kernels, damping)
    return results[:layers], *results[layers:]


def step_at(group, index):
    return index


def before_at(group, index):
    return group + index


def after_at(group, index):
    return 2 * group + index


def whole_at(group):
    return 3 * group


def matrices_kernel(group, held, out):
    channels = held.shape[1]
    for backward in range(2):
        ordered = [held[group - 1 - step].T if backward else held[step] for step in range(group)]
        product = identity(channels)
        for step in range(group):
            split = split_matrix(ordered[step])
            out[backward, step_at(group, step)] = split
            out[backward, before_at(group, step)] = split_matrix(product)
            product = ordered[0] if step == 0 else jnp.dot(split_rows(product), split, preferred_element_type=F32)
        out[backward, whole_at(group)] = split_matrix(product)
        product = identity(channels)
        for step in reversed(range(group)):
            out[backward, after_at(group, step)] = split_matrix(product)
            if step == group - 1:
                product = ordered[step]
            else:
                product = jnp.dot(split_rows(ordered[step]), split_matrix(product), preferred_element_type=F32)


def group_matrices(steps):
    group, channels, _ = steps.shape
    return pl.pallas_call(
        functools.partial(matrices_kernel, group),
        out_shape=jax.ShapeDtypeStruct((2, 3 * group + 1, 3 * channels, channels), BF16),
        in_specs=[VMEM],
        out_specs=VMEM,
        compiler_params=params(16),
    )(steps)


def flat_of(shape):
    return (shape[0] * shape[1] * shape[2], shape[3])


def carry_kernel(group, chunks, chunk, backward, place, seed, matrices, *refs):
    pieces, (carry, start, right, sems) = refs[:group], refs[group:]
    member = place[BACKWARD if backward else FORWARD]
    leads = place[BACKWARD_HEAD if backward else FORWARD_HEAD] == 1
    depth = right.shape[0] // (group + 1)
    source = piece_refs(member, group, chunks, seed, 0, chunk, True)
    loads = [(source, start), (matrices.at[backward, whole_at(group)], right.at[pl.ds(group * depth, depth)])]
    for shift in range(group):
        slab = wrapped(member - shift + group, group)
        loads.append((matrices.at[backward, after_at(group, slab)], right.at[pl.ds(shift * depth, depth)]))
    loads = load(loads, sems, 0)
    flat = flat_of(start.shape)
    left = [split_rows(pieces[shift][...].reshape(flat)) for shift in range(group)]
    finish(loads)
    left.append(split_rows(jnp.where(leads, start[...], 0.0).reshape(flat)))
    total = jnp.dot(jnp.concatenate(left, axis=1), right[...], preferred_element_type=F32)
    carry[...] = total.reshape(start.shape)


def group_carry(place, seed, matrices, pieces, group, chunks, chunk, backward):
    shape = pieces[0].shape
    depth, channels = matrices.shape[2:]
    return pl.pallas_call(
        functools.partial(carry_kernel, group, chunks, chunk, int(backward)),
        out_shape=jax.ShapeDtypeStruct(shape, F32),
        in_specs=[SMEM, ANY, ANY] + [VMEM] * group,
        out_specs=VMEM,
        scratch_shapes=[
            pltpu.VMEM(shape, F32),
            pltpu.VMEM(((group + 1) * depth, channels), BF16),
            pltpu.SemaphoreType.DMA((group + 2,)),
        ],
        compiler_params=params(24),
        cost_estimate=cost(1.0 * group, shape),
    )(place, seed, matrices, *pieces)


def partial_kernel(group, chunks, chunk, backward, place, seed, matrices, *refs):
    pieces, (begun, products, full, held, start, sets, sems) = refs[:group], refs[group:]
    member = place[BACKWARD if backward else FORWARD]
    leads = place[BACKWARD_HEAD if backward else FORWARD_HEAD] == 1
    source = piece_refs(member, group, chunks, seed, 0, chunk, True)
    loads = load([(source, start), (matrices.at[backward, pl.ds(0, 2 * group)], sets)], sems, 0)
    for shift in range(group):
        held[wrapped(member - shift + group, group)] = pieces[shift][...]
    finish(loads)
    shape = start.shape
    flat = flat_of(shape)
    state = jnp.where(leads, start[...], 0.0).reshape(flat)
    full[0] = state.reshape(shape)
    for slab in range(group - 1):
        step = sets[step_at(group, slab)]
        state = jnp.dot(split_rows(state), step, preferred_element_type=F32) + held[slab].reshape(flat)
        full[slab + 1] = state.reshape(shape)
    channels = shape[3]
    for shift in range(group):
        slab = wrapped(member + shift, group)
        begun[shift] = full[slab]
        products[:, shift * channels : (shift + 1) * channels] = sets[before_at(group, slab)]


def partial_chain(place, seed, matrices, pieces, group, chunks, chunk, backward):
    shape = pieces[0].shape
    depth, channels = matrices.shape[2:]
    stack = (group,) + shape
    return pl.pallas_call(
        functools.partial(partial_kernel, group, chunks, chunk, int(backward)),
        out_shape=[jax.ShapeDtypeStruct(stack, F32), jax.ShapeDtypeStruct((depth, group * channels), BF16)],
        in_specs=[SMEM, ANY, ANY] + [VMEM] * group,
        out_specs=[VMEM] * 2,
        scratch_shapes=[
            pltpu.VMEM(stack, F32),
            pltpu.VMEM(stack, F32),
            pltpu.VMEM(shape, F32),
            pltpu.VMEM((2 * group, depth, channels), BF16),
            pltpu.SemaphoreType.DMA((2,)),
        ],
        compiler_params=params(24),
        cost_estimate=cost(0.8 * group, shape, not backward),
    )(place, seed, matrices, *pieces)


def hop_kernel(carry, whole, own, result):
    shape = own.shape
    moved = jnp.dot(split_rows(carry[...].reshape(flat_of(shape))), whole[...], preferred_element_type=F32)
    result[...] = own[...] + moved.reshape(shape)


def hop(carry, whole, own):
    return pl.pallas_call(
        hop_kernel,
        out_shape=jax.ShapeDtypeStruct(own.shape, F32),
        in_specs=[VMEM] * 3,
        out_specs=VMEM,
        compiler_params=params(24),
        cost_estimate=cost(0.8, own.shape),
    )(carry, whole, own)


def complete_kernel(group, carry, products, begun, *outs):
    shape = carry.shape
    channels = shape[3]
    moved = jnp.dot(split_rows(carry[...].reshape(flat_of(shape))), products[...], preferred_element_type=F32)
    for shift in range(group):
        part = moved[:, shift * channels : (shift + 1) * channels]
        outs[shift][...] = begun[shift] + part.reshape(shape)


def complete_chain(carry, products, begun, group):
    shape = carry.shape
    return pl.pallas_call(
        functools.partial(complete_kernel, group),
        out_shape=[jax.ShapeDtypeStruct(shape, F32)] * group,
        in_specs=[VMEM] * 3,
        out_specs=[VMEM] * group,
        compiler_params=params(24),
        cost_estimate=cost(0.2 * group, shape),
    )(carry, products, begun)


def middle_kernel(layers, group, chunks, place, *refs):
    count_pieces = group * len(chunks)
    pieces, refs = refs[:count_pieces], refs[count_pieces:]
    (offset_hbm, cotangent_hbm, next_k_hbm, next_f_hbm, own_k_hbm, own_f_hbm, own_decay, next_decay, matrix, turned) = refs[:10]
    refs = refs[10:]
    (slab_end, coarse_end, back_offset), refs = refs[:3], refs[3:]
    state_outs, refs = refs[:layers], refs[layers:]
    act_outs, refs = refs[:layers], refs[layers:]
    back_pieces, refs = refs[:count_pieces], refs[count_pieces:]
    (begins, states, acts, offset, cotangent, tops, adjoint, first_columns, second_columns) = refs[:9]
    tools, (kernels, turned_kernels, decays, sems) = refs[9:12], refs[12:]
    paired = tools[0]
    pairs = offset.shape[0]
    last_slab = place[POSITION] == place[SIZE] - 1

    brought = bring_in(place[FORWARD], group, chunks, pieces, begins, sems, 0)
    base = count_pieces
    loads = load(
        [
            (offset_hbm, offset),
            (next_k_hbm, kernels.at[0]),
            (cotangent_hbm, tops),
            (next_f_hbm, turned_kernels.at[0]),
            (own_k_hbm, kernels.at[1]),
            (own_f_hbm, turned_kernels.at[1]),
            (cotangent_hbm, cotangent),
        ],
        sems,
        base,
    )
    base += len(loads)
    decays[0] = next_decay[...]
    decays[1] = own_decay[...]
    clear_borders(first_columns)
    clear_borders(second_columns)
    finish(brought)
    loads[0].wait()

    def coarse_rows(first, count):
        rows = pl.ds(first, count)
        for odd in range(2):
            states[0, rows, odd] = transform_rows(begins[rows, odd], matrix[...]) + offset[rows, odd]

    per_block(pairs, coarse_rows, whole=True)
    fill_forward(states.at[0], first_columns)
    out_coarse = pltpu.make_async_copy(states.at[0], coarse_end, sems.at[base])
    out_coarse.start()
    base += 1
    finish(loads[1:])
    late = [(states.at[layers], slab_end)]
    late += [(states.at[n], state_outs[n]) for n in range(layers)]
    late += [(acts.at[n], act_outs[n]) for n in range(layers)]

    def both_sweeps(index, carry):
        now, later = first_columns, second_columns
        for layer in range(layers):
            spread(paired, kernels[index, layer])

            def store(rows, first, odd, following, activation, layer=layer, target=later):
                states[layer + 1, rows, odd] = following
                acts[layer, rows, odd] = activation
                if layer < layers - 1:
                    put_columns(target, first, odd, following)
                else:
                    put_columns(target, first, odd, scaled_rows(tops[rows, odd], activation))

            forward_layer(states.at[layer], now, tools, decays[index, layer : layer + 1], store)
            now, later = later, now

        @pl.when(index == 1)
        def _():
            load(late, sems, base)

        for layer in reversed(range(layers)):
            spread(paired, turned_kernels[index, layer])

            def store_back(rows, first, odd, following, layer=layer, target=later):
                adjoint[rows, odd] = following
                if layer > 0:
                    put_columns(target, first, odd, scaled_rows(following, acts[layer - 1, rows, odd]))

            source = tops if layer == layers - 1 else adjoint
            backward_layer(source, now, tools, decays[index, layer : layer + 1], store_back)
            now, later = later, now

        @pl.when(index == 0)
        def _():
            out_coarse.wait()

            def again(first, count):
                rows = pl.ds(first, count)
                tops[rows] = jnp.where(last_slab, cotangent[rows], adjoint[rows])
                for odd in range(2):
                    begin = begins[rows, odd]
                    states[0, rows, odd] = begin
                    put_columns(first_columns, first, odd, begin)

            per_block(pairs, again)

        return carry

    lax.fori_loop(0, 2, both_sweeps, 0)

    outs = subtract_and_send(place[BACKWARD], group, chunks, adjoint, tops, turned, back_pieces, sems, 0)
    outs += load([(adjoint, back_offset)], sems, count_pieces)
    finish(outs)
    for number, (source, target) in enumerate(late):
        pltpu.make_async_copy(source, target, sems.at[base + number]).wait()


def middle(place, pieces, offset, cotangent, own, following, own_decay, next_decay, matrix, turned, group, chunks):
    layers = own[0].shape[0]
    field = offset.shape
    count = len(pieces)
    fields = [jax.ShapeDtypeStruct(field, F32)] * (3 + 2 * layers)
    results = pl.pallas_call(
        functools.partial(middle_kernel, layers, group, chunks),
        out_shape=fields + piece_shapes(field, group, chunks),
        in_specs=[SMEM] + [ANY] * (count + 6) + [VMEM] * 4,
        out_specs=[ANY] * (3 + 2 * layers + count),
        scratch_shapes=[pltpu.VMEM(field, F32)]
        + [pltpu.VMEM((layers + 1,) + field, F32), pltpu.VMEM((layers,) + field, F32)]
        + [pltpu.VMEM(field, F32)] * 4
        + scratch_of(field, 2)
        + [pltpu.VMEM((2,) + own[0].shape, BF16)] * 2
        + [pltpu.VMEM((2, layers, field[3]), F32), pltpu.SemaphoreType.DMA((count + 9 + 2 * layers,))],
        compiler_params=params(52),
        cost_estimate=cost(4.0 * layers, field),
    )(place, *pieces, offset, cotangent, *following, *own, own_decay, next_decay, matrix, turned)
    return results[:3], results[3 : 3 + layers], results[3 + layers : 3 + 2 * layers], results[3 + 2 * layers :]


def turn(whole, turned):
    taps, channels = whole.shape[0] // whole.shape[1], whole.shape[1]
    for tap in range(taps):
        block = whole[tap * channels : (tap + 1) * channels]
        other = taps - 1 - tap
        turned[other * channels : (other + 1) * channels] = block.T.astype(BF16)


def own_kernel(kernels, turned, whole):
    for layer in range(kernels.shape[0]):
        whole[...] = kernels[layer].astype(F32)
        turn(whole, turned.at[layer])


def turn_own(kernels):
    return pl.pallas_call(
        own_kernel,
        out_shape=jax.ShapeDtypeStruct(kernels.shape, BF16),
        in_specs=[VMEM],
        out_specs=VMEM,
        scratch_shapes=[pltpu.VMEM(kernels.shape[1:], F32)],
        compiler_params=params(),
    )(kernels)


def next_kernel(place, *refs):
    quarters, (kernels, turned, decay, whole) = refs[:4], refs[4:]
    layers = kernels.shape[0]
    rows = whole.shape[0] // 4
    chunk = (place[CHUNK] & 3)
    at = [chunk, chunk ^ 2, chunk ^ 1, chunk ^ 3]
    for layer in range(layers):
        for number in range(4):
            whole[pl.ds(at[number] * rows, rows)] = quarters[number][layer, 0:rows]
        kernels[layer] = whole[...].astype(BF16)
        turn(whole, turned.at[layer])
        decay[layer : layer + 1] = quarters[0][layer, rows : rows + 1]


def join_next(place, quarters):
    layers, rows, channels = quarters[0].shape
    shape = (layers, 4 * (rows - 8), channels)
    results = pl.pallas_call(
        next_kernel,
        out_shape=[jax.ShapeDtypeStruct(shape, BF16)] * 2 + [jax.ShapeDtypeStruct((layers, channels), F32)],
        in_specs=[SMEM] + [VMEM] * 4,
        out_specs=[VMEM] * 3,
        scratch_shapes=[pltpu.VMEM(shape[1:], F32)],
        compiler_params=params(),
    )(place, *quarters)
    return results[:2], results[2]


def turned_columns_kernel(state, turned, columns):
    pairs, _, side, _ = state.shape
    wide, depth = columns.shape[2:]
    clear_borders(columns)

    def fill(first, count):
        for odd in range(2):
            put_columns(columns, first, odd, state[pl.ds(first, count), odd])

    per_block(pairs, fill)
    for pair in range(pairs + 1):
        block = columns[pair].reshape(2 * wide, depth).astype(F32)
        turned[:, pair * 2 * wide : (pair + 1) * 2 * wide] = block.T.astype(BF16)


def turned_columns(state):
    shape = columns_shape(state.shape)
    return pl.pallas_call(
        turned_columns_kernel,
        out_shape=jax.ShapeDtypeStruct((shape[3], shape[0] * 2 * shape[2]), BF16),
        in_specs=[VMEM],
        out_specs=VMEM,
        scratch_shapes=[pltpu.VMEM(shape, BF16)],
        compiler_params=params(),
        cost_estimate=cost(0.4, state.shape),
    )(state)


def gradient_body(adjoint, activation, turned, ready, scaled, gradient, side):
    pairs = adjoint.shape[0]
    wide, channels = scaled.shape[2:]
    edge = jnp.zeros((2, wide, channels), BF16)
    scaled[0] = edge
    scaled[pairs + 1] = edge

    def fill(first, count):
        rows = pl.ds(first, count)
        for odd in range(2):
            own = scaled_rows(adjoint[rows, odd], activation[rows, odd])
            padded = jnp.concatenate([own, jnp.zeros((count, wide - side, channels), F32)], axis=1)
            scaled[pl.ds(first + 1, count), odd] = padded.astype(BF16)

    per_block(pairs, fill)
    ready()
    flat = scaled[...].reshape((2 * pairs + 4) * wide, channels)
    rows = (2 * pairs + 2) * wide
    shifted = [flat[(2 - tap) * wide : (2 - tap) * wide + rows] for tap in range(3)]
    products = jnp.dot(turned[...], jnp.concatenate(shifted, axis=1), preferred_element_type=F32)
    for row in range(3):
        for column in range(3):
            tap = 3 * row + column
            gradient[tap * channels : (tap + 1) * channels] = products[
                column * channels : (column + 1) * channels, row * channels : (row + 1) * channels
            ]


def scaled_shape(field):
    pairs, _, side, channels = field
    return (pairs + 2, 2, wide_of(side), channels)


def halve(place, gradient, keep, send):
    half = (place[CHUNK] & 1)
    rows = keep.shape[0]
    keep[...] = gradient[pl.ds(half * rows, rows)]
    send[...] = gradient[pl.ds((1 - half) * rows, rows)]


def top_kernel(group, chunks, place, *refs):
    count_pieces = group * len(chunks)
    pieces, refs = refs[:count_pieces], refs[count_pieces:]
    activation_hbm, turned_hbm, adjoint_out, keep, send = refs[:5]
    adjoint, activation, turned, shifted, gradient, sems = refs[5:]
    brought = bring_in(place[BACKWARD], group, chunks, pieces, adjoint, sems, 0)
    loads = load([(activation_hbm, activation), (turned_hbm, turned)], sems, count_pieces)
    finish(brought)
    out = load([(adjoint, adjoint_out)], sems, 0)
    loads[0].wait()
    gradient_body(adjoint, activation, turned, loads[1].wait, shifted, gradient, adjoint.shape[2])
    halve(place, gradient, keep, send)
    finish(out)


def top_gradient(place, pieces, activation, turned, group, chunks):
    field = activation.shape
    shape = columns_shape(field)
    taps = 9 * field[3]
    half = jax.ShapeDtypeStruct((taps // 2, field[3]), F32)
    return pl.pallas_call(
        functools.partial(top_kernel, group, chunks),
        out_shape=[jax.ShapeDtypeStruct(field, F32), half, half],
        in_specs=[SMEM] + [ANY] * (len(pieces) + 2),
        out_specs=[ANY, VMEM, VMEM],
        scratch_shapes=[
            pltpu.VMEM(field, F32),
            pltpu.VMEM(field, F32),
            pltpu.VMEM(turned.shape, BF16),
            pltpu.VMEM(scaled_shape(field), BF16),
            pltpu.VMEM((taps, field[3]), F32),
            pltpu.SemaphoreType.DMA((len(pieces) + 2,)),
        ],
        compiler_params=params(),
        cost_estimate=cost(1.5, field),
    )(place, *pieces, activation, turned)


def retreat_body(adjoint, activation, columns, tools, rate, store):
    clear_borders(columns)
    fill_backward(adjoint, activation, columns)
    backward_layer(adjoint, columns, tools, rate, store)


def lower_kernel(layer, place, adjoint, above, kernel, decay, below_hbm, turned_hbm, *refs):
    result_out, keep, send = refs[:3]
    result, below, turned, columns, paired, even, uneven, shifted, gradient, sems = refs[3:]
    loads = load([(below_hbm, below), (turned_hbm, turned)], sems, 0)
    spread(paired, kernel[layer])

    def store(rows, first, odd, fresh):
        result[rows, odd] = fresh

    retreat_body(adjoint, above, columns, (paired, even, uneven), decay[layer : layer + 1], store)
    out = load([(result, result_out)], sems, 2)
    loads[0].wait()
    gradient_body(result, below, turned, loads[1].wait, shifted, gradient, result.shape[2])
    halve(place, gradient, keep, send)
    finish(out)


def lower_gradient(place, layer, adjoint, above, kernels, decay, below, turned):
    field = adjoint.shape
    shape = columns_shape(field)
    taps = 9 * field[3]
    half = jax.ShapeDtypeStruct((taps // 2, field[3]), F32)
    return pl.pallas_call(
        functools.partial(lower_kernel, layer),
        out_shape=[jax.ShapeDtypeStruct(field, F32), half, half],
        in_specs=[SMEM] + [VMEM] * 4 + [ANY] * 2,
        out_specs=[ANY, VMEM, VMEM],
        scratch_shapes=[pltpu.VMEM(field, F32), pltpu.VMEM(field, F32), pltpu.VMEM(turned.shape, BF16)]
        + scratch_of(field, 1)
        + [pltpu.VMEM(scaled_shape(field), BF16), pltpu.VMEM((taps, field[3]), F32), pltpu.SemaphoreType.DMA((3,))],
        compiler_params=params(),
        cost_estimate=cost(2.0, field),
    )(place, adjoint, above, kernels, decay, below, turned)


def last_kernel(adjoint, activation, kernel, decay, tops, back_offset, turned, result, adjoint_end, columns, *tools):
    spread(tools[0], kernel[0])

    def store(rows, first, odd, fresh):
        result[rows, odd] = fresh

    retreat_body(adjoint, activation, columns, tools, decay[0:1], store)

    def coarse_rows(first, count):
        rows = pl.ds(first, count)
        for odd in range(2):
            adjoint_end[rows, odd] = transform_rows(tops[rows, odd], turned[...]) + back_offset[rows, odd]

    per_block(adjoint.shape[0], coarse_rows, whole=True)


def last_retreat(adjoint, activation, kernels, decay, tops, back_offset, turned):
    field = adjoint.shape
    return pl.pallas_call(
        last_kernel,
        out_shape=[jax.ShapeDtypeStruct(field, F32)] * 2,
        in_specs=[VMEM] * 7,
        out_specs=[VMEM] * 2,
        scratch_shapes=scratch_of(field, 1),
        compiler_params=params(),
        cost_estimate=cost(1.6, field),
    )(adjoint, activation, kernels, decay, tops, back_offset, turned)


def collect_kernel(layers, place, *refs):
    sources, out, held, sems = refs[:-3], refs[-3], refs[-2], refs[-1]
    half = (place[CHUNK] & 1)
    rows = out.shape[1] // 2
    if layers > 0:
        number = 0
        copies = []
        for layer in range(layers):
            for part in [half, 1 - half][: 1 if layer == 0 else 2]:
                copies.append((sources[number], out.at[layer, pl.ds(part * rows, rows)]))
                number += 1
        finish(load(copies, sems, 0))
    else:
        finish(load([(sources[0], out.at[0, pl.ds((1 - half) * rows, rows)])], sems, 0))


def collect(place, halves):
    layers = len(halves)
    rows, channels = halves[0][0].shape
    shape = jax.ShapeDtypeStruct((layers, 2 * rows, channels), F32)
    most = [half for both in halves for half in both]
    last = most.pop(1)
    scratch = [pltpu.VMEM((8, channels), F32), pltpu.SemaphoreType.DMA((2 * layers,))]
    out = pl.pallas_call(
        functools.partial(collect_kernel, layers),
        out_shape=shape,
        in_specs=[SMEM] + [VMEM] * len(most),
        out_specs=ANY,
        scratch_shapes=scratch,
        compiler_params=params(16),
        cost_estimate=cost(0.4, (rows, 2 * layers, channels)),
    )(place, *most)
    return pl.pallas_call(
        functools.partial(collect_kernel, 0),
        out_shape=shape,
        in_specs=[SMEM, VMEM, ANY],
        out_specs=ANY,
        scratch_shapes=scratch,
        input_output_aliases={2: 0},
        compiler_params=params(16),
    )(place, last, out)


def from_behind(shard, axis, by):
    devices = lax.axis_size(axis)
    pairs = [(i, i + by) for i in range(devices) if 0 <= i + by < devices]
    return lax.ppermute(shard, axis, pairs)


def swap(shard, bit):
    return lax.ppermute(shard, "dp", [(i, i ^ bit) for i in range(lax.axis_size("dp"))])


def order_of(index, size, backward):
    return size - 1 - index if backward else index


def group_of(size):
    for group in (GROUP, 2, 1):
        if size % group == 0:
            return group


def exchange(pieces, group, backward):
    size = lax.axis_size("layer")
    received = [pieces[0]]
    for shift in range(1, group):
        pairs = []
        for order in range(size):
            base = order - order % group
            target = base + (order + shift) % group
            pairs.append((order_of(order, size, backward), order_of(target, size, backward)))
        received.append(lax.ppermute(pieces[shift], "layer", pairs))
    return received


def coarse_chain(place, seed, pieces, matrices, group, chunks, backward, beside=()):
    size = lax.axis_size("layer")
    pairs = [(order_of(i, size, backward), order_of(i + group, size, backward)) for i in range(size - group)]
    received = []
    for chunk in range(len(chunks)):
        sent = pieces[chunk * group : (chunk + 1) * group]
        if chunk > 0:
            received[-1][1], *sent = lax.optimization_barrier((received[-1][1], *sent))
        received.append(exchange(sent, group, backward))
    carries = [jnp.zeros(pieces[chunk * group].shape, F32) for chunk in range(len(chunks))]
    partials = [None] * len(chunks)

    def partial_of(chunk):
        return partial_chain(place, seed, matrices, received[chunk], group, chunks, chunk, backward)

    for chunk in range(len(chunks)):
        if size > group:
            out = group_carry(place, seed, matrices, received[chunk], group, chunks, chunk, backward)
            carry = lax.ppermute(out, "layer", pairs)
            for _ in range(size // group - 2):
                carry = lax.ppermute(hop(carry, matrices[int(backward), whole_at(group)], out), "layer", pairs)
            carries[chunk] = carry
        if backward:
            partials[chunk] = partial_of(chunk)
    if backward:
        partials[-1], beside = lax.optimization_barrier((partials[-1], beside))
    else:
        if size > group:
            received, out = lax.optimization_barrier((received, out))
        partials = lax.optimization_barrier([partial_of(chunk) for chunk in range(len(chunks))])
    begins = [(carry, products, begun) for carry, (begun, products) in zip(carries, partials)]
    result = []
    for carry, products, begun in begins:
        result += exchange(complete_chain(carry, products, begun, group), group, backward)
    return result, beside


def sum_across(total):
    bit = 2
    while bit < lax.axis_size("dp"):
        total = total + swap(total, bit)
        bit *= 2
    return total


def per_device(images, kernels, damping, cotangent):
    layers, taps, channels = kernels.shape
    _, height, side, _ = images.shape
    size = lax.axis_size("layer")
    position = lax.axis_index("layer")
    dp_at = lax.axis_index("dp")
    field = (height // 2, 2, side, channels)
    images = images.reshape(field)
    cotangent = cotangent.reshape(field)
    group = group_of(size)
    quarter = field[0] // group
    chunks = chunks_of(quarter)
    back_order = size - 1 - position
    place = jnp.stack(
        [
            position,
            lax.rem(position, group),
            lax.rem(back_order, group),
            dp_at,
            (position < group).astype(jnp.int32),
            (back_order < group).astype(jnp.int32),
            jnp.int32(size),
            jnp.int32(0),
        ]
    ).astype(jnp.int32)

    parts, quarter_part, copies, matrix, turned_matrix = prelude(place, kernels, damping, group)

    lows = [from_behind(part, "layer", 1) for part in parts]
    highs = [swap(low, 1) for low in lows[:-1]]

    groups = [list(range(at, at + group)) for at in range(0, size, group)]
    lows[0], copies = lax.optimization_barrier((lows[0], copies))
    steps = lax.all_to_all(copies, "layer", 0, 0, axis_index_groups=groups, tiled=True)
    own = (kernels, turn_own(kernels))

    state = images
    for layer in range(layers - 1):
        state = fetched_layer(place, state, lows[layer], highs[layer])
    lows[-1], state, steps = lax.optimization_barrier((lows[-1], state, steps))
    highs.append(swap(lows[-1], 1))

    quarter_part, state = lax.optimization_barrier((quarter_part, state))
    first = from_behind(quarter_part, "layer", -1)

    offset, pieces = slab_offset(
        place, images, state, lows[-1], highs[-1], kernels, damping, matrix, group, chunks
    )
    first, pieces = lax.optimization_barrier((first, pieces))
    second = swap(first, 2)
    following, next_decay = join_next(place, [first, second, swap(first, 1), swap(second, 1)])
    matrices = group_matrices(steps)
    pieces, _ = coarse_chain(place, images, pieces, matrices, group, chunks, False)
    (slab_end, coarse_end, back_offset), states, acts, pieces = middle(
        place, pieces, offset, cotangent, own, following, damping, next_decay, matrix, turned_matrix, group, chunks
    )
    turned = [turned_columns(state) for state in states]
    pieces, turned = coarse_chain(place, cotangent, pieces, matrices, group, chunks, True, turned)
    tops, keep, send = top_gradient(place, pieces, acts[-1], turned[-1], group, chunks)
    adjoint = tops
    paired = [None] * layers
    halves = [None] * layers
    for layer in reversed(range(1, layers)):
        paired[layer] = (keep, send)
        adjoint, keep, send = lower_gradient(
            place, layer, adjoint, acts[layer], own[1], damping, acts[layer - 1], turned[layer - 1]
        )
        total = paired[layer][0] + swap(paired[layer][1], 1)
        adjoint, total = lax.optimization_barrier((adjoint, total))
        if layer < layers - 1:
            adjoint, summed = lax.optimization_barrier((adjoint, paired[layer + 1]))
            paired[layer + 1] = summed
        paired[layer] = sum_across(total)
    total = keep + swap(send, 1)
    adjoint, adjoint_end = last_retreat(adjoint, acts[0], own[1], damping, tops, back_offset, turned_matrix)
    adjoint, total = lax.optimization_barrier((adjoint, total))
    paired[0] = sum_across(total)
    halves = [(half, swap(half, 1)) for half in paired]
    full = (1, 1, height, side, channels)
    return (
        slab_end.reshape(full),
        coarse_end.reshape(full),
        adjoint.reshape(full),
        adjoint_end.reshape(full),
        collect(place, halves),
    )


def solution(mesh):
    in_specs = (
        P("dp", None, None, None),
        P("layer", None, None),
        P("layer", None),
        P("dp", None, None, None),
    )
    out_specs = (
        P("layer", "dp", None, None, None),
        P("layer", "dp", None, None, None),
        P("layer", "dp", None, None, None),
        P("layer", "dp", None, None, None),
        P("layer", None, None),
    )
    return jax.shard_map(
        per_device, mesh=mesh, in_specs=in_specs, out_specs=out_specs, check_vma=False
    )
```

```python
import functools
import math

import jax
import jax.numpy as jnp
from jax import lax
from jax.experimental import pallas as pl
from jax.experimental.pallas import tpu as pltpu
from jax.sharding import PartitionSpec as P

STEP = 0.125
F32 = jnp.float32
BF16 = jnp.bfloat16
BLOCK_PAIRS = 7
PRODUCT_PAIRS = 14
GROUP = 4


def wide_of(side):
    return -(-(side + 1) // 16) * 16


def columns_shape(field):
    pairs, _, side, channels = field
    return (pairs + 1, 2, wide_of(side), 3 * channels)


def block_of(pairs):
    return BLOCK_PAIRS if pairs % BLOCK_PAIRS == 0 else 1


def product_block(pairs):
    return PRODUCT_PAIRS if pairs % PRODUCT_PAIRS == 0 else block_of(pairs)


def per_block(pairs, body, whole=False):
    block = block_of(pairs)

    def step(number, carry):
        if whole:
            body(number * block, block)
        else:
            for pair in range(block):
                body(number * block + pair, 1)
        return carry

    lax.fori_loop(0, pairs // block, step, 0)


def clear_borders(columns):
    edge = jnp.zeros(columns.shape[2:], BF16)
    columns[0, 0] = edge
    columns[columns.shape[0] - 1, 1] = edge


def put_columns(columns, first, odd, rows):
    count, side, channels = rows.shape
    wide = columns.shape[2]
    here = jnp.concatenate([rows, jnp.zeros((count, wide - side, channels), F32)], axis=1)
    left = pltpu.roll(here, 1, 1)
    right = pltpu.roll(here, wide - 1, 1)
    columns[pl.ds(first + odd, count), 1 - odd] = jnp.concatenate([left, here, right], axis=2).astype(BF16)


def spread(paired, kernel):
    taps, channels = kernel.shape
    third = taps // 3
    blank = jnp.zeros((third, channels), BF16)
    paired[0:taps, 0:channels] = kernel
    paired[taps : taps + third, 0:channels] = blank
    paired[0:third, channels : 2 * channels] = blank
    paired[third : taps + third, channels : 2 * channels] = kernel


def convolve(columns, paired, results, emit, side):
    _, _, wide, depth = columns.shape
    channels = depth // 3
    pairs = columns.shape[0] - 1
    block = product_block(pairs)

    def product(number):
        first = number * block
        pieces = [
            columns[first : first + block, 0],
            columns[first : first + block, 1],
            columns[first + 1 : first + 1 + block, 0],
            columns[first + 1 : first + 1 + block, 1],
        ]
        left = jnp.concatenate([piece.reshape(block * wide, depth) for piece in pieces], axis=1)
        results[number % 2][...] = jnp.dot(left, paired[...], preferred_element_type=F32)

    product(0)
    for number in range(pairs // block):
        if number + 1 < pairs // block:
            product(number + 1)
        result = results[number % 2]
        for pair in range(block):
            for odd in range(2):
                preact = result[pair * wide : (pair + 1) * wide, odd * channels : (odd + 1) * channels]
                emit(number * block + pair, odd, preact.reshape(1, wide, channels)[:, :side])


def split_dot(left, matrix):
    high = left.astype(BF16)
    low = (left - high.astype(F32)).astype(BF16)
    m_high = matrix.astype(BF16)
    m_low = (matrix - m_high.astype(F32)).astype(BF16)
    return jnp.dot(
        jnp.concatenate([high, low, high], axis=1),
        jnp.concatenate([m_high, m_high, m_low], axis=0),
        preferred_element_type=F32,
    )


def transform_rows(rows, matrix):
    count, side, channels = rows.shape
    return split_dot(rows.reshape(count * side, channels), matrix).reshape(rows.shape)


def fill_forward(state, columns):
    def fill(first, count):
        for odd in range(2):
            put_columns(columns, first, odd, state[pl.ds(first, count), odd])

    per_block(state.shape[0], fill)


def forward_layer(current, columns, tools, rate, store):
    decay = rate.reshape(1, 1, -1)

    def emit(first, odd, preact):
        rows = pl.ds(first, 1)
        activation = jnp.tanh(preact)
        here = current[rows, odd]
        store(rows, first, odd, here + STEP * (activation - decay * here), activation)

    convolve(columns, tools[0], tools[1:], emit, current.shape[2])


def scaled_rows(adjoint, activation):
    return STEP * (1.0 - activation * activation) * adjoint


def fill_backward(state, activation, columns):
    def fill(first, count):
        rows = pl.ds(first, count)
        for odd in range(2):
            put_columns(columns, first, odd, scaled_rows(state[rows, odd], activation[rows, odd]))

    per_block(state.shape[0], fill)


def backward_layer(current, columns, tools, rate, store):
    decay = rate.reshape(1, 1, -1)

    def emit(first, odd, back_term):
        rows = pl.ds(first, 1)
        here = current[rows, odd]
        store(rows, first, odd, here - STEP * decay * here + back_term)

    convolve(columns, tools[0], tools[1:], emit, current.shape[2])


def params(mebibytes=40):
    return pltpu.CompilerParams(vmem_limit_bytes=mebibytes * 1024 * 1024)


def cost(share, shape, free=False):
    share = 0.0 if free else share
    flops = 8 * share * math.prod(shape) * shape[-1] * 9
    return pl.CostEstimate(flops=int(flops), bytes_accessed=int(8 * share * math.prod(shape)), transcendentals=0)


ANY = pl.BlockSpec(memory_space=pl.ANY)
HBM = pl.BlockSpec(memory_space=pltpu.HBM)
VMEM = pl.BlockSpec(memory_space=pltpu.VMEM)
SMEM = pl.BlockSpec(memory_space=pltpu.SMEM)

def chunks_of(quarter):
    return (quarter - quarter // 2, quarter // 2) if quarter > 1 else (quarter,)


POSITION, FORWARD, BACKWARD, CHUNK, FORWARD_HEAD, BACKWARD_HEAD, SIZE = range(7)


def load(pairs_of_refs, sems, base):
    copies = []
    for number, (source, target) in enumerate(pairs_of_refs):
        copies.append(pltpu.make_async_copy(source, target, sems.at[base + number]))
        copies[-1].start()
    return copies


def finish(copies):
    for copy in copies:
        copy.wait()


def scratch_of(field, buffers):
    shape = columns_shape(field)
    products = pltpu.VMEM((product_block(field[0]) * shape[2], 2 * field[3]), F32)
    return [pltpu.VMEM(shape, BF16)] * buffers + [pltpu.VMEM((4 * shape[3], 2 * field[3]), BF16), products, products]


def join_halves(whole, low, high, half):
    rows = whole.shape[0] // 2
    whole[pl.ds(half * rows, rows)] = low[0:rows].astype(BF16)
    whole[pl.ds((1 - half) * rows, rows)] = high[0:rows].astype(BF16)


def layer_kernel(place, field, low, high, result, columns, paired, even, uneven, whole):
    half = (place[CHUNK] & 1)
    join_halves(whole, low, high, half)
    spread(paired, whole[...])
    rows = whole.shape[0] // 2
    clear_borders(columns)
    fill_forward(field, columns)

    def store(where, first, odd, following, activation):
        result[where, odd] = following

    forward_layer(field, columns, (paired, even, uneven), low[rows : rows + 1], store)


def fetched_layer(place, field, low, high):
    rows, channels = low.shape[0] - 8, low.shape[1]
    return pl.pallas_call(
        layer_kernel,
        out_shape=jax.ShapeDtypeStruct(field.shape, F32),
        in_specs=[SMEM] + [VMEM] * 3,
        out_specs=VMEM,
        scratch_shapes=scratch_of(field.shape, 1) + [pltpu.VMEM((2 * rows, channels), BF16)],
        compiler_params=params(),
        cost_estimate=cost(1.0, field.shape),
    )(place, field, low, high)


def wrapped(index, group):
    return index & (group - 1)


def piece_refs(member, group, chunks, field, shift, chunk, forward_shift):
    quarter = field.shape[0] // group
    offset = sum(chunks[:chunk])
    turn = member + shift if forward_shift else member - shift + group
    return field.at[pl.ds(wrapped(turn, group) * quarter + offset, chunks[chunk])]


def subtract_and_send(member, group, chunks, field, tops, matrix, outs, sems, base):
    quarter = field.shape[0] // group
    copies = []
    for shift in [*range(1, group), 0]:
        rows = pl.ds(wrapped(member + shift, group) * quarter, quarter)
        for odd in range(2):
            field[rows, odd] = field[rows, odd] - transform_rows(tops[rows, odd], matrix[...])
        for chunk in range(len(chunks)):
            number = chunk * group + shift
            source = piece_refs(member, group, chunks, field, shift, chunk, True)
            copies.append(pltpu.make_async_copy(source, outs[number], sems.at[base + number]))
            copies[-1].start()
    return copies


def bring_in(member, group, chunks, pieces, field, sems, base):
    copies = []
    for chunk in range(len(chunks)):
        for shift in range(group):
            number = chunk * group + shift
            target = piece_refs(member, group, chunks, field, shift, chunk, False)
            copies.append(pltpu.make_async_copy(pieces[number], target, sems.at[base + number]))
            copies[-1].start()
    return copies


def piece_shapes(field, group, chunks):
    return [jax.ShapeDtypeStruct((count,) + field[1:], F32) for count in chunks for _ in range(group)]


def offset_kernel(layers, group, chunks, place, images_hbm, field, low, high, kernels_hbm, decay, matrix, *refs):
    count_pieces = group * len(chunks)
    out, pieces = refs[0], refs[1 : 1 + count_pieces]
    images, kernels, starts, offset, now, later, paired, even, uneven, whole, sems = refs[1 + count_pieces :]
    tools = (paired, even, uneven)
    pairs = offset.shape[0]
    loads = load([(images_hbm, images), (kernels_hbm, kernels)], sems, 0)
    half = (place[CHUNK] & 1)
    first_slab = place[POSITION] == 0
    join_halves(whole, low, high, half)
    spread(paired, whole[...])
    rows = whole.shape[0] // 2
    clear_borders(now)
    clear_borders(later)
    fill_forward(field, now)
    loads[0].wait()

    def store_start(where, first, odd, following, activation):
        begin = jnp.where(first_slab, images[where, odd], following)
        starts[where, odd] = begin
        put_columns(later, first, odd, begin)

    forward_layer(field, now, tools, low[rows : rows + 1], store_start)
    loads[1].wait()
    for layer in range(layers):
        now, later = later, now
        spread(paired, kernels[layer])

        def store(where, first, odd, following, activation, last=layer == layers - 1, target=later):
            if not last:
                put_columns(target, first, odd, following)
            offset[where, odd] = following

        source = starts if layer == 0 else offset
        forward_layer(source, now, tools, decay[layer : layer + 1], store)

    copies = subtract_and_send(place[FORWARD], group, chunks, offset, starts, matrix, pieces, sems, 3)
    copies += load([(offset, out)], sems, 2)
    finish(copies)


def slab_offset(place, images, field, low, high, kernels, decay, matrix, group, chunks):
    layers, taps, channels = kernels.shape
    shape = images.shape
    count = group * len(chunks)
    results = pl.pallas_call(
        functools.partial(offset_kernel, layers, group, chunks),
        out_shape=[jax.ShapeDtypeStruct(shape, F32)] + piece_shapes(shape, group, chunks),
        in_specs=[SMEM, ANY, VMEM, VMEM, VMEM, ANY, VMEM, VMEM],
        out_specs=[HBM] * (1 + count),
        scratch_shapes=[pltpu.VMEM(shape, F32), pltpu.VMEM(kernels.shape, BF16)]
        + [pltpu.VMEM(shape, F32)] * 2
        + scratch_of(shape, 2)
        + [pltpu.VMEM((taps, channels), BF16), pltpu.SemaphoreType.DMA((3 + count,))],
        compiler_params=params(),
        cost_estimate=cost(layers + 1.0, shape),
    )(place, images, field, low, high, kernels, decay, matrix)
    return results[0], results[1:]


def split_matrix(matrix):
    high = matrix.astype(BF16)
    low = (matrix - high.astype(F32)).astype(BF16)
    return jnp.concatenate([high, high, low], axis=0)


def split_rows(rows):
    high = rows.astype(BF16)
    low = (rows - high.astype(F32)).astype(BF16)
    return jnp.concatenate([high, low, high], axis=1)


def identity(channels):
    rows = lax.broadcasted_iota(jnp.int32, (channels, channels), 0)
    columns = lax.broadcasted_iota(jnp.int32, (channels, channels), 1)
    return (rows == columns).astype(F32)


def prelude_kernel(place, kernels, damping, *outs):
    layers, taps, channels = kernels.shape
    parts, (quarter, copies, matrix, turned) = outs[:layers], outs[layers:]
    half_rows, quarter_rows = taps // 2, taps // 4
    half, chunk = (place[CHUNK] & 1), (place[CHUNK] & 3)
    for layer in range(layers):
        rate = jnp.broadcast_to(damping[layer : layer + 1], (8, channels))
        parts[layer][0:half_rows] = kernels[layer, pl.ds(half * half_rows, half_rows)].astype(F32)
        parts[layer][half_rows : half_rows + 8] = rate
        quarter[layer, 0:quarter_rows] = kernels[layer, pl.ds(chunk * quarter_rows, quarter_rows)].astype(F32)
        quarter[layer, quarter_rows : quarter_rows + 8] = rate
    total = kernels[0, 0:channels].astype(F32)
    for tap in range(1, taps // channels):
        total += kernels[0, tap * channels : (tap + 1) * channels].astype(F32)
    diagonal = identity(channels) * (1.0 - layers * STEP * damping[0:1])
    coarse = diagonal + layers * STEP * total
    for member in range(copies.shape[0]):
        copies[member] = coarse
    matrix[...] = coarse
    turned[...] = coarse.T


def prelude(place, kernels, damping, group):
    layers, taps, channels = kernels.shape
    part = jax.ShapeDtypeStruct((taps // 2 + 8, channels), F32)
    quarter = jax.ShapeDtypeStruct((layers, taps // 4 + 8, channels), F32)
    square = jax.ShapeDtypeStruct((channels, channels), F32)
    results = pl.pallas_call(
        prelude_kernel,
        out_shape=[part] * layers + [quarter, jax.ShapeDtypeStruct((group, channels, channels), F32), square, square],
        in_specs=[SMEM] + [VMEM] * 2,
        out_specs=[VMEM] * (layers + 4),
        compiler_params=params(60),
    )(place, kernels, damping)
    return results[:layers], *results[layers:]


def step_at(group, index):
    return index


def before_at(group, index):
    return group + index


def after_at(group, index):
    return 2 * group + index


def whole_at(group):
    return 3 * group


def matrices_kernel(group, held, out):
    channels = held.shape[1]
    for backward in range(2):
        ordered = [held[group - 1 - step].T if backward else held[step] for step in range(group)]
        product = identity(channels)
        for step in range(group):
            split = split_matrix(ordered[step])
            out[backward, step_at(group, step)] = split
            out[backward, before_at(group, step)] = split_matrix(product)
            product = ordered[0] if step == 0 else jnp.dot(split_rows(product), split, preferred_element_type=F32)
        out[backward, whole_at(group)] = split_matrix(product)
        product = identity(channels)
        for step in reversed(range(group)):
            out[backward, after_at(group, step)] = split_matrix(product)
            if step == group - 1:
                product = ordered[step]
            else:
                product = jnp.dot(split_rows(ordered[step]), split_matrix(product), preferred_element_type=F32)


def group_matrices(steps):
    group, channels, _ = steps.shape
    return pl.pallas_call(
        functools.partial(matrices_kernel, group),
        out_shape=jax.ShapeDtypeStruct((2, 3 * group + 1, 3 * channels, channels), BF16),
        in_specs=[VMEM],
        out_specs=VMEM,
        compiler_params=params(16),
    )(steps)


def flat_of(shape):
    return (shape[0] * shape[1] * shape[2], shape[3])


def carry_kernel(group, chunks, chunk, backward, place, seed, matrices, *refs):
    pieces, (carry, start, right, sems) = refs[:group], refs[group:]
    member = place[BACKWARD if backward else FORWARD]
    leads = place[BACKWARD_HEAD if backward else FORWARD_HEAD] == 1
    depth = right.shape[0] // (group + 1)
    source = piece_refs(member, group, chunks, seed, 0, chunk, True)
    loads = [(source, start), (matrices.at[backward, whole_at(group)], right.at[pl.ds(group * depth, depth)])]
    for shift in range(group):
        slab = wrapped(member - shift + group, group)
        loads.append((matrices.at[backward, after_at(group, slab)], right.at[pl.ds(shift * depth, depth)]))
    loads = load(loads, sems, 0)
    flat = flat_of(start.shape)
    left = [split_rows(pieces[shift][...].reshape(flat)) for shift in range(group)]
    finish(loads)
    left.append(split_rows(jnp.where(leads, start[...], 0.0).reshape(flat)))
    total = jnp.dot(jnp.concatenate(left, axis=1), right[...], preferred_element_type=F32)
    carry[...] = total.reshape(start.shape)


def group_carry(place, seed, matrices, pieces, group, chunks, chunk, backward):
    shape = pieces[0].shape
    depth, channels = matrices.shape[2:]
    return pl.pallas_call(
        functools.partial(carry_kernel, group, chunks, chunk, int(backward)),
        out_shape=jax.ShapeDtypeStruct(shape, F32),
        in_specs=[SMEM, ANY, ANY] + [VMEM] * group,
        out_specs=VMEM,
        scratch_shapes=[
            pltpu.VMEM(shape, F32),
            pltpu.VMEM(((group + 1) * depth, channels), BF16),
            pltpu.SemaphoreType.DMA((group + 2,)),
        ],
        compiler_params=params(24),
        cost_estimate=cost(1.0 * group, shape),
    )(place, seed, matrices, *pieces)


def partial_kernel(group, chunks, chunk, backward, place, seed, matrices, *refs):
    pieces, (begun, products, full, held, start, sets, sems) = refs[:group], refs[group:]
    member = place[BACKWARD if backward else FORWARD]
    leads = place[BACKWARD_HEAD if backward else FORWARD_HEAD] == 1
    source = piece_refs(member, group, chunks, seed, 0, chunk, True)
    loads = load([(source, start), (matrices.at[backward, pl.ds(0, 2 * group)], sets)], sems, 0)
    for shift in range(group):
        held[wrapped(member - shift + group, group)] = pieces[shift][...]
    finish(loads)
    shape = start.shape
    flat = flat_of(shape)
    state = jnp.where(leads, start[...], 0.0).reshape(flat)
    full[0] = state.reshape(shape)
    for slab in range(group - 1):
        step = sets[step_at(group, slab)]
        state = jnp.dot(split_rows(state), step, preferred_element_type=F32) + held[slab].reshape(flat)
        full[slab + 1] = state.reshape(shape)
    channels = shape[3]
    for shift in range(group):
        slab = wrapped(member + shift, group)
        begun[shift] = full[slab]
        products[:, shift * channels : (shift + 1) * channels] = sets[before_at(group, slab)]


def partial_chain(place, seed, matrices, pieces, group, chunks, chunk, backward):
    shape = pieces[0].shape
    depth, channels = matrices.shape[2:]
    stack = (group,) + shape
    return pl.pallas_call(
        functools.partial(partial_kernel, group, chunks, chunk, int(backward)),
        out_shape=[jax.ShapeDtypeStruct(stack, F32), jax.ShapeDtypeStruct((depth, group * channels), BF16)],
        in_specs=[SMEM, ANY, ANY] + [VMEM] * group,
        out_specs=[VMEM] * 2,
        scratch_shapes=[
            pltpu.VMEM(stack, F32),
            pltpu.VMEM(stack, F32),
            pltpu.VMEM(shape, F32),
            pltpu.VMEM((2 * group, depth, channels), BF16),
            pltpu.SemaphoreType.DMA((2,)),
        ],
        compiler_params=params(24),
        cost_estimate=cost(0.8 * group, shape, not backward),
    )(place, seed, matrices, *pieces)


def hop_kernel(carry, whole, own, result):
    shape = own.shape
    moved = jnp.dot(split_rows(carry[...].reshape(flat_of(shape))), whole[...], preferred_element_type=F32)
    result[...] = own[...] + moved.reshape(shape)


def hop(carry, whole, own):
    return pl.pallas_call(
        hop_kernel,
        out_shape=jax.ShapeDtypeStruct(own.shape, F32),
        in_specs=[VMEM] * 3,
        out_specs=VMEM,
        compiler_params=params(24),
        cost_estimate=cost(0.8, own.shape),
    )(carry, whole, own)


def complete_kernel(group, carry, products, begun, *outs):
    shape = carry.shape
    channels = shape[3]
    moved = jnp.dot(split_rows(carry[...].reshape(flat_of(shape))), products[...], preferred_element_type=F32)
    for shift in range(group):
        part = moved[:, shift * channels : (shift + 1) * channels]
        outs[shift][...] = begun[shift] + part.reshape(shape)


def complete_chain(carry, products, begun, group):
    shape = carry.shape
    return pl.pallas_call(
        functools.partial(complete_kernel, group),
        out_shape=[jax.ShapeDtypeStruct(shape, F32)] * group,
        in_specs=[VMEM] * 3,
        out_specs=[VMEM] * group,
        compiler_params=params(24),
        cost_estimate=cost(0.2 * group, shape),
    )(carry, products, begun)


def middle_kernel(layers, group, chunks, place, *refs):
    count_pieces = group * len(chunks)
    pieces, refs = refs[:count_pieces], refs[count_pieces:]
    (offset_hbm, cotangent_hbm, next_k_hbm, next_f_hbm, own_k_hbm, own_f_hbm, own_decay, next_decay, matrix, turned) = refs[:10]
    refs = refs[10:]
    (slab_end, coarse_end, back_offset), refs = refs[:3], refs[3:]
    state_outs, refs = refs[:layers], refs[layers:]
    act_outs, refs = refs[:layers], refs[layers:]
    back_pieces, refs = refs[:count_pieces], refs[count_pieces:]
    (begins, states, acts, offset, cotangent, tops, adjoint, first_columns, second_columns) = refs[:9]
    tools, (kernels, turned_kernels, decays, sems) = refs[9:12], refs[12:]
    paired = tools[0]
    pairs = offset.shape[0]
    last_slab = place[POSITION] == place[SIZE] - 1

    brought = bring_in(place[FORWARD], group, chunks, pieces, begins, sems, 0)
    base = count_pieces
    loads = load(
        [
            (offset_hbm, offset),
            (next_k_hbm, kernels.at[0]),
            (cotangent_hbm, tops),
            (next_f_hbm, turned_kernels.at[0]),
            (own_k_hbm, kernels.at[1]),
            (own_f_hbm, turned_kernels.at[1]),
            (cotangent_hbm, cotangent),
        ],
        sems,
        base,
    )
    base += len(loads)
    decays[0] = next_decay[...]
    decays[1] = own_decay[...]
    clear_borders(first_columns)
    clear_borders(second_columns)
    finish(brought)
    loads[0].wait()

    def coarse_rows(first, count):
        rows = pl.ds(first, count)
        for odd in range(2):
            states[0, rows, odd] = transform_rows(begins[rows, odd], matrix[...]) + offset[rows, odd]

    per_block(pairs, coarse_rows, whole=True)
    fill_forward(states.at[0], first_columns)
    out_coarse = pltpu.make_async_copy(states.at[0], coarse_end, sems.at[base])
    out_coarse.start()
    base += 1
    finish(loads[1:])
    late = [(states.at[layers], slab_end)]
    late += [(states.at[n], state_outs[n]) for n in range(layers)]
    late += [(acts.at[n], act_outs[n]) for n in range(layers)]

    def both_sweeps(index, carry):
        now, later = first_columns, second_columns
        for layer in range(layers):
            spread(paired, kernels[index, layer])

            def store(rows, first, odd, following, activation, layer=layer, target=later):
                states[layer + 1, rows, odd] = following
                acts[layer, rows, odd] = activation
                if layer < layers - 1:
                    put_columns(target, first, odd, following)
                else:
                    put_columns(target, first, odd, scaled_rows(tops[rows, odd], activation))

            forward_layer(states.at[layer], now, tools, decays[index, layer : layer + 1], store)
            now, later = later, now

        @pl.when(index == 1)
        def _():
            load(late, sems, base)

        for layer in reversed(range(layers)):
            spread(paired, turned_kernels[index, layer])

            def store_back(rows, first, odd, following, layer=layer, target=later):
                adjoint[rows, odd] = following
                if layer > 0:
                    put_columns(target, first, odd, scaled_rows(following, acts[layer - 1, rows, odd]))

            source = tops if layer == layers - 1 else adjoint
            backward_layer(source, now, tools, decays[index, layer : layer + 1], store_back)
            now, later = later, now

        @pl.when(index == 0)
        def _():
            out_coarse.wait()

            def again(first, count):
                rows = pl.ds(first, count)
                tops[rows] = jnp.where(last_slab, cotangent[rows], adjoint[rows])
                for odd in range(2):
                    begin = begins[rows, odd]
                    states[0, rows, odd] = begin
                    put_columns(first_columns, first, odd, begin)

            per_block(pairs, again)

        return carry

    lax.fori_loop(0, 2, both_sweeps, 0)

    outs = subtract_and_send(place[BACKWARD], group, chunks, adjoint, tops, turned, back_pieces, sems, 0)
    outs += load([(adjoint, back_offset)], sems, count_pieces)
    finish(outs)
    for number, (source, target) in enumerate(late):
        pltpu.make_async_copy(source, target, sems.at[base + number]).wait()


def middle(place, pieces, offset, cotangent, own, following, own_decay, next_decay, matrix, turned, group, chunks):
    layers = own[0].shape[0]
    field = offset.shape
    count = len(pieces)
    fields = [jax.ShapeDtypeStruct(field, F32)] * (3 + 2 * layers)
    results = pl.pallas_call(
        functools.partial(middle_kernel, layers, group, chunks),
        out_shape=fields + piece_shapes(field, group, chunks),
        in_specs=[SMEM] + [ANY] * (count + 6) + [VMEM] * 4,
        out_specs=[ANY] * (3 + 2 * layers + count),
        scratch_shapes=[pltpu.VMEM(field, F32)]
        + [pltpu.VMEM((layers + 1,) + field, F32), pltpu.VMEM((layers,) + field, F32)]
        + [pltpu.VMEM(field, F32)] * 4
        + scratch_of(field, 2)
        + [pltpu.VMEM((2,) + own[0].shape, BF16)] * 2
        + [pltpu.VMEM((2, layers, field[3]), F32), pltpu.SemaphoreType.DMA((count + 9 + 2 * layers,))],
        compiler_params=params(52),
        cost_estimate=cost(4.0 * layers, field),
    )(place, *pieces, offset, cotangent, *following, *own, own_decay, next_decay, matrix, turned)
    return results[:3], results[3 : 3 + layers], results[3 + layers : 3 + 2 * layers], results[3 + 2 * layers :]


def turn(whole, turned):
    taps, channels = whole.shape[0] // whole.shape[1], whole.shape[1]
    for tap in range(taps):
        block = whole[tap * channels : (tap + 1) * channels]
        other = taps - 1 - tap
        turned[other * channels : (other + 1) * channels] = block.T.astype(BF16)


def own_kernel(kernels, turned, whole):
    for layer in range(kernels.shape[0]):
        whole[...] = kernels[layer].astype(F32)
        turn(whole, turned.at[layer])


def turn_own(kernels):
    return pl.pallas_call(
        own_kernel,
        out_shape=jax.ShapeDtypeStruct(kernels.shape, BF16),
        in_specs=[VMEM],
        out_specs=VMEM,
        scratch_shapes=[pltpu.VMEM(kernels.shape[1:], F32)],
        compiler_params=params(),
    )(kernels)


def next_kernel(place, *refs):
    quarters, (kernels, turned, decay, whole) = refs[:4], refs[4:]
    layers = kernels.shape[0]
    rows = whole.shape[0] // 4
    chunk = (place[CHUNK] & 3)
    at = [chunk, chunk ^ 2, chunk ^ 1, chunk ^ 3]
    for layer in range(layers):
        for number in range(4):
            whole[pl.ds(at[number] * rows, rows)] = quarters[number][layer, 0:rows]
        kernels[layer] = whole[...].astype(BF16)
        turn(whole, turned.at[layer])
        decay[layer : layer + 1] = quarters[0][layer, rows : rows + 1]


def join_next(place, quarters):
    layers, rows, channels = quarters[0].shape
    shape = (layers, 4 * (rows - 8), channels)
    results = pl.pallas_call(
        next_kernel,
        out_shape=[jax.ShapeDtypeStruct(shape, BF16)] * 2 + [jax.ShapeDtypeStruct((layers, channels), F32)],
        in_specs=[SMEM] + [VMEM] * 4,
        out_specs=[VMEM] * 3,
        scratch_shapes=[pltpu.VMEM(shape[1:], F32)],
        compiler_params=params(),
    )(place, *quarters)
    return results[:2], results[2]


def turned_columns_kernel(state, turned, columns):
    pairs, _, side, _ = state.shape
    wide, depth = columns.shape[2:]
    clear_borders(columns)

    def fill(first, count):
        for odd in range(2):
            put_columns(columns, first, odd, state[pl.ds(first, count), odd])

    per_block(pairs, fill)
    for pair in range(pairs + 1):
        block = columns[pair].reshape(2 * wide, depth).astype(F32)
        turned[:, pair * 2 * wide : (pair + 1) * 2 * wide] = block.T.astype(BF16)


def turned_columns(state):
    shape = columns_shape(state.shape)
    return pl.pallas_call(
        turned_columns_kernel,
        out_shape=jax.ShapeDtypeStruct((shape[3], shape[0] * 2 * shape[2]), BF16),
        in_specs=[VMEM],
        out_specs=VMEM,
        scratch_shapes=[pltpu.VMEM(shape, BF16)],
        compiler_params=params(),
        cost_estimate=cost(0.4, state.shape),
    )(state)


def gradient_body(adjoint, activation, turned, ready, scaled, gradient, side):
    pairs = adjoint.shape[0]
    wide, channels = scaled.shape[2:]
    edge = jnp.zeros((2, wide, channels), BF16)
    scaled[0] = edge
    scaled[pairs + 1] = edge

    def fill(first, count):
        rows = pl.ds(first, count)
        for odd in range(2):
            own = scaled_rows(adjoint[rows, odd], activation[rows, odd])
            padded = jnp.concatenate([own, jnp.zeros((count, wide - side, channels), F32)], axis=1)
            scaled[pl.ds(first + 1, count), odd] = padded.astype(BF16)

    per_block(pairs, fill)
    ready()
    flat = scaled[...].reshape((2 * pairs + 4) * wide, channels)
    rows = (2 * pairs + 2) * wide
    shifted = [flat[(2 - tap) * wide : (2 - tap) * wide + rows] for tap in range(3)]
    products = jnp.dot(turned[...], jnp.concatenate(shifted, axis=1), preferred_element_type=F32)
    for row in range(3):
        for column in range(3):
            tap = 3 * row + column
            gradient[tap * channels : (tap + 1) * channels] = products[
                column * channels : (column + 1) * channels, row * channels : (row + 1) * channels
            ]


def scaled_shape(field):
    pairs, _, side, channels = field
    return (pairs + 2, 2, wide_of(side), channels)


def halve(place, gradient, keep, send):
    half = (place[CHUNK] & 1)
    rows = keep.shape[0]
    keep[...] = gradient[pl.ds(half * rows, rows)]
    send[...] = gradient[pl.ds((1 - half) * rows, rows)]


def top_kernel(group, chunks, place, *refs):
    count_pieces = group * len(chunks)
    pieces, refs = refs[:count_pieces], refs[count_pieces:]
    activation_hbm, turned_hbm, adjoint_out, keep, send = refs[:5]
    adjoint, activation, turned, shifted, gradient, sems = refs[5:]
    brought = bring_in(place[BACKWARD], group, chunks, pieces, adjoint, sems, 0)
    loads = load([(activation_hbm, activation), (turned_hbm, turned)], sems, count_pieces)
    finish(brought)
    out = load([(adjoint, adjoint_out)], sems, 0)
    loads[0].wait()
    gradient_body(adjoint, activation, turned, loads[1].wait, shifted, gradient, adjoint.shape[2])
    halve(place, gradient, keep, send)
    finish(out)


def top_gradient(place, pieces, activation, turned, group, chunks):
    field = activation.shape
    shape = columns_shape(field)
    taps = 9 * field[3]
    half = jax.ShapeDtypeStruct((taps // 2, field[3]), F32)
    return pl.pallas_call(
        functools.partial(top_kernel, group, chunks),
        out_shape=[jax.ShapeDtypeStruct(field, F32), half, half],
        in_specs=[SMEM] + [ANY] * len(pieces) + [HBM] * 2,
        out_specs=[ANY, VMEM, VMEM],
        scratch_shapes=[
            pltpu.VMEM(field, F32),
            pltpu.VMEM(field, F32),
            pltpu.VMEM(turned.shape, BF16),
            pltpu.VMEM(scaled_shape(field), BF16),
            pltpu.VMEM((taps, field[3]), F32),
            pltpu.SemaphoreType.DMA((len(pieces) + 2,)),
        ],
        compiler_params=params(),
        cost_estimate=cost(1.5, field),
    )(place, *pieces, activation, turned)


def retreat_body(adjoint, activation, columns, tools, rate, store):
    clear_borders(columns)
    fill_backward(adjoint, activation, columns)
    backward_layer(adjoint, columns, tools, rate, store)


def lower_kernel(layer, place, adjoint, above, kernel, decay, below_hbm, turned_hbm, *refs):
    result_out, keep, send = refs[:3]
    result, below, turned, columns, paired, even, uneven, shifted, gradient, sems = refs[3:]
    loads = load([(below_hbm, below), (turned_hbm, turned)], sems, 0)
    spread(paired, kernel[layer])

    def store(rows, first, odd, fresh):
        result[rows, odd] = fresh

    retreat_body(adjoint, above, columns, (paired, even, uneven), decay[layer : layer + 1], store)
    out = load([(result, result_out)], sems, 2)
    loads[0].wait()
    gradient_body(result, below, turned, loads[1].wait, shifted, gradient, result.shape[2])
    halve(place, gradient, keep, send)
    finish(out)


def lower_gradient(place, layer, adjoint, above, kernels, decay, below, turned):
    field = adjoint.shape
    shape = columns_shape(field)
    taps = 9 * field[3]
    half = jax.ShapeDtypeStruct((taps // 2, field[3]), F32)
    return pl.pallas_call(
        functools.partial(lower_kernel, layer),
        out_shape=[jax.ShapeDtypeStruct(field, F32), half, half],
        in_specs=[SMEM] + [VMEM] * 4 + [ANY] * 2,
        out_specs=[ANY, VMEM, VMEM],
        scratch_shapes=[pltpu.VMEM(field, F32), pltpu.VMEM(field, F32), pltpu.VMEM(turned.shape, BF16)]
        + scratch_of(field, 1)
        + [pltpu.VMEM(scaled_shape(field), BF16), pltpu.VMEM((taps, field[3]), F32), pltpu.SemaphoreType.DMA((3,))],
        compiler_params=params(),
        cost_estimate=cost(2.0, field),
    )(place, adjoint, above, kernels, decay, below, turned)


def last_kernel(adjoint, activation, kernel, decay, tops, back_offset, turned, result, adjoint_end, columns, *tools):
    spread(tools[0], kernel[0])

    def store(rows, first, odd, fresh):
        result[rows, odd] = fresh

    retreat_body(adjoint, activation, columns, tools, decay[0:1], store)

    def coarse_rows(first, count):
        rows = pl.ds(first, count)
        for odd in range(2):
            adjoint_end[rows, odd] = transform_rows(tops[rows, odd], turned[...]) + back_offset[rows, odd]

    per_block(adjoint.shape[0], coarse_rows, whole=True)


def last_retreat(adjoint, activation, kernels, decay, tops, back_offset, turned):
    field = adjoint.shape
    return pl.pallas_call(
        last_kernel,
        out_shape=[jax.ShapeDtypeStruct(field, F32)] * 2,
        in_specs=[VMEM] * 7,
        out_specs=[VMEM] * 2,
        scratch_shapes=scratch_of(field, 1),
        compiler_params=params(),
        cost_estimate=cost(1.6, field),
    )(adjoint, activation, kernels, decay, tops, back_offset, turned)


def collect_kernel(layers, place, *refs):
    sources, out, held, sems = refs[:-3], refs[-3], refs[-2], refs[-1]
    half = (place[CHUNK] & 1)
    rows = out.shape[1] // 2
    if layers > 0:
        number = 0
        copies = []
        for layer in range(layers):
            for part in [half, 1 - half][: 1 if layer == 0 else 2]:
                copies.append((sources[number], out.at[layer, pl.ds(part * rows, rows)]))
                number += 1
        finish(load(copies, sems, 0))
    else:
        finish(load([(sources[0], out.at[0, pl.ds((1 - half) * rows, rows)])], sems, 0))


def collect(place, halves):
    layers = len(halves)
    rows, channels = halves[0][0].shape
    shape = jax.ShapeDtypeStruct((layers, 2 * rows, channels), F32)
    most = [half for both in halves for half in both]
    last = most.pop(1)
    scratch = [pltpu.VMEM((8, channels), F32), pltpu.SemaphoreType.DMA((2 * layers,))]
    out = pl.pallas_call(
        functools.partial(collect_kernel, layers),
        out_shape=shape,
        in_specs=[SMEM] + [VMEM] * len(most),
        out_specs=ANY,
        scratch_shapes=scratch,
        compiler_params=params(16),
        cost_estimate=cost(0.4, (rows, 2 * layers, channels)),
    )(place, *most)
    return pl.pallas_call(
        functools.partial(collect_kernel, 0),
        out_shape=shape,
        in_specs=[SMEM, VMEM, ANY],
        out_specs=ANY,
        scratch_shapes=scratch,
        input_output_aliases={2: 0},
        compiler_params=params(16),
    )(place, last, out)


def from_behind(shard, axis, by):
    devices = lax.axis_size(axis)
    pairs = [(i, i + by) for i in range(devices) if 0 <= i + by < devices]
    return lax.ppermute(shard, axis, pairs)


def swap(shard, bit):
    return lax.ppermute(shard, "dp", [(i, i ^ bit) for i in range(lax.axis_size("dp"))])


def order_of(index, size, backward):
    return size - 1 - index if backward else index


def group_of(size):
    for group in (GROUP, 2, 1):
        if size % group == 0:
            return group


def exchange(pieces, group, backward):
    size = lax.axis_size("layer")
    received = [pieces[0]]
    for shift in range(1, group):
        pairs = []
        for order in range(size):
            base = order - order % group
            target = base + (order + shift) % group
            pairs.append((order_of(order, size, backward), order_of(target, size, backward)))
        received.append(lax.ppermute(pieces[shift], "layer", pairs))
    return received


def coarse_chain(place, seed, pieces, matrices, group, chunks, backward, beside=()):
    size = lax.axis_size("layer")
    pairs = [(order_of(i, size, backward), order_of(i + group, size, backward)) for i in range(size - group)]
    received = []
    for chunk in range(len(chunks)):
        sent = pieces[chunk * group : (chunk + 1) * group]
        if chunk > 0:
            received[-1][1], *sent = lax.optimization_barrier((received[-1][1], *sent))
        received.append(exchange(sent, group, backward))
    carries = [jnp.zeros(pieces[chunk * group].shape, F32) for chunk in range(len(chunks))]
    partials = [None] * len(chunks)

    def partial_of(chunk):
        return partial_chain(place, seed, matrices, received[chunk], group, chunks, chunk, backward)

    for chunk in range(len(chunks)):
        if size > group:
            out = group_carry(place, seed, matrices, received[chunk], group, chunks, chunk, backward)
            carry = lax.ppermute(out, "layer", pairs)
            for _ in range(size // group - 2):
                carry = lax.ppermute(hop(carry, matrices[int(backward), whole_at(group)], out), "layer", pairs)
            carries[chunk] = carry
        if backward:
            partials[chunk] = partial_of(chunk)
    if backward:
        partials[-1], beside = lax.optimization_barrier((partials[-1], beside))
    else:
        if size > group:
            received, out = lax.optimization_barrier((received, out))
        partials = lax.optimization_barrier([partial_of(chunk) for chunk in range(len(chunks))])
    begins = [(carry, products, begun) for carry, (begun, products) in zip(carries, partials)]
    result = []
    for carry, products, begun in begins:
        result += exchange(complete_chain(carry, products, begun, group), group, backward)
    return result, beside


def sum_across(total):
    bit = 2
    while bit < lax.axis_size("dp"):
        total = total + swap(total, bit)
        bit *= 2
    return total


def per_device(images, kernels, damping, cotangent):
    layers, taps, channels = kernels.shape
    _, height, side, _ = images.shape
    size = lax.axis_size("layer")
    position = lax.axis_index("layer")
    dp_at = lax.axis_index("dp")
    field = (height // 2, 2, side, channels)
    images = images.reshape(field)
    cotangent = cotangent.reshape(field)
    group = group_of(size)
    quarter = field[0] // group
    chunks = chunks_of(quarter)
    back_order = size - 1 - position
    place = jnp.stack(
        [
            position,
            lax.rem(position, group),
            lax.rem(back_order, group),
            dp_at,
            (position < group).astype(jnp.int32),
            (back_order < group).astype(jnp.int32),
            jnp.int32(size),
            jnp.int32(0),
        ]
    ).astype(jnp.int32)

    parts, quarter_part, copies, matrix, turned_matrix = prelude(place, kernels, damping, group)

    lows = [from_behind(part, "layer", 1) for part in parts]
    highs = [swap(low, 1) for low in lows[:-1]]

    groups = [list(range(at, at + group)) for at in range(0, size, group)]
    lows[0], copies = lax.optimization_barrier((lows[0], copies))
    steps = lax.all_to_all(copies, "layer", 0, 0, axis_index_groups=groups, tiled=True)
    own = (kernels, turn_own(kernels))

    state = images
    for layer in range(layers - 1):
        state = fetched_layer(place, state, lows[layer], highs[layer])
    lows[-1], state, steps = lax.optimization_barrier((lows[-1], state, steps))
    highs.append(swap(lows[-1], 1))

    quarter_part, state = lax.optimization_barrier((quarter_part, state))
    first = from_behind(quarter_part, "layer", -1)

    offset, pieces = slab_offset(
        place, images, state, lows[-1], highs[-1], kernels, damping, matrix, group, chunks
    )
    first, pieces = lax.optimization_barrier((first, pieces))
    second = swap(first, 2)
    following, next_decay = join_next(place, [first, second, swap(first, 1), swap(second, 1)])
    matrices = group_matrices(steps)
    pieces, _ = coarse_chain(place, images, pieces, matrices, group, chunks, False)
    (slab_end, coarse_end, back_offset), states, acts, pieces = middle(
        place, pieces, offset, cotangent, own, following, damping, next_decay, matrix, turned_matrix, group, chunks
    )
    turned = [turned_columns(state) for state in states]
    pieces, turned = coarse_chain(place, cotangent, pieces, matrices, group, chunks, True, turned)
    tops, keep, send = top_gradient(place, pieces, acts[-1], turned[-1], group, chunks)
    adjoint = tops
    paired = [None] * layers
    halves = [None] * layers
    for layer in reversed(range(1, layers)):
        paired[layer] = (keep, send)
        adjoint, keep, send = lower_gradient(
            place, layer, adjoint, acts[layer], own[1], damping, acts[layer - 1], turned[layer - 1]
        )
        total = paired[layer][0] + swap(paired[layer][1], 1)
        adjoint, total = lax.optimization_barrier((adjoint, total))
        if layer < layers - 1:
            adjoint, summed = lax.optimization_barrier((adjoint, paired[layer + 1]))
            paired[layer + 1] = summed
        paired[layer] = sum_across(total)
    total = keep + swap(send, 1)
    adjoint, adjoint_end = last_retreat(adjoint, acts[0], own[1], damping, tops, back_offset, turned_matrix)
    adjoint, total = lax.optimization_barrier((adjoint, total))
    paired[0] = sum_across(total)
    halves = [(half, swap(half, 1)) for half in paired]
    full = (1, 1, height, side, channels)
    return (
        slab_end.reshape(full),
        coarse_end.reshape(full),
        adjoint.reshape(full),
        adjoint_end.reshape(full),
        collect(place, halves),
    )


def solution(mesh):
    in_specs = (
        P("dp", None, None, None),
        P("layer", None, None),
        P("layer", None),
        P("dp", None, None, None),
    )
    out_specs = (
        P("layer", "dp", None, None, None),
        P("layer", "dp", None, None, None),
        P("layer", "dp", None, None, None),
        P("layer", "dp", None, None, None),
        P("layer", None, None),
    )
    return jax.shard_map(
        per_device, mesh=mesh, in_specs=in_specs, out_specs=out_specs, check_vma=False
    )
```

```python
import functools
import math

import jax
import jax.numpy as jnp
from jax import lax
from jax.experimental import pallas as pl
from jax.experimental.pallas import tpu as pltpu
from jax.sharding import PartitionSpec as P

STEP = 0.125
F32 = jnp.float32
BF16 = jnp.bfloat16
BLOCK_PAIRS = 7
PRODUCT_PAIRS = 14
GROUP = 4


def wide_of(side):
    return -(-(side + 1) // 16) * 16


def columns_shape(field):
    pairs, _, side, channels = field
    return (pairs + 1, 2, wide_of(side), 3 * channels)


def block_of(pairs):
    return BLOCK_PAIRS if pairs % BLOCK_PAIRS == 0 else 1


def product_block(pairs):
    return PRODUCT_PAIRS if pairs % PRODUCT_PAIRS == 0 else block_of(pairs)


def per_block(pairs, body, whole=False):
    block = block_of(pairs)

    def step(number, carry):
        if whole:
            body(number * block, block)
        else:
            for pair in range(block):
                body(number * block + pair, 1)
        return carry

    lax.fori_loop(0, pairs // block, step, 0)


def clear_borders(columns):
    edge = jnp.zeros(columns.shape[2:], BF16)
    columns[0, 0] = edge
    columns[columns.shape[0] - 1, 1] = edge


def put_columns(columns, first, odd, rows):
    count, side, channels = rows.shape
    wide = columns.shape[2]
    here = jnp.concatenate([rows, jnp.zeros((count, wide - side, channels), F32)], axis=1)
    left = pltpu.roll(here, 1, 1)
    right = pltpu.roll(here, wide - 1, 1)
    columns[pl.ds(first + odd, count), 1 - odd] = jnp.concatenate([left, here, right], axis=2).astype(BF16)


def spread(paired, kernel):
    taps, channels = kernel.shape
    third = taps // 3
    blank = jnp.zeros((third, channels), BF16)
    paired[0:taps, 0:channels] = kernel
    paired[taps : taps + third, 0:channels] = blank
    paired[0:third, channels : 2 * channels] = blank
    paired[third : taps + third, channels : 2 * channels] = kernel


def convolve(columns, paired, results, emit, side):
    _, _, wide, depth = columns.shape
    channels = depth // 3
    pairs = columns.shape[0] - 1
    block = product_block(pairs)

    def product(number):
        first = number * block
        pieces = [
            columns[first : first + block, 0],
            columns[first : first + block, 1],
            columns[first + 1 : first + 1 + block, 0],
            columns[first + 1 : first + 1 + block, 1],
        ]
        left = jnp.concatenate([piece.reshape(block * wide, depth) for piece in pieces], axis=1)
        results[number % 2][...] = jnp.dot(left, paired[...], preferred_element_type=F32)

    product(0)
    for number in range(pairs // block):
        if number + 1 < pairs // block:
            product(number + 1)
        result = results[number % 2]
        for pair in range(block):
            for odd in range(2):
                preact = result[pair * wide : (pair + 1) * wide, odd * channels : (odd + 1) * channels]
                emit(number * block + pair, odd, preact.reshape(1, wide, channels)[:, :side])


def split_dot(left, matrix):
    high = left.astype(BF16)
    low = (left - high.astype(F32)).astype(BF16)
    m_high = matrix.astype(BF16)
    m_low = (matrix - m_high.astype(F32)).astype(BF16)
    return jnp.dot(
        jnp.concatenate([high, low, high], axis=1),
        jnp.concatenate([m_high, m_high, m_low], axis=0),
        preferred_element_type=F32,
    )


def transform_rows(rows, matrix):
    count, side, channels = rows.shape
    return split_dot(rows.reshape(count * side, channels), matrix).reshape(rows.shape)


def fill_forward(state, columns):
    def fill(first, count):
        for odd in range(2):
            put_columns(columns, first, odd, state[pl.ds(first, count), odd])

    per_block(state.shape[0], fill)


def forward_layer(current, columns, tools, rate, store):
    decay = rate.reshape(1, 1, -1)

    def emit(first, odd, preact):
        rows = pl.ds(first, 1)
        activation = jnp.tanh(preact)
        here = current[rows, odd]
        store(rows, first, odd, here + STEP * (activation - decay * here), activation)

    convolve(columns, tools[0], tools[1:], emit, current.shape[2])


def scaled_rows(adjoint, activation):
    return STEP * (1.0 - activation * activation) * adjoint


def fill_backward(state, activation, columns):
    def fill(first, count):
        rows = pl.ds(first, count)
        for odd in range(2):
            put_columns(columns, first, odd, scaled_rows(state[rows, odd], activation[rows, odd]))

    per_block(state.shape[0], fill)


def backward_layer(current, columns, tools, rate, store):
    decay = rate.reshape(1, 1, -1)

    def emit(first, odd, back_term):
        rows = pl.ds(first, 1)
        here = current[rows, odd]
        store(rows, first, odd, here - STEP * decay * here + back_term)

    convolve(columns, tools[0], tools[1:], emit, current.shape[2])


def params(mebibytes=40):
    return pltpu.CompilerParams(vmem_limit_bytes=mebibytes * 1024 * 1024)


def cost(share, shape, free=False):
    share = 0.0 if free else share
    flops = 8 * share * math.prod(shape) * shape[-1] * 9
    return pl.CostEstimate(flops=int(flops), bytes_accessed=int(8 * share * math.prod(shape)), transcendentals=0)


ANY = pl.BlockSpec(memory_space=pl.ANY)
HBM = pl.BlockSpec(memory_space=pltpu.HBM)
VMEM = pl.BlockSpec(memory_space=pltpu.VMEM)
SMEM = pl.BlockSpec(memory_space=pltpu.SMEM)

def chunks_of(quarter):
    return (quarter - quarter // 2, quarter // 2) if quarter > 1 else (quarter,)


POSITION, FORWARD, BACKWARD, CHUNK, FORWARD_HEAD, BACKWARD_HEAD, SIZE = range(7)


def load(pairs_of_refs, sems, base):
    copies = []
    for number, (source, target) in enumerate(pairs_of_refs):
        copies.append(pltpu.make_async_copy(source, target, sems.at[base + number]))
        copies[-1].start()
    return copies


def finish(copies):
    for copy in copies:
        copy.wait()


def scratch_of(field, buffers):
    shape = columns_shape(field)
    products = pltpu.VMEM((product_block(field[0]) * shape[2], 2 * field[3]), F32)
    return [pltpu.VMEM(shape, BF16)] * buffers + [pltpu.VMEM((4 * shape[3], 2 * field[3]), BF16), products, products]


def join_halves(whole, low, high, half):
    rows = whole.shape[0] // 2
    whole[pl.ds(half * rows, rows)] = low[0:rows].astype(BF16)
    whole[pl.ds((1 - half) * rows, rows)] = high[0:rows].astype(BF16)


def layer_kernel(place, field, low, high, result, columns, paired, even, uneven, whole):
    half = (place[CHUNK] & 1)
    join_halves(whole, low, high, half)
    spread(paired, whole[...])
    rows = whole.shape[0] // 2
    clear_borders(columns)
    fill_forward(field, columns)

    def store(where, first, odd, following, activation):
        result[where, odd] = following

    forward_layer(field, columns, (paired, even, uneven), low[rows : rows + 1], store)


def fetched_layer(place, field, low, high):
    rows, channels = low.shape[0] - 8, low.shape[1]
    return pl.pallas_call(
        layer_kernel,
        out_shape=jax.ShapeDtypeStruct(field.shape, F32),
        in_specs=[SMEM] + [VMEM] * 3,
        out_specs=VMEM,
        scratch_shapes=scratch_of(field.shape, 1) + [pltpu.VMEM((2 * rows, channels), BF16)],
        compiler_params=params(),
        cost_estimate=cost(1.0, field.shape),
    )(place, field, low, high)


def wrapped(index, group):
    return index & (group - 1)


def piece_refs(member, group, chunks, field, shift, chunk, forward_shift):
    quarter = field.shape[0] // group
    offset = sum(chunks[:chunk])
    turn = member + shift if forward_shift else member - shift + group
    return field.at[pl.ds(wrapped(turn, group) * quarter + offset, chunks[chunk])]


def subtract_and_send(member, group, chunks, field, tops, matrix, outs, sems, base):
    quarter = field.shape[0] // group
    copies = []
    for shift in [*range(1, group), 0]:
        rows = pl.ds(wrapped(member + shift, group) * quarter, quarter)
        for odd in range(2):
            field[rows, odd] = field[rows, odd] - transform_rows(tops[rows, odd], matrix[...])
        for chunk in range(len(chunks)):
            number = chunk * group + shift
            source = piece_refs(member, group, chunks, field, shift, chunk, True)
            copies.append(pltpu.make_async_copy(source, outs[number], sems.at[base + number]))
            copies[-1].start()
    return copies


def bring_in(member, group, chunks, pieces, field, sems, base):
    copies = []
    for chunk in range(len(chunks)):
        for shift in range(group):
            number = chunk * group + shift
            target = piece_refs(member, group, chunks, field, shift, chunk, False)
            copies.append(pltpu.make_async_copy(pieces[number], target, sems.at[base + number]))
            copies[-1].start()
    return copies


def piece_shapes(field, group, chunks):
    return [jax.ShapeDtypeStruct((count,) + field[1:], F32) for count in chunks for _ in range(group)]


def offset_kernel(layers, group, chunks, place, images_hbm, field, low, high, kernels_hbm, decay, matrix, *refs):
    count_pieces = group * len(chunks)
    out, pieces = refs[0], refs[1 : 1 + count_pieces]
    images, kernels, starts, offset, now, later, paired, even, uneven, whole, sems = refs[1 + count_pieces :]
    tools = (paired, even, uneven)
    pairs = offset.shape[0]
    loads = load([(images_hbm, images), (kernels_hbm, kernels)], sems, 0)
    half = (place[CHUNK] & 1)
    first_slab = place[POSITION] == 0
    join_halves(whole, low, high, half)
    spread(paired, whole[...])
    rows = whole.shape[0] // 2
    clear_borders(now)
    clear_borders(later)
    fill_forward(field, now)
    loads[0].wait()

    def store_start(where, first, odd, following, activation):
        begin = jnp.where(first_slab, images[where, odd], following)
        starts[where, odd] = begin
        put_columns(later, first, odd, begin)

    forward_layer(field, now, tools, low[rows : rows + 1], store_start)
    loads[1].wait()
    for layer in range(layers):
        now, later = later, now
        spread(paired, kernels[layer])

        def store(where, first, odd, following, activation, last=layer == layers - 1, target=later):
            if not last:
                put_columns(target, first, odd, following)
            offset[where, odd] = following

        source = starts if layer == 0 else offset
        forward_layer(source, now, tools, decay[layer : layer + 1], store)

    copies = subtract_and_send(place[FORWARD], group, chunks, offset, starts, matrix, pieces, sems, 3)
    copies += load([(offset, out)], sems, 2)
    finish(copies)


def slab_offset(place, images, field, low, high, kernels, decay, matrix, group, chunks):
    layers, taps, channels = kernels.shape
    shape = images.shape
    count = group * len(chunks)
    results = pl.pallas_call(
        functools.partial(offset_kernel, layers, group, chunks),
        out_shape=[jax.ShapeDtypeStruct(shape, F32)] + piece_shapes(shape, group, chunks),
        in_specs=[SMEM, ANY, VMEM, VMEM, VMEM, ANY, VMEM, VMEM],
        out_specs=[HBM] * (1 + count),
        scratch_shapes=[pltpu.VMEM(shape, F32), pltpu.VMEM(kernels.shape, BF16)]
        + [pltpu.VMEM(shape, F32)] * 2
        + scratch_of(shape, 2)
        + [pltpu.VMEM((taps, channels), BF16), pltpu.SemaphoreType.DMA((3 + count,))],
        compiler_params=params(),
        cost_estimate=cost(layers + 1.0, shape),
    )(place, images, field, low, high, kernels, decay, matrix)
    return results[0], results[1:]


def split_matrix(matrix):
    high = matrix.astype(BF16)
    low = (matrix - high.astype(F32)).astype(BF16)
    return jnp.concatenate([high, high, low], axis=0)


def split_rows(rows):
    high = rows.astype(BF16)
    low = (rows - high.astype(F32)).astype(BF16)
    return jnp.concatenate([high, low, high], axis=1)


def identity(channels):
    rows = lax.broadcasted_iota(jnp.int32, (channels, channels), 0)
    columns = lax.broadcasted_iota(jnp.int32, (channels, channels), 1)
    return (rows == columns).astype(F32)


def prelude_kernel(place, kernels, damping, *outs):
    layers, taps, channels = kernels.shape
    parts, (quarter, copies, matrix, turned) = outs[:layers], outs[layers:]
    half_rows, quarter_rows = taps // 2, taps // 4
    half, chunk = (place[CHUNK] & 1), (place[CHUNK] & 3)
    for layer in range(layers):
        rate = jnp.broadcast_to(damping[layer : layer + 1], (8, channels))
        parts[layer][0:half_rows] = kernels[layer, pl.ds(half * half_rows, half_rows)].astype(F32)
        parts[layer][half_rows : half_rows + 8] = rate
        quarter[layer, 0:quarter_rows] = kernels[layer, pl.ds(chunk * quarter_rows, quarter_rows)].astype(F32)
        quarter[layer, quarter_rows : quarter_rows + 8] = rate
    total = kernels[0, 0:channels].astype(F32)
    for tap in range(1, taps // channels):
        total += kernels[0, tap * channels : (tap + 1) * channels].astype(F32)
    diagonal = identity(channels) * (1.0 - layers * STEP * damping[0:1])
    coarse = diagonal + layers * STEP * total
    for member in range(copies.shape[0]):
        copies[member] = coarse
    matrix[...] = coarse
    turned[...] = coarse.T


def prelude(place, kernels, damping, group):
    layers, taps, channels = kernels.shape
    part = jax.ShapeDtypeStruct((taps // 2 + 8, channels), F32)
    quarter = jax.ShapeDtypeStruct((layers, taps // 4 + 8, channels), F32)
    square = jax.ShapeDtypeStruct((channels, channels), F32)
    results = pl.pallas_call(
        prelude_kernel,
        out_shape=[part] * layers + [quarter, jax.ShapeDtypeStruct((group, channels, channels), F32), square, square],
        in_specs=[SMEM] + [VMEM] * 2,
        out_specs=[VMEM] * (layers + 4),
        compiler_params=params(60),
    )(place, kernels, damping)
    return results[:layers], *results[layers:]


def step_at(group, index):
    return index


def before_at(group, index):
    return group + index


def after_at(group, index):
    return 2 * group + index


def whole_at(group):
    return 3 * group


def matrices_kernel(group, held, out):
    channels = held.shape[1]
    for backward in range(2):
        ordered = [held[group - 1 - step].T if backward else held[step] for step in range(group)]
        product = identity(channels)
        for step in range(group):
            split = split_matrix(ordered[step])
            out[backward, step_at(group, step)] = split
            out[backward, before_at(group, step)] = split_matrix(product)
            product = ordered[0] if step == 0 else jnp.dot(split_rows(product), split, preferred_element_type=F32)
        out[backward, whole_at(group)] = split_matrix(product)
        product = identity(channels)
        for step in reversed(range(group)):
            out[backward, after_at(group, step)] = split_matrix(product)
            if step == group - 1:
                product = ordered[step]
            else:
                product = jnp.dot(split_rows(ordered[step]), split_matrix(product), preferred_element_type=F32)


def group_matrices(steps):
    group, channels, _ = steps.shape
    return pl.pallas_call(
        functools.partial(matrices_kernel, group),
        out_shape=jax.ShapeDtypeStruct((2, 3 * group + 1, 3 * channels, channels), BF16),
        in_specs=[VMEM],
        out_specs=VMEM,
        compiler_params=params(16),
    )(steps)


def flat_of(shape):
    return (shape[0] * shape[1] * shape[2], shape[3])


def carry_kernel(group, chunks, chunk, backward, place, seed, matrices, *refs):
    pieces, (carry, start, right, sems) = refs[:group], refs[group:]
    member = place[BACKWARD if backward else FORWARD]
    leads = place[BACKWARD_HEAD if backward else FORWARD_HEAD] == 1
    depth = right.shape[0] // (group + 1)
    source = piece_refs(member, group, chunks, seed, 0, chunk, True)
    loads = [(source, start), (matrices.at[backward, whole_at(group)], right.at[pl.ds(group * depth, depth)])]
    for shift in range(group):
        slab = wrapped(member - shift + group, group)
        loads.append((matrices.at[backward, after_at(group, slab)], right.at[pl.ds(shift * depth, depth)]))
    loads = load(loads, sems, 0)
    flat = flat_of(start.shape)
    left = [split_rows(pieces[shift][...].reshape(flat)) for shift in range(group)]
    finish(loads)
    left.append(split_rows(jnp.where(leads, start[...], 0.0).reshape(flat)))
    total = jnp.dot(jnp.concatenate(left, axis=1), right[...], preferred_element_type=F32)
    carry[...] = total.reshape(start.shape)


def group_carry(place, seed, matrices, pieces, group, chunks, chunk, backward):
    shape = pieces[0].shape
    depth, channels = matrices.shape[2:]
    return pl.pallas_call(
        functools.partial(carry_kernel, group, chunks, chunk, int(backward)),
        out_shape=jax.ShapeDtypeStruct(shape, F32),
        in_specs=[SMEM, ANY, ANY] + [VMEM] * group,
        out_specs=VMEM,
        scratch_shapes=[
            pltpu.VMEM(shape, F32),
            pltpu.VMEM(((group + 1) * depth, channels), BF16),
            pltpu.SemaphoreType.DMA((group + 2,)),
        ],
        compiler_params=params(24),
        cost_estimate=cost(1.0 * group, shape),
    )(place, seed, matrices, *pieces)


def partial_kernel(group, chunks, chunk, backward, place, seed, matrices, *refs):
    pieces, (begun, products, full, held, start, sets, sems) = refs[:group], refs[group:]
    member = place[BACKWARD if backward else FORWARD]
    leads = place[BACKWARD_HEAD if backward else FORWARD_HEAD] == 1
    source = piece_refs(member, group, chunks, seed, 0, chunk, True)
    loads = load([(source, start), (matrices.at[backward, pl.ds(0, 2 * group)], sets)], sems, 0)
    for shift in range(group):
        held[wrapped(member - shift + group, group)] = pieces[shift][...]
    finish(loads)
    shape = start.shape
    flat = flat_of(shape)
    state = jnp.where(leads, start[...], 0.0).reshape(flat)
    full[0] = state.reshape(shape)
    for slab in range(group - 1):
        step = sets[step_at(group, slab)]
        state = jnp.dot(split_rows(state), step, preferred_element_type=F32) + held[slab].reshape(flat)
        full[slab + 1] = state.reshape(shape)
    channels = shape[3]
    for shift in range(group):
        slab = wrapped(member + shift, group)
        begun[shift] = full[slab]
        products[:, shift * channels : (shift + 1) * channels] = sets[before_at(group, slab)]


def partial_chain(place, seed, matrices, pieces, group, chunks, chunk, backward):
    shape = pieces[0].shape
    depth, channels = matrices.shape[2:]
    stack = (group,) + shape
    return pl.pallas_call(
        functools.partial(partial_kernel, group, chunks, chunk, int(backward)),
        out_shape=[jax.ShapeDtypeStruct(stack, F32), jax.ShapeDtypeStruct((depth, group * channels), BF16)],
        in_specs=[SMEM, ANY, ANY] + [VMEM] * group,
        out_specs=[VMEM] * 2,
        scratch_shapes=[
            pltpu.VMEM(stack, F32),
            pltpu.VMEM(stack, F32),
            pltpu.VMEM(shape, F32),
            pltpu.VMEM((2 * group, depth, channels), BF16),
            pltpu.SemaphoreType.DMA((2,)),
        ],
        compiler_params=params(24),
        cost_estimate=cost(0.8 * group, shape, not backward),
    )(place, seed, matrices, *pieces)


def hop_kernel(carry, whole, own, result):
    shape = own.shape
    moved = jnp.dot(split_rows(carry[...].reshape(flat_of(shape))), whole[...], preferred_element_type=F32)
    result[...] = own[...] + moved.reshape(shape)


def hop(carry, whole, own):
    return pl.pallas_call(
        hop_kernel,
        out_shape=jax.ShapeDtypeStruct(own.shape, F32),
        in_specs=[VMEM] * 3,
        out_specs=VMEM,
        compiler_params=params(24),
        cost_estimate=cost(0.8, own.shape),
    )(carry, whole, own)


def complete_kernel(group, carry, products, begun, *outs):
    shape = carry.shape
    channels = shape[3]
    moved = jnp.dot(split_rows(carry[...].reshape(flat_of(shape))), products[...], preferred_element_type=F32)
    for shift in range(group):
        part = moved[:, shift * channels : (shift + 1) * channels]
        outs[shift][...] = begun[shift] + part.reshape(shape)


def complete_chain(carry, products, begun, group):
    shape = carry.shape
    return pl.pallas_call(
        functools.partial(complete_kernel, group),
        out_shape=[jax.ShapeDtypeStruct(shape, F32)] * group,
        in_specs=[VMEM] * 3,
        out_specs=[VMEM] * group,
        compiler_params=params(24),
        cost_estimate=cost(0.2 * group, shape),
    )(carry, products, begun)


def middle_kernel(layers, group, chunks, place, *refs):
    count_pieces = group * len(chunks)
    pieces, refs = refs[:count_pieces], refs[count_pieces:]
    (offset_hbm, cotangent_hbm, next_k_hbm, next_f_hbm, own_k_hbm, own_f_hbm, own_decay, next_decay, matrix, turned) = refs[:10]
    refs = refs[10:]
    (slab_end, coarse_end, back_offset), refs = refs[:3], refs[3:]
    state_outs, refs = refs[:layers], refs[layers:]
    act_outs, refs = refs[:layers], refs[layers:]
    back_pieces, refs = refs[:count_pieces], refs[count_pieces:]
    (begins, states, acts, offset, cotangent, tops, adjoint, first_columns, second_columns) = refs[:9]
    tools, (kernels, turned_kernels, decays, sems) = refs[9:12], refs[12:]
    paired = tools[0]
    pairs = offset.shape[0]
    last_slab = place[POSITION] == place[SIZE] - 1

    brought = bring_in(place[FORWARD], group, chunks, pieces, begins, sems, 0)
    base = count_pieces
    loads = load(
        [
            (offset_hbm, offset),
            (next_k_hbm, kernels.at[0]),
            (cotangent_hbm, tops),
            (next_f_hbm, turned_kernels.at[0]),
            (own_k_hbm, kernels.at[1]),
            (own_f_hbm, turned_kernels.at[1]),
            (cotangent_hbm, cotangent),
        ],
        sems,
        base,
    )
    base += len(loads)
    decays[0] = next_decay[...]
    decays[1] = own_decay[...]
    clear_borders(first_columns)
    clear_borders(second_columns)
    finish(brought)
    loads[0].wait()

    def coarse_rows(first, count):
        rows = pl.ds(first, count)
        for odd in range(2):
            states[0, rows, odd] = transform_rows(begins[rows, odd], matrix[...]) + offset[rows, odd]

    per_block(pairs, coarse_rows, whole=True)
    fill_forward(states.at[0], first_columns)
    out_coarse = pltpu.make_async_copy(states.at[0], coarse_end, sems.at[base])
    out_coarse.start()
    base += 1
    finish(loads[1:])
    late = [(states.at[layers], slab_end)]
    late += [(states.at[n], state_outs[n]) for n in range(layers)]
    late += [(acts.at[n], act_outs[n]) for n in range(layers)]

    def both_sweeps(index, carry):
        now, later = first_columns, second_columns
        for layer in range(layers):
            spread(paired, kernels[index, layer])

            def store(rows, first, odd, following, activation, layer=layer, target=later):
                states[layer + 1, rows, odd] = following
                acts[layer, rows, odd] = activation
                if layer < layers - 1:
                    put_columns(target, first, odd, following)
                else:
                    put_columns(target, first, odd, scaled_rows(tops[rows, odd], activation))

            forward_layer(states.at[layer], now, tools, decays[index, layer : layer + 1], store)
            now, later = later, now

        @pl.when(index == 1)
        def _():
            load(late, sems, base)

        for layer in reversed(range(layers)):
            spread(paired, turned_kernels[index, layer])

            def store_back(rows, first, odd, following, layer=layer, target=later):
                adjoint[rows, odd] = following
                if layer > 0:
                    put_columns(target, first, odd, scaled_rows(following, acts[layer - 1, rows, odd]))

            source = tops if layer == layers - 1 else adjoint
            backward_layer(source, now, tools, decays[index, layer : layer + 1], store_back)
            now, later = later, now

        @pl.when(index == 0)
        def _():
            out_coarse.wait()

            def again(first, count):
                rows = pl.ds(first, count)
                tops[rows] = jnp.where(last_slab, cotangent[rows], adjoint[rows])
                for odd in range(2):
                    begin = begins[rows, odd]
                    states[0, rows, odd] = begin
                    put_columns(first_columns, first, odd, begin)

            per_block(pairs, again)

        return carry

    lax.fori_loop(0, 2, both_sweeps, 0)

    outs = subtract_and_send(place[BACKWARD], group, chunks, adjoint, tops, turned, back_pieces, sems, 0)
    outs += load([(adjoint, back_offset)], sems, count_pieces)
    finish(outs)
    for number, (source, target) in enumerate(late):
        pltpu.make_async_copy(source, target, sems.at[base + number]).wait()


def middle(place, pieces, offset, cotangent, own, following, own_decay, next_decay, matrix, turned, group, chunks):
    layers = own[0].shape[0]
    field = offset.shape
    count = len(pieces)
    fields = [jax.ShapeDtypeStruct(field, F32)] * (3 + 2 * layers)
    results = pl.pallas_call(
        functools.partial(middle_kernel, layers, group, chunks),
        out_shape=fields + piece_shapes(field, group, chunks),
        in_specs=[SMEM] + [ANY] * (count + 6) + [VMEM] * 4,
        out_specs=[ANY] * (3 + 2 * layers + count),
        scratch_shapes=[pltpu.VMEM(field, F32)]
        + [pltpu.VMEM((layers + 1,) + field, F32), pltpu.VMEM((layers,) + field, F32)]
        + [pltpu.VMEM(field, F32)] * 4
        + scratch_of(field, 2)
        + [pltpu.VMEM((2,) + own[0].shape, BF16)] * 2
        + [pltpu.VMEM((2, layers, field[3]), F32), pltpu.SemaphoreType.DMA((count + 9 + 2 * layers,))],
        compiler_params=params(52),
        cost_estimate=cost(4.0 * layers, field),
    )(place, *pieces, offset, cotangent, *following, *own, own_decay, next_decay, matrix, turned)
    return results[:3], results[3 : 3 + layers], results[3 + layers : 3 + 2 * layers], results[3 + 2 * layers :]


def turn(whole, turned):
    taps, channels = whole.shape[0] // whole.shape[1], whole.shape[1]
    for tap in range(taps):
        block = whole[tap * channels : (tap + 1) * channels]
        other = taps - 1 - tap
        turned[other * channels : (other + 1) * channels] = block.T.astype(BF16)


def own_kernel(kernels, turned, whole):
    for layer in range(kernels.shape[0]):
        whole[...] = kernels[layer].astype(F32)
        turn(whole, turned.at[layer])


def turn_own(kernels):
    return pl.pallas_call(
        own_kernel,
        out_shape=jax.ShapeDtypeStruct(kernels.shape, BF16),
        in_specs=[VMEM],
        out_specs=VMEM,
        scratch_shapes=[pltpu.VMEM(kernels.shape[1:], F32)],
        compiler_params=params(),
    )(kernels)


def next_kernel(place, *refs):
    quarters, (kernels, turned, decay, whole) = refs[:4], refs[4:]
    layers = kernels.shape[0]
    rows = whole.shape[0] // 4
    chunk = (place[CHUNK] & 3)
    at = [chunk, chunk ^ 2, chunk ^ 1, chunk ^ 3]
    for layer in range(layers):
        for number in range(4):
            whole[pl.ds(at[number] * rows, rows)] = quarters[number][layer, 0:rows]
        kernels[layer] = whole[...].astype(BF16)
        turn(whole, turned.at[layer])
        decay[layer : layer + 1] = quarters[0][layer, rows : rows + 1]


def join_next(place, quarters):
    layers, rows, channels = quarters[0].shape
    shape = (layers, 4 * (rows - 8), channels)
    results = pl.pallas_call(
        next_kernel,
        out_shape=[jax.ShapeDtypeStruct(shape, BF16)] * 2 + [jax.ShapeDtypeStruct((layers, channels), F32)],
        in_specs=[SMEM] + [VMEM] * 4,
        out_specs=[VMEM] * 3,
        scratch_shapes=[pltpu.VMEM(shape[1:], F32)],
        compiler_params=params(),
    )(place, *quarters)
    return results[:2], results[2]


def turned_columns_kernel(state, turned, columns):
    pairs, _, side, _ = state.shape
    wide, depth = columns.shape[2:]
    clear_borders(columns)

    def fill(first, count):
        for odd in range(2):
            put_columns(columns, first, odd, state[pl.ds(first, count), odd])

    per_block(pairs, fill)
    for pair in range(pairs + 1):
        block = columns[pair].reshape(2 * wide, depth).astype(F32)
        turned[:, pair * 2 * wide : (pair + 1) * 2 * wide] = block.T.astype(BF16)


def turned_columns(state):
    shape = columns_shape(state.shape)
    return pl.pallas_call(
        turned_columns_kernel,
        out_shape=jax.ShapeDtypeStruct((shape[3], shape[0] * 2 * shape[2]), BF16),
        in_specs=[VMEM],
        out_specs=VMEM,
        scratch_shapes=[pltpu.VMEM(shape, BF16)],
        compiler_params=params(),
        cost_estimate=cost(0.4, state.shape),
    )(state)


def gradient_body(adjoint, activation, turned, ready, scaled, gradient, side):
    pairs = adjoint.shape[0]
    wide, channels = scaled.shape[2:]
    edge = jnp.zeros((2, wide, channels), BF16)
    scaled[0] = edge
    scaled[pairs + 1] = edge

    def fill(first, count):
        rows = pl.ds(first, count)
        for odd in range(2):
            own = scaled_rows(adjoint[rows, odd], activation[rows, odd])
            padded = jnp.concatenate([own, jnp.zeros((count, wide - side, channels), F32)], axis=1)
            scaled[pl.ds(first + 1, count), odd] = padded.astype(BF16)

    per_block(pairs, fill)
    ready()
    flat = scaled[...].reshape((2 * pairs + 4) * wide, channels)
    rows = (2 * pairs + 2) * wide
    shifted = [flat[(2 - tap) * wide : (2 - tap) * wide + rows] for tap in range(3)]
    products = jnp.dot(turned[...], jnp.concatenate(shifted, axis=1), preferred_element_type=F32)
    for row in range(3):
        for column in range(3):
            tap = 3 * row + column
            gradient[tap * channels : (tap + 1) * channels] = products[
                column * channels : (column + 1) * channels, row * channels : (row + 1) * channels
            ]


def scaled_shape(field):
    pairs, _, side, channels = field
    return (pairs + 2, 2, wide_of(side), channels)


def halve(place, gradient, keep, send):
    half = (place[CHUNK] & 1)
    rows = keep.shape[0]
    keep[...] = gradient[pl.ds(half * rows, rows)]
    send[...] = gradient[pl.ds((1 - half) * rows, rows)]


def top_kernel(group, chunks, place, *refs):
    count_pieces = group * len(chunks)
    pieces, refs = refs[:count_pieces], refs[count_pieces:]
    activation_hbm, turned_hbm, adjoint_out, keep, send = refs[:5]
    adjoint, activation, turned, shifted, gradient, sems = refs[5:]
    brought = bring_in(place[BACKWARD], group, chunks, pieces, adjoint, sems, 0)
    loads = load([(activation_hbm, activation), (turned_hbm, turned)], sems, count_pieces)
    finish(brought)
    out = load([(adjoint, adjoint_out)], sems, 0)
    loads[0].wait()
    gradient_body(adjoint, activation, turned, loads[1].wait, shifted, gradient, adjoint.shape[2])
    halve(place, gradient, keep, send)
    finish(out)


def top_gradient(place, pieces, activation, turned, group, chunks):
    field = activation.shape
    shape = columns_shape(field)
    taps = 9 * field[3]
    half = jax.ShapeDtypeStruct((taps // 2, field[3]), F32)
    return pl.pallas_call(
        functools.partial(top_kernel, group, chunks),
        out_shape=[jax.ShapeDtypeStruct(field, F32), half, half],
        in_specs=[SMEM] + [ANY] * len(pieces) + [HBM] * 2,
        out_specs=[ANY, VMEM, VMEM],
        scratch_shapes=[
            pltpu.VMEM(field, F32),
            pltpu.VMEM(field, F32),
            pltpu.VMEM(turned.shape, BF16),
            pltpu.VMEM(scaled_shape(field), BF16),
            pltpu.VMEM((taps, field[3]), F32),
            pltpu.SemaphoreType.DMA((len(pieces) + 2,)),
        ],
        compiler_params=params(),
        cost_estimate=cost(1.5, field),
    )(place, *pieces, activation, turned)


def retreat_body(adjoint, activation, columns, tools, rate, store):
    clear_borders(columns)
    fill_backward(adjoint, activation, columns)
    backward_layer(adjoint, columns, tools, rate, store)


def lower_kernel(layer, place, adjoint, above, kernel, decay, below_hbm, turned_hbm, *refs):
    result_out, keep, send = refs[:3]
    result, below, turned, columns, paired, even, uneven, shifted, gradient, sems = refs[3:]
    loads = load([(below_hbm, below), (turned_hbm, turned)], sems, 0)
    spread(paired, kernel[layer])

    def store(rows, first, odd, fresh):
        result[rows, odd] = fresh

    retreat_body(adjoint, above, columns, (paired, even, uneven), decay[layer : layer + 1], store)
    out = load([(result, result_out)], sems, 2)
    loads[0].wait()
    gradient_body(result, below, turned, loads[1].wait, shifted, gradient, result.shape[2])
    halve(place, gradient, keep, send)
    finish(out)


def lower_gradient(place, layer, adjoint, above, kernels, decay, below, turned):
    field = adjoint.shape
    shape = columns_shape(field)
    taps = 9 * field[3]
    half = jax.ShapeDtypeStruct((taps // 2, field[3]), F32)
    return pl.pallas_call(
        functools.partial(lower_kernel, layer),
        out_shape=[jax.ShapeDtypeStruct(field, F32), half, half],
        in_specs=[SMEM] + [VMEM] * 4 + [ANY] * 2,
        out_specs=[ANY, VMEM, VMEM],
        scratch_shapes=[pltpu.VMEM(field, F32), pltpu.VMEM(field, F32), pltpu.VMEM(turned.shape, BF16)]
        + scratch_of(field, 1)
        + [pltpu.VMEM(scaled_shape(field), BF16), pltpu.VMEM((taps, field[3]), F32), pltpu.SemaphoreType.DMA((3,))],
        compiler_params=params(),
        cost_estimate=cost(2.0, field),
    )(place, adjoint, above, kernels, decay, below, turned)


def last_kernel(adjoint, activation, kernel, decay, tops, back_offset, turned, result, adjoint_end, columns, *tools):
    spread(tools[0], kernel[0])

    def store(rows, first, odd, fresh):
        result[rows, odd] = fresh

    retreat_body(adjoint, activation, columns, tools, decay[0:1], store)

    def coarse_rows(first, count):
        rows = pl.ds(first, count)
        for odd in range(2):
            adjoint_end[rows, odd] = transform_rows(tops[rows, odd], turned[...]) + back_offset[rows, odd]

    per_block(adjoint.shape[0], coarse_rows, whole=True)


def last_retreat(adjoint, activation, kernels, decay, tops, back_offset, turned):
    field = adjoint.shape
    return pl.pallas_call(
        last_kernel,
        out_shape=[jax.ShapeDtypeStruct(field, F32)] * 2,
        in_specs=[VMEM] * 7,
        out_specs=[VMEM] * 2,
        scratch_shapes=scratch_of(field, 1),
        compiler_params=params(),
        cost_estimate=cost(1.6, field),
    )(adjoint, activation, kernels, decay, tops, back_offset, turned)


def collect_kernel(layers, place, *refs):
    sources, out, held, sems = refs[:-3], refs[-3], refs[-2], refs[-1]
    half = (place[CHUNK] & 1)
    rows = out.shape[1] // 2
    if layers > 0:
        number = 0
        copies = []
        for layer in range(layers):
            for part in [half, 1 - half][: 1 if layer == 0 else 2]:
                copies.append((sources[number], out.at[layer, pl.ds(part * rows, rows)]))
                number += 1
        finish(load(copies, sems, 0))
    else:
        finish(load([(sources[0], out.at[0, pl.ds((1 - half) * rows, rows)])], sems, 0))


def collect(place, halves):
    layers = len(halves)
    rows, channels = halves[0][0].shape
    shape = jax.ShapeDtypeStruct((layers, 2 * rows, channels), F32)
    most = [half for both in halves for half in both]
    last = most.pop(1)
    scratch = [pltpu.VMEM((8, channels), F32), pltpu.SemaphoreType.DMA((2 * layers,))]
    out = pl.pallas_call(
        functools.partial(collect_kernel, layers),
        out_shape=shape,
        in_specs=[SMEM] + [VMEM] * len(most),
        out_specs=ANY,
        scratch_shapes=scratch,
        compiler_params=params(16),
        cost_estimate=cost(0.4, (rows, 2 * layers, channels)),
    )(place, *most)
    return pl.pallas_call(
        functools.partial(collect_kernel, 0),
        out_shape=shape,
        in_specs=[SMEM, VMEM, ANY],
        out_specs=ANY,
        scratch_shapes=scratch,
        input_output_aliases={2: 0},
        compiler_params=params(16),
    )(place, last, out)


def from_behind(shard, axis, by):
    devices = lax.axis_size(axis)
    pairs = [(i, i + by) for i in range(devices) if 0 <= i + by < devices]
    return lax.ppermute(shard, axis, pairs)


def swap(shard, bit):
    return lax.ppermute(shard, "dp", [(i, i ^ bit) for i in range(lax.axis_size("dp"))])


def order_of(index, size, backward):
    return size - 1 - index if backward else index


def group_of(size):
    for group in (GROUP, 2, 1):
        if size % group == 0:
            return group


def exchange(pieces, group, backward):
    size = lax.axis_size("layer")
    received = [pieces[0]]
    for shift in range(1, group):
        pairs = []
        for order in range(size):
            base = order - order % group
            target = base + (order + shift) % group
            pairs.append((order_of(order, size, backward), order_of(target, size, backward)))
        received.append(lax.ppermute(pieces[shift], "layer", pairs))
    return received


def coarse_chain(place, seed, pieces, matrices, group, chunks, backward, beside=()):
    size = lax.axis_size("layer")
    pairs = [(order_of(i, size, backward), order_of(i + group, size, backward)) for i in range(size - group)]
    received = []
    for chunk in range(len(chunks)):
        sent = pieces[chunk * group : (chunk + 1) * group]
        if chunk > 0:
            received[-1][1], *sent = lax.optimization_barrier((received[-1][1], *sent))
        received.append(exchange(sent, group, backward))
    carries = [jnp.zeros(pieces[chunk * group].shape, F32) for chunk in range(len(chunks))]
    partials = [None] * len(chunks)

    def partial_of(chunk):
        return partial_chain(place, seed, matrices, received[chunk], group, chunks, chunk, backward)

    for chunk in range(len(chunks)):
        if size > group:
            out = group_carry(place, seed, matrices, received[chunk], group, chunks, chunk, backward)
            carry = lax.ppermute(out, "layer", pairs)
            for _ in range(size // group - 2):
                carry = lax.ppermute(hop(carry, matrices[int(backward), whole_at(group)], out), "layer", pairs)
            carries[chunk] = carry
        if backward:
            partials[chunk] = partial_of(chunk)
    if backward:
        partials[-1], beside = lax.optimization_barrier((partials[-1], beside))
    else:
        if size > group:
            received, out = lax.optimization_barrier((received, out))
        partials = lax.optimization_barrier([partial_of(chunk) for chunk in range(len(chunks))])
    begins = [(carry, products, begun) for carry, (begun, products) in zip(carries, partials)]
    result = []
    for carry, products, begun in begins:
        result += exchange(complete_chain(carry, products, begun, group), group, backward)
    return result, beside


def sum_across(total):
    bit = 2
    while bit < lax.axis_size("dp"):
        total = total + swap(total, bit)
        bit *= 2
    return total


def per_device(images, kernels, damping, cotangent):
    layers, taps, channels = kernels.shape
    _, height, side, _ = images.shape
    size = lax.axis_size("layer")
    position = lax.axis_index("layer")
    dp_at = lax.axis_index("dp")
    field = (height // 2, 2, side, channels)
    images = images.reshape(field)
    cotangent = cotangent.reshape(field)
    group = group_of(size)
    quarter = field[0] // group
    chunks = chunks_of(quarter)
    back_order = size - 1 - position
    place = jnp.stack(
        [
            position,
            lax.rem(position, group),
            lax.rem(back_order, group),
            dp_at,
            (position < group).astype(jnp.int32),
            (back_order < group).astype(jnp.int32),
            jnp.int32(size),
            jnp.int32(0),
        ]
    ).astype(jnp.int32)

    parts, quarter_part, copies, matrix, turned_matrix = prelude(place, kernels, damping, group)

    lows = [from_behind(part, "layer", 1) for part in parts]
    highs = [swap(low, 1) for low in lows[:-1]]

    groups = [list(range(at, at + group)) for at in range(0, size, group)]
    lows[0], copies = lax.optimization_barrier((lows[0], copies))
    steps = lax.all_to_all(copies, "layer", 0, 0, axis_index_groups=groups, tiled=True)
    own = (kernels, turn_own(kernels))

    state = images
    for layer in range(layers - 1):
        state = fetched_layer(place, state, lows[layer], highs[layer])
    lows[-1], _, steps = lax.optimization_barrier((lows[-1], state, steps))
    highs.append(swap(lows[-1], 1))

    quarter_part, _ = lax.optimization_barrier((quarter_part, state))
    first = from_behind(quarter_part, "layer", -1)

    offset, pieces = slab_offset(
        place, images, state, lows[-1], highs[-1], kernels, damping, matrix, group, chunks
    )
    first, pieces = lax.optimization_barrier((first, pieces))
    second = swap(first, 2)
    following, next_decay = join_next(place, [first, second, swap(first, 1), swap(second, 1)])
    matrices = group_matrices(steps)
    pieces, _ = coarse_chain(place, images, pieces, matrices, group, chunks, False)
    (slab_end, coarse_end, back_offset), states, acts, pieces = middle(
        place, pieces, offset, cotangent, own, following, damping, next_decay, matrix, turned_matrix, group, chunks
    )
    turned = [turned_columns(state) for state in states]
    pieces, turned = coarse_chain(place, cotangent, pieces, matrices, group, chunks, True, turned)
    tops, keep, send = top_gradient(place, pieces, acts[-1], turned[-1], group, chunks)
    adjoint = tops
    paired = [None] * layers
    halves = [None] * layers
    for layer in reversed(range(1, layers)):
        paired[layer] = (keep, send)
        adjoint, keep, send = lower_gradient(
            place, layer, adjoint, acts[layer], own[1], damping, acts[layer - 1], turned[layer - 1]
        )
        total = paired[layer][0] + swap(paired[layer][1], 1)
        adjoint, total = lax.optimization_barrier((adjoint, total))
        if layer < layers - 1:
            adjoint, summed = lax.optimization_barrier((adjoint, paired[layer + 1]))
            paired[layer + 1] = summed
        paired[layer] = sum_across(total)
    total = keep + swap(send, 1)
    adjoint, adjoint_end = last_retreat(adjoint, acts[0], own[1], damping, tops, back_offset, turned_matrix)
    adjoint, total = lax.optimization_barrier((adjoint, total))
    paired[0] = sum_across(total)
    halves = [(half, swap(half, 1)) for half in paired]
    full = (1, 1, height, side, channels)
    return (
        slab_end.reshape(full),
        coarse_end.reshape(full),
        adjoint.reshape(full),
        adjoint_end.reshape(full),
        collect(place, halves),
    )


def solution(mesh):
    in_specs = (
        P("dp", None, None, None),
        P("layer", None, None),
        P("layer", None),
        P("dp", None, None, None),
    )
    out_specs = (
        P("layer", "dp", None, None, None),
        P("layer", "dp", None, None, None),
        P("layer", "dp", None, None, None),
        P("layer", "dp", None, None, None),
        P("layer", None, None),
    )
    return jax.shard_map(
        per_device, mesh=mesh, in_specs=in_specs, out_specs=out_specs, check_vma=False
    )
```
